32 devices in a mesh: sec: 4 (over y, core), brick: 8 (over z, x).
Axes of the slice: x: 2, y: 2, z: 4, core: 2. Of those that a mesh axis runs over, the one named last changes fastest.
Arguments:
- potentials: float32 [4, 256, 32, 128], P('sec', 'brick'), may hold values from -0.3 to 1.2
- coefficient: float32 [4, 256, 32, 128], P('sec', 'brick'), may hold values from 0.04 to 0.32
- recovery: float32 [256, 32, 128], P('brick'), may hold values from 0 to 1
- excitable: int32 [256, 32, 128], P('brick'), may hold values 0 or 1
- row_of: int32 [8], P('brick'), may hold values from 0 to 2
Outputs:
- updated: float32 [4, 256, 32, 128], P('sec', 'brick')
The draws below stay inside these ranges and needn't reach their ends.
Inputs may be any that keep to these rules, and one draw needn't show every extreme that they name: row_of[p] is the torso layer on which heart brick p lies.
All inputs are finite; a program needn't handle non-finite values. No bound on the sum of `excitable` on one device may be relied on, other than what follows from the above.
Results may differ from the reference program's by a relative error of at most 0.0003.
Values sent between devices are 32-bit elements; how exact they have to be, the bound alone decides.
A program may use at most 64 MiB of HBM per device.

```python
import math
import jax
import jax.numpy as jnp

CX = 32
CY = 32
CZ = 128
SUBSTEPS = 8
SWEEPS = 16
STEPS = 2
NX = 256
N_SEC = 4
N_BRICK = 8


def with_ends(entries, own_key, low, high):
    index_at = [jax.random.randint(jax.random.fold_in(own_key, axis), (), 0, length) for axis, length in enumerate(entries.shape)]
    longest = entries.shape.index(max(entries.shape))
    next_to = index_at[:longest] + [(index_at[longest] + 1) % entries.shape[longest]] + index_at[longest + 1:]
    return entries.at[tuple(index_at)].set(low).at[tuple(next_to)].set(high)


def levels(stream_key, shape, pieces, smallest, largest):
    level = 1.0
    for dim, shards_of in pieces:
        steps = jax.random.uniform(jax.random.fold_in(jax.random.fold_in(stream_key, 6), dim), (shards_of,), jnp.float32, smallest / len(pieces), largest / len(pieces))
        level = level * jnp.repeat(jnp.exp(steps), shape[dim] // shards_of).reshape((-1,) + (1,) * (len(shape) - 1 - dim))
    return level


def setup_inputs(seed: int = 0) -> dict:
    key_of = jax.random.split(jax.random.key(seed), 6)
    potentials = jnp.clip(-0.3 + 1.5 * jax.random.uniform(key_of[0], (N_SEC, NX, CY, CZ), jnp.float32) ** levels(key_of[0], (N_SEC, NX, CY, CZ), ((0, 4), (1, 8)), -0.2, 0.2), -0.3, 1.2)
    coefficient = jnp.clip(jnp.exp(math.log(0.32) - 2.0794415 * jax.random.uniform(key_of[1], (N_SEC, NX, CY, CZ), jnp.float32) ** levels(key_of[1], (N_SEC, NX, CY, CZ), ((0, 4), (1, 8)), -0.2, 0.2)), 0.04, 0.32)
    recovery = jnp.clip(1.0 * jax.random.uniform(key_of[2], (NX, CY, CZ), jnp.float32) ** levels(key_of[2], (NX, CY, CZ), ((0, 8),), -0.2, 0.2), 0.0, 1.0)
    excitable = with_ends((jax.random.randint(key_of[3], (NX, CY, CZ), 0, 5) < 4).astype(jnp.int32), jax.random.fold_in(key_of[3], 1), 0, 1)
    row_of = with_ends(jax.random.randint(key_of[4], (N_BRICK,), 0, N_SEC - 1), jax.random.fold_in(key_of[4], 1), 0, (N_SEC - 1) - 1).astype(jnp.int32)
    return dict(potentials=potentials, coefficient=coefficient, recovery=recovery, excitable=excitable, row_of=row_of)


coupling_gain = 0.1
ionic_timestep = 0.05
ionic_gain = 8.0
recovery_rate = 0.1
recovery_decay = 0.5
spectrum_low = 0.04
spectrum_high = 12.32


def chebyshev_weights(count):
    center = 0.5 * (spectrum_high + spectrum_low)
    spread = 0.5 * (spectrum_high - spectrum_low)
    ratio = center / spread
    current = 1.0 / ratio
    keeps = []
    pushes = []
    for number in range(count):
        following = 1.0 / (2.0 * ratio - current)
        keeps.append(following * current)
        pushes.append(2.0 * following / spread)
        current = following
    return center, keeps, pushes


def ionic(voltage, recovery, threshold, active):
    for substep in range(SUBSTEPS):
        drive = ionic_gain * voltage * (voltage - threshold) * (1.0 - voltage) - recovery
        relax = recovery_rate * (voltage - recovery_decay * recovery)
        voltage = voltage + ionic_timestep * active * drive
        recovery = recovery + ionic_timestep * active * relax
    return voltage, recovery


def heart_laplace(voltage):
    padded = jnp.pad(voltage, 1, mode="edge")
    total = padded[2:, 1:-1, 1:-1] + padded[:-2, 1:-1, 1:-1]
    total = total + padded[1:-1, 2:, 1:-1] + padded[1:-1, :-2, 1:-1]
    total = total + padded[1:-1, 1:-1, 2:] + padded[1:-1, 1:-1, :-2]
    return total - 6.0 * voltage


def beside_all(field):
    padded = jnp.pad(field, 1)
    total = padded[2:, 1:-1, 1:-1] + padded[:-2, 1:-1, 1:-1]
    total = total + padded[1:-1, 2:, 1:-1] + padded[1:-1, :-2, 1:-1]
    total = total + padded[1:-1, 1:-1, 2:] + padded[1:-1, 1:-1, :-2]
    return total


def to_grid(layers):
    return jnp.transpose(layers, (1, 0, 2, 3)).reshape(NX, 3 * CY, CZ)


def from_grid(field):
    return jnp.transpose(field.reshape(NX, 3, CY, CZ), (1, 0, 2, 3))


def reference(potentials, coefficient, recovery, excitable, row_of):
    voltage = potentials[3]
    threshold = coefficient[3]
    potential = to_grid(potentials[:3])
    absorption = to_grid(coefficient[:3])
    active = excitable.astype(jnp.float32)
    layers = jnp.arange(3, dtype=jnp.int32)
    select = (row_of[:, None] == layers[None, :]).astype(jnp.float32)[:, None, :, None, None]
    center, keeps, pushes = chebyshev_weights(SWEEPS - 1)
    source = heart_laplace(voltage)
    for coupling_step in range(STEPS):
        neighbours = beside_all(potential)
        current = (neighbours - 6.0 * potential).reshape(N_BRICK, CX, 3, CY, CZ)
        heart_current = jnp.sum(current * select, axis=2).reshape(NX, CY, CZ)
        placed = (source.reshape(N_BRICK, CX, 1, CY, CZ) * select).reshape(NX, 3 * CY, CZ)
        voltage, recovery = ionic(voltage, recovery, threshold, active)
        fresh = heart_laplace(voltage)
        voltage = voltage + coupling_gain * (fresh + heart_current)
        residual = placed - ((6.0 + absorption) * potential - neighbours)
        direction = residual / center
        for number in range(SWEEPS - 1):
            potential = potential + direction
            residual = residual - ((6.0 + absorption) * direction - beside_all(direction))
            direction = keeps[number] * direction + pushes[number] * residual
        potential = potential + direction
        source = fresh
    return jnp.concatenate([from_grid(potential), voltage[None]], axis=0)
```

```python
import functools

import jax
import jax.numpy as jnp
import numpy as np
from jax import lax
from jax.experimental import pallas as pl
from jax.experimental.pallas import tpu as pltpu
from jax.sharding import PartitionSpec as P

SUBSTEPS = 8
SWEEPS = 16
STEPS = 2
GROUPS = SWEEPS // 2

coupling_gain = 0.1
ionic_timestep = 0.05
ionic_gain = 8.0
recovery_rate = 0.1
recovery_decay = 0.5
spectrum_low = 0.04
spectrum_high = 12.32

center = 0.5 * (spectrum_high + spectrum_low)
spread = 0.5 * (spectrum_high - spectrum_low)
back = (0.5 * spread) ** 2


def push_weights():
    ratio = center / spread
    values = [1.0, ratio]
    while len(values) <= SWEEPS:
        values.append(2.0 * ratio * values[-1] - values[-2])
    return [(0.5 * spread) ** k * values[k] for k in range(SWEEPS + 1)]


PUSHES = push_weights()
FINAL = 1.0 / PUSHES[SWEEPS]
MESH = pl.DeviceIdType.MESH
PAD = 8
DIAGONAL = ((0, 0), (0, 1), (1, 0), (1, 1))


def largest_divisor(count, limit):
    return max(u for u in range(1, limit + 1) if count % u == 0)


def for_planes(first, count, limit, work):
    unroll = largest_divisor(count, limit)

    def chunk(i, carry):
        done = [work(first + i * unroll + j) for j in range(unroll)]
        for value, store in done:
            store(value)
        return carry

    lax.fori_loop(0, count // unroll, chunk, 0)


def kernel(sections, bricks, pot, coef, rec, exc, push, row, out,
           A, B, EB, GB, BB, JA, JB, W, T, M, HX, HY, HC, SY, SC, R, R2, ER, SE, BR, PR, VH,
           lsem, xsend, xrecv, isend, irecv, gsend, grecv, jsend, jrecv, vsend, vrecv):
    X, Y, Z = W.shape
    sec = lax.axis_index("sec")
    brick = lax.axis_index("brick")
    heart = sections - 1
    is_heart = sec == heart
    has_x = (brick > 0, brick < bricks - 1)
    to_x = (brick - 1, brick + 1)
    has_y = (jnp.logical_and(sec > 0, sec < heart), sec < heart - 1)
    to_y = (sec - 1, sec + 1)
    rows = pl.ds(PAD, Y)
    lane = lax.broadcasted_iota(jnp.int32, (Y, Z), 1)
    lane_x = lax.broadcasted_iota(jnp.int32, (X, Z), 1)

    def remote(src, dst, send, recv, s, b):
        return pltpu.make_async_remote_copy(
            src_ref=src, dst_ref=dst, send_sem=send, recv_sem=recv,
            device_id={"sec": s, "brick": b}, device_id_type=MESH)

    field = pltpu.make_async_copy(pot.at[0], A.at[pl.ds(2, X), rows], lsem.at[0])
    second = pltpu.make_async_copy(coef.at[0], T, lsem.at[1])
    field.start()
    second.start()

    barrier = pltpu.get_barrier_semaphore()

    @pl.when(jnp.logical_not(is_heart))
    def _():
        def clear(i, carry):
            for buf in (A, B):
                buf[i, 0:PAD, :] = jnp.zeros((PAD, Z), jnp.float32)
                buf[i, pl.ds(PAD + Y, PAD), :] = jnp.zeros((PAD, Z), jnp.float32)
            return carry

        lax.fori_loop(0, X + 4, clear, 0)
        for buf in (HX, HY, HC, ER, R2):
            buf[...] = jnp.zeros(buf.shape, jnp.float32)
        EB[0] = jnp.zeros((Y, Z), jnp.float32)
        EB[X + 1] = jnp.zeros((Y, Z), jnp.float32)
        PR[...] = jnp.full(PR.shape, -1.0, jnp.float32)

    for d in range(1, sections):
        pl.semaphore_signal(barrier, inc=1, device_id={"sec": lax.rem(sec + d, sections)},
                            device_id_type=MESH)
    total = sections - 1
    for i in range(2):
        @pl.when(has_x[i])
        def _():
            pl.semaphore_signal(barrier, inc=1, device_id={"sec": sec, "brick": to_x[i]},
                                device_id_type=MESH)
        total = total + has_x[i].astype(jnp.int32)
    for i, j in DIAGONAL:
        both = jnp.logical_and(has_x[i], has_y[j])

        @pl.when(both)
        def _():
            pl.semaphore_signal(barrier, inc=1, device_id={"sec": to_y[j], "brick": to_x[i]},
                                device_id_type=MESH)
        total = total + both.astype(jnp.int32)
    pl.semaphore_wait(barrier, total)
    field.wait()

    def heart_program():
        recover = pltpu.make_async_copy(rec, W, lsem.at[2])
        excite = pltpu.make_async_copy(exc, M, lsem.at[3])
        recover.start()
        excite.start()

        def sides(round_number):
            for i in range(2):
                src = A.at[pl.ds(2, 2) if i == 0 else pl.ds(X, 2), rows]

                @pl.when(has_x[i])
                def _():
                    remote(src, VH.at[round_number, 1 - i], vsend.at[i],
                           vrecv.at[round_number, 1 - i], sec, to_x[i]).start()
            for i in range(2):
                src = A.at[pl.ds(2, 2) if i == 0 else pl.ds(X, 2), rows]
                at = 0 if i == 0 else X + 2

                @pl.when(has_x[i])
                def _():
                    got = remote(src, VH.at[round_number, i], vsend.at[i],
                                 vrecv.at[round_number, i], sec, to_x[i])
                    got.wait_recv()
                    got.wait_send()
                    for j in range(2):
                        A[at + j, rows, :] = VH[round_number, i, j]

                @pl.when(jnp.logical_not(has_x[i]))
                def _():
                    for j in range(2):
                        A[at + j, rows, :] = A[2 if i == 0 else X + 1, rows, :]

            def edge(i, carry):
                A[i, pl.ds(PAD - 1, 1), :] = A[i, pl.ds(PAD, 1), :]
                A[i, pl.ds(PAD + Y, 1), :] = A[i, pl.ds(PAD + Y - 1, 1), :]
                return carry

            lax.fori_loop(0, X + 4, edge, 0)

        def laplace(x):
            c = A[x + 2, rows, :]
            total = A[x + 1, rows, :] + A[x + 3, rows, :]
            total = total + A[x + 2, pl.ds(PAD - 1, Y), :] + A[x + 2, pl.ds(PAD + 1, Y), :]
            total = total + jnp.where(lane == 0, c, pltpu.roll(c, 1, 1))
            total = total + jnp.where(lane == Z - 1, c, pltpu.roll(c, Z - 1, 1))
            return total - 6.0 * c

        def ionic(x):
            v = A[x + 2, rows, :]
            w = W[x]
            thresh = T[x]
            active = ionic_timestep * M[x].astype(jnp.float32)
            for _ in range(SUBSTEPS):
                drive = ionic_gain * v * (v - thresh) * (1.0 - v) - w
                relax = recovery_rate * (v - recovery_decay * w)
                v = v + active * drive
                w = w + active * relax

            def store(value):
                A[x + 2, rows, :] = value[0]
                W[x] = value[1]
            return (v, w), store

        def source(step):
            def work(x):
                def store(value):
                    GB[step, x + 1] = value
                return laplace(x), store
            for_planes(-1, X + 2, 4, work)
            for n in range(2):
                remote(GB.at[step], GB.at[step], gsend.at[step, n], grecv.at[step],
                       heart - 1 - n, brick).start()

        def current(step):
            for n in range(2):
                remote(JB.at[step, n], JB.at[step, n], jsend.at[step], jrecv.at[step, n],
                       heart - 1 - n, brick).wait_recv()

        sides(0)
        source(0)
        second.wait()
        recover.wait()
        excite.wait()
        for step in range(STEPS):
            for_planes(0, X, 2, ionic)
            sides(step + 1)
            if step + 1 < STEPS:
                source(step + 1)
                current(step)

                def advance(x):
                    def store(value):
                        A[x + 2, rows, :] = value
                    gain = GB[step + 1, x + 1] + (JB[step, 0, x] + JB[step, 1, x])
                    return A[x + 2, rows, :] + coupling_gain * gain, store
                for_planes(0, X, 4, advance)
            else:
                def before(x):
                    def store(value):
                        BB[x] = value
                    return A[x + 2, rows, :] + coupling_gain * laplace(x), store
                for_planes(0, X, 4, before)
                current(step)

                def final(x):
                    def store(value):
                        out[0, x] = value
                    return BB[x] + coupling_gain * (JB[step, 0, x] + JB[step, 1, x]), store
                for_planes(0, X, 4, final)
        for step in range(STEPS):
            for n in range(2):
                remote(GB.at[step], GB.at[step], gsend.at[step, n], grecv.at[step],
                       heart - 1 - n, brick).wait_send()

    def torso_program():
        one = jnp.ones((), jnp.float32)
        zero = jnp.zeros((), jnp.float32)
        inside_x = [jnp.where(h, one, zero) for h in has_x]
        inside_y = [jnp.where(h, one, zero) for h in has_y]
        section = sec.astype(jnp.float32)
        own = jnp.where(row[...] == section, 1.0, 0.0)
        own_y = (jnp.where(row[...] == section - 1.0, 1.0, 0.0),
                 jnp.where(row[...] == section + 1.0, 1.0, 0.0))

        def messages(slot):
            found = []
            for i in range(2):
                found.append((has_x[i], A.at[pl.ds(2, 2) if i == 0 else pl.ds(X, 2), rows],
                              HX.at[slot, 1 - i], HX.at[slot, i], 1 - i, i, sec, to_x[i]))
            for j in range(2):
                found.append((has_y[j], SY.at[j], HY.at[slot, 1 - j], HY.at[slot, j],
                              3 - j, 2 + j, to_y[j], brick))
            for n, (i, j) in enumerate(DIAGONAL):
                found.append((jnp.logical_and(has_x[i], has_y[j]), SC.at[n], HC.at[slot, 3 - n],
                              HC.at[slot, n], 7 - n, 4 + n, to_y[j], to_x[i]))
            return found

        def send_all(slot):
            for there, src, dst, land, far, near, s, b in messages(slot):
                @pl.when(there)
                def _():
                    remote(src, dst, xsend.at[near], xrecv.at[slot, far], s, b).start()

        def wait_all(slot, sent):
            for there, src, dst, land, far, near, s, b in messages(slot):
                @pl.when(there)
                def _():
                    got = remote(src, land, xsend.at[near], xrecv.at[slot, near], s, b)
                    if sent:
                        got.wait_send()
                    else:
                        got.wait_recv()

        def pack():
            def one_plane(x, carry):
                for j in range(2):
                    for n in range(2):
                        at = PAD + n if j == 0 else PAD + Y - 1 - n
                        SY[j, n, pl.ds(x, 1), :] = A[x + 2, pl.ds(at, 1), :]
                return carry
            lax.fori_loop(0, X, one_plane, 0, unroll=True)
            for n, (i, j) in enumerate(DIAGONAL):
                SC[n, 0:1, :] = A[2 if i == 0 else X + 1, pl.ds(PAD if j == 0 else PAD + Y - 1, 1), :]

        def stencil(src, x):
            c = src[x + 2, rows, :]
            total = src[x + 1, rows, :] + src[x + 3, rows, :]
            total = total + (src[x + 2, pl.ds(PAD - 1, Y), :] + src[x + 2, pl.ds(PAD + 1, Y), :])
            total = total + (jnp.where(lane == 0, 0.0, pltpu.roll(c, 1, 1))
                             + jnp.where(lane == Z - 1, 0.0, pltpu.roll(c, Z - 1, 1)))
            return total + EB[x + 1] * c

        def plane(src, dst, first, weight):
            def work(x):
                value = stencil(src, x)
                if first:
                    value = 0.5 * value
                else:
                    value = (value + weight * BB[x + 1]) - back * dst[x + 2, rows, :]

                def store(value):
                    dst[x + 2, rows, :] = value
                return value, store
            return work

        def mend(dst, low, high, halo, offset, scale):
            def one_plane(x, carry):
                for j, at in ((0, PAD), (1, PAD + Y - 1)):
                    dst[x + 2, pl.ds(at, 1), :] = (dst[x + 2, pl.ds(at, 1), :]
                                                   + scale * halo[j, pl.ds(x + offset, 1), :])
                return carry
            lax.fori_loop(low, high, one_plane, 0, unroll=True)

        def fringe(slot, first, weight):
            for j in range(2):
                c = R[j, pl.ds(PAD, X), :]
                total = R[j, pl.ds(PAD - 1, X), :] + R[j, pl.ds(PAD + 1, X), :]
                total = total + SY[j, 0] + HY[slot, j, 1]
                total = total + jnp.where(lane_x == 0, 0.0, pltpu.roll(c, 1, 1))
                total = total + jnp.where(lane_x == Z - 1, 0.0, pltpu.roll(c, Z - 1, 1))
                total = total + ER[j] * c
                if first:
                    R2[j] = (0.5 * inside_y[j]) * total
                else:
                    R2[j] = inside_y[j] * (total + weight * BR[j] - back * R2[j])

        def landed(slot):
            for j in range(2):
                A[j, rows, :] = HX[slot, 0, j]
                A[X + 2 + j, rows, :] = HX[slot, 1, j]
                R[j, pl.ds(PAD, X), :] = HY[slot, j, 0]
            for n, (i, j) in enumerate(DIAGONAL):
                R[j, pl.ds(PAD - 1 if i == 0 else PAD + X, 1), :] = HC[slot, n, 0:1, :]

        def edges(first, weight):
            for x in (-1, 0, X - 1, X):
                value, store = plane(A, B, first, weight)(x)
                store(value)

        def close_edges():
            B[1, rows, :] = inside_x[0] * B[1, rows, :]
            B[X + 2, rows, :] = inside_x[1] * B[X + 2, rows, :]

        def relay_source(step):
            return remote(GB.at[step], GB.at[step], gsend.at[step, 2], grecv.at[step],
                          heart - 3, brick)

        def wait_source(step):
            remote(GB.at[step], GB.at[step], gsend.at[step, 2], grecv.at[step],
                   heart, brick).wait_recv()

        def current_copy(step):
            inner = sec == heart - 3
            target = jnp.where(inner, heart - 2, heart)
            place = jnp.where(sec == heart - 2, 1, 0)
            return remote(JA.at[step], JB.at[step, place], jsend.at[step], jrecv.at[step, place],
                          target, brick)

        def init_copies():
            found = []
            for i in range(2):
                found.append((has_x[i], EB.at[1 if i == 0 else X], EB.at[X + 1 if i == 0 else 0],
                              EB.at[0 if i == 0 else X + 1], 1 - i, i, sec, to_x[i]))
                found.append((has_x[i], row, PR.at[1 - i], PR.at[i], 5 - i, 4 + i, sec, to_x[i]))
            for j in range(2):
                found.append((has_y[j], SE.at[j], ER.at[1 - j], ER.at[j], 3 - j, 2 + j,
                              to_y[j], brick))
            return found

        def set_up():
            second.wait()

            def absorb(x):
                def store(value):
                    EB[x + 1] = value
                return (center - 6.0) - T[x], store
            for_planes(0, X, 4, absorb)

            def one_plane(x, carry):
                SE[0, pl.ds(x, 1), :] = EB[x + 1, 0:1, :]
                SE[1, pl.ds(x, 1), :] = EB[x + 1, pl.ds(Y - 1, 1), :]
                return carry
            lax.fori_loop(0, X, one_plane, 0, unroll=True)
            for there, src, dst, land, far, near, s, b in init_copies():
                @pl.when(there)
                def _():
                    remote(src, dst, isend.at[near], irecv.at[far], s, b).start()

        def step_body(step, carry):
            pack()
            send_all(0)

            @pl.when(step == 0)
            def _():
                set_up()
            for_planes(1, X - 2, 6, plane(A, B, True, None))
            wait_all(0, False)

            @pl.when(step == 0)
            def _():
                for there, src, dst, land, far, near, s, b in init_copies():
                    @pl.when(there)
                    def _():
                        got = remote(src, land, isend.at[near], irecv.at[near], s, b)
                        got.wait_recv()
                        got.wait_send()
            landed(0)
            edges(True, None)
            fringe(0, True, None)
            mend(B, -1, X + 1, R, PAD, 0.5)
            close_edges()

            def current(x):
                def store(value):
                    JA[step, x] = value
                own_v = jnp.broadcast_to(own[0:1], (Y, Z))
                value = 2.0 * B[x + 2, rows, :] - (EB[x + 1] + 6.0) * A[x + 2, rows, :]
                return own_v * value, store
            for_planes(0, X, 4, current)

            @pl.when(sec != heart - 2)
            def _():
                current_copy(step).start()

            @pl.when(jnp.logical_or(sec != heart - 2, step == 0))
            def _():
                wait_source(step)

            @pl.when(jnp.logical_and(sec == heart - 2, step == 0))
            def _():
                relay_source(step).start()

            flags = [jnp.where(PR[i] == section, 1.0, 0.0) for i in range(2)]

            def place(flag):
                def work(x):
                    value = jnp.broadcast_to(flag[0:1], (Y, Z)) * GB[step, x + 1]

                    def store(value):
                        BB[x + 1] = value
                        B[x + 2, rows, :] = B[x + 2, rows, :] + 0.5 * value
                    return value, store
                return work
            for_planes(0, X, 4, place(own))
            for x, flag in ((-1, flags[0]), (X, flags[1])):
                value, store = place(flag)(x)
                store(value)

            def source_rows(x, carry):
                BR[0, pl.ds(x, 1), :] = own_y[0][0:1] * GB[step, x + 1, pl.ds(Y - 1, 1), :]
                BR[1, pl.ds(x, 1), :] = own_y[1][0:1] * GB[step, x + 1, pl.ds(0, 1), :]
                return carry
            lax.fori_loop(0, X, source_rows, 0, unroll=True)
            for j in range(2):
                R2[j] = R2[j] + 0.5 * BR[j]
            wait_all(0, True)
            for_planes(0, X, 8, plane(B, A, False, push[1]))
            mend(A, 0, X, R2, 0, 1.0)

            def group(g, carry):
                slot = lax.rem(g, 2)
                pack()
                send_all(slot)

                @pl.when(jnp.logical_and(g == 1, sec == heart - 2))
                def _():
                    remote(JB.at[step, 0], JB.at[step, 0], jsend.at[step], jrecv.at[step, 0],
                           heart, brick).wait_recv()

                    def add(x):
                        def store(value):
                            JA[step, x] = value
                        return JA[step, x] + JB[step, 0, x], store
                    for_planes(0, X, 4, add)
                    current_copy(step).start()

                @pl.when(jnp.logical_and(jnp.logical_and(g == GROUPS - 3, step + 1 < STEPS),
                                         sec == heart - 2))
                def _():
                    wait_source(step + 1)
                    relay_source(step + 1).start()

                first = push[2 * g]
                for_planes(1, X - 2, 6, plane(A, B, False, first))
                wait_all(slot, False)
                landed(slot)
                edges(False, first)
                fringe(slot, False, first)
                mend(B, -1, X + 1, R, PAD, 1.0)
                close_edges()
                wait_all(slot, True)
                for_planes(0, X, 8, plane(B, A, False, push[2 * g + 1]))
                mend(A, 0, X, R2, 0, 1.0)
                return carry

            lax.fori_loop(1, GROUPS, group, 0)

            def scale(x):
                def store(value):
                    A[x + 2, rows, :] = value
                return FINAL * A[x + 2, rows, :], store
            for_planes(0, X, 8, scale)
            return carry

        lax.fori_loop(0, STEPS, step_body, 0)

        def write(x):
            def store(value):
                out[0, x] = value
            return A[x + 2, rows, :], store
        for_planes(0, X, 8, write)
        for step in range(STEPS):
            current_copy(step).wait_send()

            @pl.when(sec == heart - 2)
            def _():
                relay_source(step).wait_send()

    pl.when(is_heart)(heart_program)
    pl.when(jnp.logical_not(is_heart))(torso_program)


def body(mesh, potentials, coefficient, recovery, excitable, row_of):
    sections, bricks = mesh.shape["sec"], mesh.shape["brick"]
    _, X, Y, Z = potentials.shape
    row = jnp.broadcast_to(row_of.astype(jnp.float32)[:, None], (8, Z))
    f32 = jnp.float32
    scratch = [
        ((X + 4, Y + 2 * PAD, Z), f32), ((X + 4, Y + 2 * PAD, Z), f32),
        ((X + 2, Y, Z), f32), ((STEPS, X + 2, Y, Z), f32), ((X + 2, Y, Z), f32),
        ((STEPS, X, Y, Z), f32), ((STEPS, 2, X, Y, Z), f32),
        ((X, Y, Z), f32), ((X, Y, Z), f32), ((X, Y, Z), jnp.int32),
        ((2, 2, 2, Y, Z), f32), ((2, 2, 2, X, Z), f32), ((2, 4, 8, Z), f32),
        ((2, 2, X, Z), f32), ((4, 8, Z), f32),
        ((2, X + 2 * PAD, Z), f32), ((2, X, Z), f32),
        ((2, X, Z), f32), ((2, X, Z), f32), ((2, X, Z), f32),
        ((2, 8, Z), f32), ((STEPS + 1, 2, 2, Y, Z), f32),
    ]
    sems = [(4,), (8,), (2, 8), (6,), (6,), (STEPS, 3), (STEPS,), (STEPS,), (STEPS, 2),
            (2,), (STEPS + 1, 2)]
    vmem = pl.BlockSpec(memory_space=pltpu.VMEM)
    anywhere = pl.BlockSpec(memory_space=pl.ANY)
    cells = X * Y * Z
    return pl.pallas_call(
        functools.partial(kernel, sections, bricks),
        out_shape=jax.ShapeDtypeStruct(potentials.shape, f32),
        in_specs=[anywhere] * 4 + [pl.BlockSpec(memory_space=pltpu.SMEM), vmem],
        out_specs=vmem,
        scratch_shapes=[pltpu.VMEM(s, t) for s, t in scratch]
        + [pltpu.SemaphoreType.DMA(s) for s in sems],
        compiler_params=pltpu.CompilerParams(
            collective_id=0, has_side_effects=True, vmem_limit_bytes=40 * 2**20),
        cost_estimate=pl.CostEstimate(
            flops=cells * STEPS * SWEEPS * 12, bytes_accessed=20 * cells, transcendentals=0),
    )(potentials, coefficient, recovery, excitable, jnp.asarray(np.array(PUSHES, np.float32)), row)


def solution(mesh):
    in_specs = (
        P("sec", "brick", None, None),
        P("sec", "brick", None, None),
        P("brick", None, None),
        P("brick", None, None),
        P("brick"),
    )
    out_specs = P("sec", "brick", None, None)
    return jax.shard_map(functools.partial(body, mesh), mesh=mesh, in_specs=in_specs,
                         out_specs=out_specs, check_vma=False)
```

```python
import functools

import jax
import jax.numpy as jnp
from jax import lax
from jax.experimental import pallas as pl
from jax.experimental.pallas import tpu as pltpu
from jax.sharding import PartitionSpec as P

SUBSTEPS = 8
SWEEPS = 16
STEPS = 2
GROUPS = SWEEPS // 2

coupling_gain = 0.1
ionic_timestep = 0.05
ionic_gain = 8.0
recovery_rate = 0.1
recovery_decay = 0.5
spectrum_low = 0.04
spectrum_high = 12.32

center = 0.5 * (spectrum_high + spectrum_low)
spread = 0.5 * (spectrum_high - spectrum_low)
back = (0.5 * spread) ** 2


def push_weights():
    ratio = center / spread
    values = [1.0, ratio]
    while len(values) <= SWEEPS:
        values.append(2.0 * ratio * values[-1] - values[-2])
    grown = [(0.5 * spread) ** k * values[k] for k in range(SWEEPS + 1)]
    return grown[:SWEEPS] + [1.0] * (GROUPS - 1) + [1.0 / grown[SWEEPS]]


PUSHES = push_weights()
MESH = pl.DeviceIdType.MESH
PAD = 8
DIAGONAL = ((0, 0), (0, 1), (1, 0), (1, 1))


def largest_divisor(count, limit):
    return max(u for u in range(1, limit + 1) if count % u == 0)


def for_planes(first, count, limit, work):
    unroll = largest_divisor(count, limit)

    def chunk(i, carry):
        done = [work(first + i * unroll + j) for j in range(unroll)]
        for value, store in done:
            store(value)
        return carry

    lax.fori_loop(0, count // unroll, chunk, 0)


def kernel(sections, bricks, pot, coef, rec, exc, row_of, out,
           A, B, EB, GB, BB, JA, JB, W, T, M, HX, HY, HC, SY, SC, R, R2, ER, SE, BR, PR, VH, row, push,
           lsem, xsend, xrecv, isend, irecv, gsend, grecv, jsend, jrecv, vsend, vrecv):
    X, Y, Z = W.shape
    sec = lax.axis_index("sec")
    brick = lax.axis_index("brick")
    heart = sections - 1
    is_heart = sec == heart
    has_x = (brick > 0, brick < bricks - 1)
    to_x = (brick - 1, brick + 1)
    has_y = (jnp.logical_and(sec > 0, sec < heart), sec < heart - 1)
    to_y = (sec - 1, sec + 1)
    rows = pl.ds(PAD, Y)
    lane = lax.broadcasted_iota(jnp.int32, (Y, Z), 1)
    lane_x = lax.broadcasted_iota(jnp.int32, (X, Z), 1)

    def across(buf, at, first, count, pitch):
        return buf.reshape(buf.size // Z, Z), pl.ds(first * pitch + at, count, stride=pitch)

    def remote(src, dst, send, recv, s, b):
        return pltpu.make_async_remote_copy(
            src_ref=src, dst_ref=dst, send_sem=send, recv_sem=recv,
            device_id={"sec": s, "brick": b}, device_id_type=MESH)

    for n, value in enumerate(PUSHES):
        push[n] = jnp.float32(value)
    field = pltpu.make_async_copy(pot.at[0], A.at[pl.ds(2, X), rows], lsem.at[0])
    second = pltpu.make_async_copy(coef.at[0], T, lsem.at[1])
    field.start()
    second.start()

    barrier = pltpu.get_barrier_semaphore()

    @pl.when(jnp.logical_not(is_heart))
    def _():
        def clear(i, carry):
            for buf in (A, B):
                buf[i, 0:PAD, :] = jnp.zeros((PAD, Z), jnp.float32)
                buf[i, pl.ds(PAD + Y, PAD), :] = jnp.zeros((PAD, Z), jnp.float32)
            return carry

        lax.fori_loop(0, X + 4, clear, 0)
        for buf in (HX, HY, HC, ER, R2):
            buf[...] = jnp.zeros(buf.shape, jnp.float32)
        EB[0] = jnp.zeros((Y, Z), jnp.float32)
        EB[X + 1] = jnp.zeros((Y, Z), jnp.float32)
        PR[...] = jnp.full(PR.shape, -1.0, jnp.float32)
        row[...] = jnp.full(row.shape, row_of[0].astype(jnp.float32), jnp.float32)

    for d in range(1, sections):
        pl.semaphore_signal(barrier, inc=1, device_id={"sec": lax.rem(sec + d, sections)},
                            device_id_type=MESH)
    total = sections - 1
    for i in range(2):
        @pl.when(has_x[i])
        def _():
            pl.semaphore_signal(barrier, inc=1, device_id={"sec": sec, "brick": to_x[i]},
                                device_id_type=MESH)
        total = total + has_x[i].astype(jnp.int32)
    for i, j in DIAGONAL:
        both = jnp.logical_and(has_x[i], has_y[j])

        @pl.when(both)
        def _():
            pl.semaphore_signal(barrier, inc=1, device_id={"sec": to_y[j], "brick": to_x[i]},
                                device_id_type=MESH)
        total = total + both.astype(jnp.int32)
    pl.semaphore_wait(barrier, total)
    field.wait()

    cuts = largest_divisor(X - 2, 3)
    size = (X - 2) // cuts
    parts = [(2 + n * size, size) for n in range(cuts)] + [(0, 2), (X, 2)]
    inner, outer = range(cuts), range(cuts, cuts + 2)

    def source_copy(step, n, lane_number, target):
        ref = GB.at[step, pl.ds(parts[n][0], parts[n][1])]
        return remote(ref, ref, gsend.at[step, n, lane_number], grecv.at[step, n], target, brick)

    def heart_program():
        recover = pltpu.make_async_copy(rec, W, lsem.at[2])
        excite = pltpu.make_async_copy(exc, M, lsem.at[3])
        recover.start()
        excite.start()

        def send_sides(round_number):
            for i in range(2):
                src = A.at[pl.ds(2, 2) if i == 0 else pl.ds(X, 2), rows]

                @pl.when(has_x[i])
                def _():
                    remote(src, VH.at[round_number, 1 - i], vsend.at[i],
                           vrecv.at[round_number, 1 - i], sec, to_x[i]).start()

        def sides(round_number):
            for i in range(2):
                src = A.at[pl.ds(2, 2) if i == 0 else pl.ds(X, 2), rows]
                at = 0 if i == 0 else X + 2

                @pl.when(has_x[i])
                def _():
                    got = remote(src, VH.at[round_number, i], vsend.at[i],
                                 vrecv.at[round_number, i], sec, to_x[i])
                    got.wait_recv()
                    got.wait_send()
                    for j in range(2):
                        A[at + j, rows, :] = VH[round_number, i, j]

                @pl.when(jnp.logical_not(has_x[i]))
                def _():
                    for j in range(2):
                        A[at + j, rows, :] = A[2 if i == 0 else X + 1, rows, :]

            edge_rows(0, 2)
            edge_rows(X + 2, X + 4)

        def edge_rows(low, high):
            def edge(i, carry):
                A[i, pl.ds(PAD - 1, 1), :] = A[i, pl.ds(PAD, 1), :]
                A[i, pl.ds(PAD + Y, 1), :] = A[i, pl.ds(PAD + Y - 1, 1), :]
                return carry

            lax.fori_loop(low, high, edge, 0)

        def laplace(x):
            c = A[x + 2, rows, :]
            total = A[x + 1, rows, :] + A[x + 3, rows, :]
            total = total + A[x + 2, pl.ds(PAD - 1, Y), :] + A[x + 2, pl.ds(PAD + 1, Y), :]
            total = total + jnp.where(lane == 0, c, pltpu.roll(c, 1, 1))
            total = total + jnp.where(lane == Z - 1, c, pltpu.roll(c, Z - 1, 1))
            return total - 6.0 * c

        def ionic(x):
            v = A[x + 2, rows, :]
            w = W[x]
            thresh = T[x]
            active = ionic_timestep * M[x].astype(jnp.float32)
            for _ in range(SUBSTEPS):
                drive = ionic_gain * v * (v - thresh) * (1.0 - v) - w
                relax = recovery_rate * (v - recovery_decay * w)
                v = v + active * drive
                w = w + active * relax

            def store(value):
                A[x + 2, rows, :] = value[0]
                W[x] = value[1]
            return (v, w), store

        def source(step, chunks):
            def work(x):
                def store(value):
                    GB[step, x + 1] = value
                return laplace(x), store
            for n in chunks:
                low, count = parts[n]
                for_planes(low - 1, count, 5, work)
                for far in (2, 1):
                    source_copy(step, n, far - 1, heart - far).start()

        def current(step):
            for n in range(2):
                remote(JB.at[step, n], JB.at[step, n], jsend.at[step], jrecv.at[step, n],
                       heart - 1 - n, brick).wait_recv()

        edge_rows(2, X + 2)
        send_sides(0)
        source(0, inner)
        sides(0)
        source(0, outer)
        second.wait()
        recover.wait()
        excite.wait()
        for step in range(STEPS):
            for_planes(0, X, 2, ionic)
            send_sides(step + 1)
            edge_rows(2, X + 2)
            sides(step + 1)
            if step + 1 < STEPS:
                source(step + 1, range(len(parts)))
                current(step)

                def advance(x):
                    def store(value):
                        A[x + 2, rows, :] = value
                    gain = GB[step + 1, x + 1] + (JB[step, 0, x] + JB[step, 1, x])
                    return A[x + 2, rows, :] + coupling_gain * gain, store
                for_planes(0, X, 4, advance)
            else:
                def before(x):
                    def store(value):
                        BB[x] = value
                    return A[x + 2, rows, :] + coupling_gain * laplace(x), store
                for_planes(0, X, 4, before)
                current(step)

                def final(x):
                    def store(value):
                        out[0, x] = value
                    return BB[x] + coupling_gain * (JB[step, 0, x] + JB[step, 1, x]), store
                for_planes(0, X, 4, final)
        for step in range(STEPS):
            for n in range(len(parts)):
                for far in (2, 1):
                    source_copy(step, n, far - 1, heart - far).wait_send()

    def torso_program():
        one = jnp.ones((), jnp.float32)
        zero = jnp.zeros((), jnp.float32)
        inside_x = [jnp.where(h, one, zero) for h in has_x]
        inside_y = [jnp.where(h, one, zero) for h in has_y]
        section = sec.astype(jnp.float32)
        own = jnp.where(row[...] == section, 1.0, 0.0)
        own_y = (jnp.where(row[...] == section - 1.0, 1.0, 0.0),
                 jnp.where(row[...] == section + 1.0, 1.0, 0.0))

        def messages(slot):
            found = []
            for i in range(2):
                found.append((has_x[i], A.at[pl.ds(2, 2) if i == 0 else pl.ds(X, 2), rows],
                              HX.at[slot, 1 - i], HX.at[slot, i], 1 - i, i, sec, to_x[i]))
            for j in range(2):
                found.append((has_y[j], SY.at[j], HY.at[slot, 1 - j], HY.at[slot, j],
                              3 - j, 2 + j, to_y[j], brick))
            for n, (i, j) in enumerate(DIAGONAL):
                found.append((jnp.logical_and(has_x[i], has_y[j]), SC.at[n], HC.at[slot, 3 - n],
                              HC.at[slot, n], 7 - n, 4 + n, to_y[j], to_x[i]))
            return found

        def send(slot, which, more):
            for there, src, dst, land, far, near, s, b in [messages(slot)[n] for n in which]:
                @pl.when(jnp.logical_and(there, more))
                def _():
                    remote(src, dst, xsend.at[near], xrecv.at[slot, far], s, b).start()

        def wait_all(slot, sent):
            for there, src, dst, land, far, near, s, b in messages(slot):
                @pl.when(there)
                def _():
                    got = remote(src, land, xsend.at[near], xrecv.at[slot, near], s, b)
                    if sent:
                        got.wait_send()
                    else:
                        got.wait_recv()

        def pack_rows():
            for j in range(2):
                for n in range(2):
                    at = PAD + n if j == 0 else PAD + Y - 1 - n
                    flat, where = across(A, at, 2, X, Y + 2 * PAD)
                    SY[j, n] = flat[where, :]

        def pack_corners():
            for n, (i, j) in enumerate(DIAGONAL):
                SC[n, 0:1, :] = A[2 if i == 0 else X + 1, pl.ds(PAD if j == 0 else PAD + Y - 1, 1), :]

        def stencil(src, x):
            c = src[x + 2, rows, :]
            total = src[x + 1, rows, :] + src[x + 3, rows, :]
            total = total + (src[x + 2, pl.ds(PAD - 1, Y), :] + src[x + 2, pl.ds(PAD + 1, Y), :])
            total = total + (jnp.where(lane == 0, 0.0, pltpu.roll(c, 1, 1))
                             + jnp.where(lane == Z - 1, 0.0, pltpu.roll(c, Z - 1, 1)))
            return total + EB[x + 1] * c

        def plane(src, dst, first, weight, scale=None):
            def work(x):
                value = stencil(src, x)
                if first:
                    value = 0.5 * value
                else:
                    value = (value + weight * BB[x + 1]) - back * dst[x + 2, rows, :]
                if scale is not None:
                    value = scale * value

                def store(value):
                    dst[x + 2, rows, :] = value
                return value, store
            return work

        def mend(dst, low, high, halo, offset, scale):
            for j, at in ((0, PAD), (1, PAD + Y - 1)):
                flat, where = across(dst, at, low + 2, high - low, Y + 2 * PAD)
                flat[where, :] = flat[where, :] + scale * halo[j, pl.ds(low + offset, high - low), :]

        def fringe(slot, first, weight):
            for j in range(2):
                c = R[j, pl.ds(PAD, X), :]
                total = R[j, pl.ds(PAD - 1, X), :] + R[j, pl.ds(PAD + 1, X), :]
                total = total + SY[j, 0] + HY[slot, j, 1]
                total = total + jnp.where(lane_x == 0, 0.0, pltpu.roll(c, 1, 1))
                total = total + jnp.where(lane_x == Z - 1, 0.0, pltpu.roll(c, Z - 1, 1))
                total = total + ER[j] * c
                if first:
                    R2[j] = (0.5 * inside_y[j]) * total
                else:
                    R2[j] = inside_y[j] * (total + weight * BR[j] - back * R2[j])

        def landed(slot):
            for j in range(2):
                A[j, rows, :] = HX[slot, 0, j]
                A[X + 2 + j, rows, :] = HX[slot, 1, j]
                R[j, pl.ds(PAD, X), :] = HY[slot, j, 0]
            for n, (i, j) in enumerate(DIAGONAL):
                R[j, pl.ds(PAD - 1 if i == 0 else PAD + X, 1), :] = HC[slot, n, 0:1, :]

        def edges(first, weight):
            for x in (-1, 0, X - 1, X):
                value, store = plane(A, B, first, weight)(x)
                store(value)

        def close_edges():
            B[1, rows, :] = inside_x[0] * B[1, rows, :]
            B[X + 2, rows, :] = inside_x[1] * B[X + 2, rows, :]

        def relay_source(step, n):
            return source_copy(step, n, 2, heart - 3)

        def wait_source(step, n):
            source_copy(step, n, 2, heart).wait_recv()

        def current_copy(step):
            inner = sec == heart - 3
            target = jnp.where(inner, heart - 2, heart)
            place = jnp.where(sec == heart - 2, 1, 0)
            return remote(JA.at[step], JB.at[step, place], jsend.at[step], jrecv.at[step, place],
                          target, brick)

        def init_copies():
            found = []
            for i in range(2):
                found.append((has_x[i], EB.at[1 if i == 0 else X], EB.at[X + 1 if i == 0 else 0],
                              EB.at[0 if i == 0 else X + 1], 1 - i, i, sec, to_x[i]))
                found.append((has_x[i], row, PR.at[1 - i], PR.at[i], 5 - i, 4 + i, sec, to_x[i]))
            for j in range(2):
                found.append((has_y[j], SE.at[j], ER.at[1 - j], ER.at[j], 3 - j, 2 + j,
                              to_y[j], brick))
            return found

        def set_up():
            second.wait()

            def absorb(x):
                def store(value):
                    EB[x + 1] = value
                return (center - 6.0) - T[x], store
            for_planes(0, X, 4, absorb)

            for j, at in ((0, 0), (1, Y - 1)):
                flat, where = across(EB, at, 1, X, Y)
                SE[j] = flat[where, :]
            for there, src, dst, land, far, near, s, b in init_copies():
                @pl.when(there)
                def _():
                    remote(src, dst, isend.at[near], irecv.at[far], s, b).start()

        BESIDE, ACROSS = (0, 1, 4, 5, 6, 7), (2, 3)

        def second_sweep(slot, weight, scale, more):
            wait_all(slot, True)
            after = 1 - slot
            work = plane(B, A, False, weight, scale)
            done = [work(x) for x in (0, 1, X - 2, X - 1)]
            for value, store in done:
                store(value)
            for low in (0, X - 2):
                mend(A, low, low + 2, R2, 0, scale)
            pack_corners()
            send(after, BESIDE, more)
            for_planes(2, X - 4, 7, work)
            mend(A, 2, X - 2, R2, 0, scale)
            pack_rows()
            send(after, ACROSS, more)

        def step_body(step, carry):
            @pl.when(step == 0)
            def _():
                set_up()
            for_planes(1, X - 2, 6, plane(A, B, True, None))
            wait_all(0, False)

            @pl.when(step == 0)
            def _():
                for there, src, dst, land, far, near, s, b in init_copies():
                    @pl.when(there)
                    def _():
                        got = remote(src, land, isend.at[near], irecv.at[near], s, b)
                        got.wait_recv()
                        got.wait_send()
            landed(0)
            edges(True, None)
            fringe(0, True, None)
            mend(B, -1, X + 1, R, PAD, 0.5)
            close_edges()

            def current(x):
                def store(value):
                    JA[step, x] = value
                own_v = jnp.broadcast_to(own[0:1], (Y, Z))
                value = 2.0 * B[x + 2, rows, :] - (EB[x + 1] + 6.0) * A[x + 2, rows, :]
                return own_v * value, store
            for_planes(0, X, 4, current)

            @pl.when(sec != heart - 2)
            def _():
                current_copy(step).start()

            flags = [jnp.where(PR[i] == section, 1.0, 0.0) for i in range(2)]

            def place(flag):
                def work(x):
                    value = jnp.broadcast_to(flag[0:1], (Y, Z)) * GB[step, x + 1]

                    def store(value):
                        BB[x + 1] = value
                        B[x + 2, rows, :] = B[x + 2, rows, :] + 0.5 * value
                    return value, store
                return work
            for n, (low, count) in enumerate(parts):
                @pl.when(jnp.logical_or(sec != heart - 2, step == 0))
                def _():
                    wait_source(step, n)

                @pl.when(jnp.logical_and(sec == heart - 2, step == 0))
                def _():
                    relay_source(step, n).start()
                if n in inner:
                    for_planes(low - 1, count, 5, place(own))
                else:
                    for x in (low - 1, low):
                        value, store = place({-1: flags[0], X: flags[1]}.get(x, own))(x)
                        store(value)

            for j, at in ((0, Y - 1), (1, 0)):
                flat, where = across(GB, at, step * (X + 2) + 1, X, Y)
                BR[j] = jnp.broadcast_to(own_y[j][0:1], (X, Z)) * flat[where, :]
                R2[j] = R2[j] + 0.5 * BR[j]
            second_sweep(0, push[1], 1.0, True)

            def group(g, carry):
                slot = lax.rem(g, 2)

                @pl.when(jnp.logical_and(g == 1, sec == heart - 2))
                def _():
                    remote(JB.at[step, 0], JB.at[step, 0], jsend.at[step], jrecv.at[step, 0],
                           heart, brick).wait_recv()

                    def add(x):
                        def store(value):
                            JA[step, x] = value
                        return JA[step, x] + JB[step, 0, x], store
                    for_planes(0, X, 4, add)
                    current_copy(step).start()

                @pl.when(jnp.logical_and(jnp.logical_and(g == GROUPS - 3, step + 1 < STEPS),
                                         sec == heart - 2))
                def _():
                    for n in range(len(parts)):
                        wait_source(step + 1, n)
                        relay_source(step + 1, n).start()

                first = push[2 * g]
                for_planes(1, X - 2, 6, plane(A, B, False, first))
                wait_all(slot, False)
                landed(slot)
                edges(False, first)
                fringe(slot, False, first)
                mend(B, -1, X + 1, R, PAD, 1.0)
                close_edges()
                second_sweep(slot, push[2 * g + 1], push[SWEEPS + g],
                             jnp.logical_or(g < GROUPS - 1, step < STEPS - 1))
                return carry

            lax.fori_loop(1, GROUPS, group, 0)
            return carry

        pack_corners()
        send(0, BESIDE, True)
        pack_rows()
        send(0, ACROSS, True)
        lax.fori_loop(0, STEPS, step_body, 0)

        def write(x):
            def store(value):
                out[0, x] = value
            return A[x + 2, rows, :], store
        for_planes(0, X, 8, write)
        for step in range(STEPS):
            current_copy(step).wait_send()

            @pl.when(sec == heart - 2)
            def _():
                for n in range(len(parts)):
                    relay_source(step, n).wait_send()

    pl.when(is_heart)(heart_program)
    pl.when(jnp.logical_not(is_heart))(torso_program)


def body(mesh, potentials, coefficient, recovery, excitable, row_of):
    sections, bricks = mesh.shape["sec"], mesh.shape["brick"]
    _, X, Y, Z = potentials.shape
    f32 = jnp.float32
    scratch = [
        ((X + 4, Y + 2 * PAD, Z), f32), ((X + 4, Y + 2 * PAD, Z), f32),
        ((X + 2, Y, Z), f32), ((STEPS, X + 2, Y, Z), f32), ((X + 2, Y, Z), f32),
        ((STEPS, X, Y, Z), f32), ((STEPS, 2, X, Y, Z), f32),
        ((X, Y, Z), f32), ((X, Y, Z), f32), ((X, Y, Z), jnp.int32),
        ((2, 2, 2, Y, Z), f32), ((2, 2, 2, X, Z), f32), ((2, 4, 8, Z), f32),
        ((2, 2, X, Z), f32), ((4, 8, Z), f32),
        ((2, X + 2 * PAD, Z), f32), ((2, X, Z), f32),
        ((2, X, Z), f32), ((2, X, Z), f32), ((2, X, Z), f32),
        ((2, 8, Z), f32), ((STEPS + 1, 2, 2, Y, Z), f32), ((8, Z), f32),
    ]
    sems = [(4,), (8,), (2, 8), (6,), (6,), (STEPS, 5, 3), (STEPS, 5), (STEPS,), (STEPS, 2),
            (2,), (STEPS + 1, 2)]
    vmem = pl.BlockSpec(memory_space=pltpu.VMEM)
    hbm = pl.BlockSpec(memory_space=pltpu.HBM)
    cells = X * Y * Z
    return pl.pallas_call(
        functools.partial(kernel, sections, bricks),
        out_shape=jax.ShapeDtypeStruct(potentials.shape, f32),
        in_specs=[hbm] * 4 + [pl.BlockSpec(memory_space=pltpu.SMEM)],
        out_specs=vmem,
        scratch_shapes=[pltpu.VMEM(s, t) for s, t in scratch]
        + [pltpu.SMEM((len(PUSHES),), f32)]
        + [pltpu.SemaphoreType.DMA(s) for s in sems],
        compiler_params=pltpu.CompilerParams(
            collective_id=0, has_side_effects=True, vmem_limit_bytes=63 * 2**20 + 2**19),
        cost_estimate=pl.CostEstimate(
            flops=cells * STEPS * SWEEPS * 12, bytes_accessed=20 * cells, transcendentals=0),
    )(potentials, coefficient, recovery, excitable, row_of)


def solution(mesh):
    in_specs = (
        P("sec", "brick", None, None),
        P("sec", "brick", None, None),
        P("brick", None, None),
        P("brick", None, None),
        P("brick"),
    )
    out_specs = P("sec", "brick", None, None)
    return jax.shard_map(functools.partial(body, mesh), mesh=mesh, in_specs=in_specs,
                         out_specs=out_specs, check_vma=False)
```

```python
import functools

import jax
import jax.numpy as jnp
from jax import lax
from jax.experimental import pallas as pl
from jax.experimental.pallas import tpu as pltpu
from jax.sharding import PartitionSpec as P

SUBSTEPS = 8
SWEEPS = 16
STEPS = 2
GROUPS = SWEEPS // 2

coupling_gain = 0.1
ionic_timestep = 0.05
ionic_gain = 8.0
recovery_rate = 0.1
recovery_decay = 0.5
spectrum_low = 0.04
spectrum_high = 12.32

center = 0.5 * (spectrum_high + spectrum_low)
spread = 0.5 * (spectrum_high - spectrum_low)
back = (0.5 * spread) ** 2


def push_weights():
    ratio = center / spread
    values = [1.0, ratio]
    while len(values) <= SWEEPS:
        values.append(2.0 * ratio * values[-1] - values[-2])
    grown = [(0.5 * spread) ** k * values[k] for k in range(SWEEPS + 1)]
    return grown[:SWEEPS] + [1.0] * (GROUPS - 1) + [1.0 / grown[SWEEPS]]


PUSHES = push_weights()
MESH = pl.DeviceIdType.MESH
PAD = 8
DIAGONAL = ((0, 0), (0, 1), (1, 0), (1, 1))


def largest_divisor(count, limit):
    return max(u for u in range(1, limit + 1) if count % u == 0)


def for_planes(first, count, limit, work):
    unroll = largest_divisor(count, limit)

    def chunk(i, carry):
        done = [work(first + i * unroll + j) for j in range(unroll)]
        for value, store in done:
            store(value)
        return carry

    lax.fori_loop(0, count // unroll, chunk, 0)


def kernel(sections, bricks, pot, coef, rec, exc, row_of, out,
           A, B, EB, GB, BB, JA, JB, W, T, M, H, S, DUMP, ZB, R, R2, ER, SE, BR, PR, VH, row, push,
           lsem, sent, landing, isend, irecv, gsend, grecv, jsend, jrecv, vsend, vrecv):
    X, Y, Z = W.shape
    sec = lax.axis_index("sec")
    brick = lax.axis_index("brick")
    heart = sections - 1
    is_heart = sec == heart
    has_x = (brick > 0, brick < bricks - 1)
    to_x = (brick - 1, brick + 1)
    has_y = (jnp.logical_and(sec > 0, sec < heart), sec < heart - 1)
    to_y = (sec - 1, sec + 1)
    rows = pl.ds(PAD, Y)
    lane = lax.broadcasted_iota(jnp.int32, (Y, Z), 1)
    lane_x = lax.broadcasted_iota(jnp.int32, (X, Z), 1)

    def across(buf, at, first, count, pitch):
        return buf.reshape(buf.size // Z, Z), pl.ds(first * pitch + at, count, stride=pitch)

    def remote(src, dst, send, recv, s, b):
        return pltpu.make_async_remote_copy(
            src_ref=src, dst_ref=dst, send_sem=send, recv_sem=recv,
            device_id={"sec": s, "brick": b}, device_id_type=MESH)

    for n, value in enumerate(PUSHES):
        push[n] = jnp.float32(value)
    field = pltpu.make_async_copy(pot.at[0], A.at[pl.ds(2, X), rows], lsem.at[0])
    second = pltpu.make_async_copy(coef.at[0], T, lsem.at[1])
    field.start()
    second.start()

    barrier = pltpu.get_barrier_semaphore()

    @pl.when(jnp.logical_not(is_heart))
    def _():
        def clear(i, carry):
            for buf in (A, B):
                buf[i, 0:PAD, :] = jnp.zeros((PAD, Z), jnp.float32)
                buf[i, pl.ds(PAD + Y, PAD), :] = jnp.zeros((PAD, Z), jnp.float32)
            return carry

        lax.fori_loop(0, X + 4, clear, 0)
        for buf in (ZB, ER, R2):
            buf[...] = jnp.zeros(buf.shape, jnp.float32)
        EB[0] = jnp.zeros((Y, Z), jnp.float32)
        EB[X + 1] = jnp.zeros((Y, Z), jnp.float32)
        PR[...] = jnp.full(PR.shape, -1.0, jnp.float32)
        row[...] = jnp.full(row.shape, row_of[0].astype(jnp.float32), jnp.float32)

    for d in range(1, sections):
        pl.semaphore_signal(barrier, inc=1, device_id={"sec": lax.rem(sec + d, sections)},
                            device_id_type=MESH)
    total = sections - 1
    for i in range(2):
        @pl.when(has_x[i])
        def _():
            pl.semaphore_signal(barrier, inc=1, device_id={"sec": sec, "brick": to_x[i]},
                                device_id_type=MESH)
        total = total + has_x[i].astype(jnp.int32)
    for i, j in DIAGONAL:
        both = jnp.logical_and(has_x[i], has_y[j])

        @pl.when(both)
        def _():
            pl.semaphore_signal(barrier, inc=1, device_id={"sec": to_y[j], "brick": to_x[i]},
                                device_id_type=MESH)
        total = total + both.astype(jnp.int32)
    pl.semaphore_wait(barrier, total)
    field.wait()

    cuts = largest_divisor(X - 2, 3)
    size = (X - 2) // cuts
    parts = [(2 + n * size, size) for n in range(cuts)] + [(0, 2), (X, 2)]
    inner, outer = range(cuts), range(cuts, cuts + 2)

    def source_copy(step, n, lane_number, target):
        ref = GB.at[step, pl.ds(parts[n][0], parts[n][1])]
        return remote(ref, ref, gsend.at[step, n, lane_number], grecv.at[step, n], target, brick)

    def heart_program():
        recover = pltpu.make_async_copy(rec, W, lsem.at[2])
        excite = pltpu.make_async_copy(exc, M, lsem.at[3])
        recover.start()
        excite.start()

        def send_sides(round_number):
            for i in range(2):
                src = A.at[pl.ds(2, 2) if i == 0 else pl.ds(X, 2), rows]

                @pl.when(has_x[i])
                def _():
                    remote(src, VH.at[round_number, 1 - i], vsend.at[i],
                           vrecv.at[round_number, 1 - i], sec, to_x[i]).start()

        def sides(round_number):
            for i in range(2):
                src = A.at[pl.ds(2, 2) if i == 0 else pl.ds(X, 2), rows]
                at = 0 if i == 0 else X + 2

                @pl.when(has_x[i])
                def _():
                    got = remote(src, VH.at[round_number, i], vsend.at[i],
                                 vrecv.at[round_number, i], sec, to_x[i])
                    got.wait_recv()
                    got.wait_send()
                    for j in range(2):
                        A[at + j, rows, :] = VH[round_number, i, j]

                @pl.when(jnp.logical_not(has_x[i]))
                def _():
                    for j in range(2):
                        A[at + j, rows, :] = A[2 if i == 0 else X + 1, rows, :]

            edge_rows(0, 2)
            edge_rows(X + 2, X + 4)

        def edge_rows(low, high):
            def edge(i, carry):
                A[i, pl.ds(PAD - 1, 1), :] = A[i, pl.ds(PAD, 1), :]
                A[i, pl.ds(PAD + Y, 1), :] = A[i, pl.ds(PAD + Y - 1, 1), :]
                return carry

            lax.fori_loop(low, high, edge, 0)

        def laplace(x):
            c = A[x + 2, rows, :]
            total = A[x + 1, rows, :] + A[x + 3, rows, :]
            total = total + A[x + 2, pl.ds(PAD - 1, Y), :] + A[x + 2, pl.ds(PAD + 1, Y), :]
            total = total + jnp.where(lane == 0, c, pltpu.roll(c, 1, 1))
            total = total + jnp.where(lane == Z - 1, c, pltpu.roll(c, Z - 1, 1))
            return total - 6.0 * c

        def ionic(x):
            v = A[x + 2, rows, :]
            w = W[x]
            thresh = T[x]
            active = ionic_timestep * M[x].astype(jnp.float32)
            for _ in range(SUBSTEPS):
                drive = ionic_gain * v * (v - thresh) * (1.0 - v) - w
                relax = recovery_rate * (v - recovery_decay * w)
                v = v + active * drive
                w = w + active * relax

            def store(value):
                A[x + 2, rows, :] = value[0]
                W[x] = value[1]
            return (v, w), store

        def source(step, chunks):
            def work(x):
                def store(value):
                    GB[step, x + 1] = value
                return laplace(x), store
            for n in chunks:
                low, count = parts[n]
                for_planes(low - 1, count, 5, work)
                for far in (2, 1):
                    source_copy(step, n, far - 1, heart - far).start()

        def current(step):
            for n in range(2):
                remote(JB.at[step, n], JB.at[step, n], jsend.at[step], jrecv.at[step, n],
                       heart - 1 - n, brick).wait_recv()

        edge_rows(2, X + 2)
        send_sides(0)
        source(0, inner)
        sides(0)
        source(0, outer)
        second.wait()
        recover.wait()
        excite.wait()
        for step in range(STEPS):
            for_planes(0, X, 2, ionic)
            send_sides(step + 1)
            edge_rows(2, X + 2)
            sides(step + 1)
            if step + 1 < STEPS:
                source(step + 1, range(len(parts)))
                current(step)

                def advance(x):
                    def store(value):
                        A[x + 2, rows, :] = value
                    gain = GB[step + 1, x + 1] + (JB[step, 0, x] + JB[step, 1, x])
                    return A[x + 2, rows, :] + coupling_gain * gain, store
                for_planes(0, X, 4, advance)
            else:
                def before(x):
                    def store(value):
                        BB[x] = value
                    return A[x + 2, rows, :] + coupling_gain * laplace(x), store
                for_planes(0, X, 4, before)
                current(step)

                def final(x):
                    def store(value):
                        out[0, x] = value
                    return BB[x] + coupling_gain * (JB[step, 0, x] + JB[step, 1, x]), store
                for_planes(0, X, 4, final)
        for step in range(STEPS):
            for n in range(len(parts)):
                for far in (2, 1):
                    source_copy(step, n, far - 1, heart - far).wait_send()

    def torso_program():
        one = jnp.ones((), jnp.float32)
        zero = jnp.zeros((), jnp.float32)
        inside_x = [jnp.where(h, one, zero) for h in has_x]
        inside_y = [jnp.where(h, one, zero) for h in has_y]
        section = sec.astype(jnp.float32)
        own = jnp.where(row[...] == section, 1.0, 0.0)
        own_y = (jnp.where(row[...] == section - 1.0, 1.0, 0.0),
                 jnp.where(row[...] == section + 1.0, 1.0, 0.0))

        at_x = [(2 * Y * i, 2 * Y) for i in range(2)]
        at_y = [(4 * Y + 2 * X * j, 2 * X) for j in range(2)]
        at_c = [(4 * (X + Y) + 8 * n, 8) for n in range(4)]

        def message(slot, there, here, s, b):
            there_at, here_at = pl.ds(*there), pl.ds(*here)
            return remote(S.at[slot, here_at], H.at[slot, there_at], sent.at[slot],
                          landing.at[slot], s, b)

        def nothing(slot, here):
            zeros = ZB.at[pl.ds(0, here[1])]
            pltpu.make_async_copy(zeros, H.at[slot, pl.ds(*here)], landing.at[slot]).start()
            pltpu.make_async_copy(zeros, DUMP.at[slot, pl.ds(*here)], sent.at[slot]).start()

        def send_beside(slot):
            for i in range(2):
                @pl.when(has_x[i])
                def _():
                    message(slot, at_x[1 - i], at_x[i], sec, to_x[i]).start()
                    for j in range(2):
                        n = 2 * i + j

                        @pl.when(has_y[j])
                        def _():
                            message(slot, at_c[3 - n], at_c[n], to_y[j], to_x[i]).start()

                        @pl.when(jnp.logical_not(has_y[j]))
                        def _():
                            nothing(slot, at_c[n])

                @pl.when(jnp.logical_not(has_x[i]))
                def _():
                    nothing(slot, at_x[i])
                    for j in range(2):
                        nothing(slot, at_c[2 * i + j])

        def send_across(slot):
            for j in range(2):
                @pl.when(has_y[j])
                def _():
                    message(slot, at_y[1 - j], at_y[j], to_y[j], brick).start()

                @pl.when(jnp.logical_not(has_y[j]))
                def _():
                    nothing(slot, at_y[j])

        def wait_landed(slot):
            pltpu.make_async_copy(S.at[slot], H.at[slot], landing.at[slot]).wait()

        def wait_sent(slot):
            pltpu.make_async_copy(S.at[slot], DUMP.at[slot], sent.at[slot]).wait()

        def pack_rows(slot):
            for j in range(2):
                for n in range(2):
                    at = PAD + n if j == 0 else PAD + Y - 1 - n
                    flat, where = across(A, at, 2, X, Y + 2 * PAD)
                    S[slot, pl.ds(at_y[j][0] + n * X, X), :] = flat[where, :]

        def pack_planes(slot):
            for i in range(2):
                for n in range(2):
                    value = A[(2 if i == 0 else X) + n, rows, :]
                    S[slot, pl.ds(at_x[i][0] + n * Y, Y), :] = value
            for n, (i, j) in enumerate(DIAGONAL):
                corner = A[2 if i == 0 else X + 1, pl.ds(PAD if j == 0 else PAD + Y - 1, 1), :]
                S[slot, pl.ds(at_c[n][0], 1), :] = corner

        def stencil(src, x):
            c = src[x + 2, rows, :]
            total = src[x + 1, rows, :] + src[x + 3, rows, :]
            total = total + (src[x + 2, pl.ds(PAD - 1, Y), :] + src[x + 2, pl.ds(PAD + 1, Y), :])
            total = total + (jnp.where(lane == 0, 0.0, pltpu.roll(c, 1, 1))
                             + jnp.where(lane == Z - 1, 0.0, pltpu.roll(c, Z - 1, 1)))
            return total + EB[x + 1] * c

        def plane(src, dst, first, weight, scale=None):
            def work(x):
                value = stencil(src, x)
                if first:
                    value = 0.5 * value
                else:
                    value = (value + weight * BB[x + 1]) - back * dst[x + 2, rows, :]
                if scale is not None:
                    value = scale * value

                def store(value):
                    dst[x + 2, rows, :] = value
                return value, store
            return work

        def mend(dst, low, high, halo, offset, scale):
            for j, at in ((0, PAD), (1, PAD + Y - 1)):
                flat, where = across(dst, at, low + 2, high - low, Y + 2 * PAD)
                flat[where, :] = flat[where, :] + scale * halo[j, pl.ds(low + offset, high - low), :]

        def fringe(slot, first, weight):
            for j in range(2):
                c = R[j, pl.ds(PAD, X), :]
                total = R[j, pl.ds(PAD - 1, X), :] + R[j, pl.ds(PAD + 1, X), :]
                total = total + S[slot, pl.ds(at_y[j][0], X), :] + H[slot, pl.ds(at_y[j][0] + X, X), :]
                total = total + jnp.where(lane_x == 0, 0.0, pltpu.roll(c, 1, 1))
                total = total + jnp.where(lane_x == Z - 1, 0.0, pltpu.roll(c, Z - 1, 1))
                total = total + ER[j] * c
                if first:
                    R2[j] = (0.5 * inside_y[j]) * total
                else:
                    R2[j] = inside_y[j] * (total + weight * BR[j] - back * R2[j])

        def landed(slot):
            for j in range(2):
                A[j, rows, :] = H[slot, pl.ds(at_x[0][0] + j * Y, Y), :]
                A[X + 2 + j, rows, :] = H[slot, pl.ds(at_x[1][0] + j * Y, Y), :]
                R[j, pl.ds(PAD, X), :] = H[slot, pl.ds(at_y[j][0], X), :]
            for n, (i, j) in enumerate(DIAGONAL):
                R[j, pl.ds(PAD - 1 if i == 0 else PAD + X, 1), :] = H[slot, pl.ds(at_c[n][0], 1), :]

        def first_sweep(slot, number, first, weight, prepare=lambda: None):
            for_planes(1, X - 2, 6, plane(A, B, first, weight))

            @pl.when(number > 0)
            def _():
                wait_sent(1 - slot)
            wait_landed(slot)
            prepare()
            landed(slot)
            done = [plane(A, B, first, weight, scale)(x) for x, scale in
                    ((-1, inside_x[0]), (0, None), (X - 1, None), (X, inside_x[1]))]
            for value, store in done:
                store(value)
            fringe(slot, first, weight)
            mend(B, -1, X + 1, R, PAD, 0.5 if first else 1.0)

        def relay_source(step, n):
            return source_copy(step, n, 2, heart - 3)

        def wait_source(step, n):
            source_copy(step, n, 2, heart).wait_recv()

        def current_copy(step):
            inner = sec == heart - 3
            target = jnp.where(inner, heart - 2, heart)
            place = jnp.where(sec == heart - 2, 1, 0)
            return remote(JA.at[step], JB.at[step, place], jsend.at[step], jrecv.at[step, place],
                          target, brick)

        def init_copies():
            found = []
            for i in range(2):
                found.append((has_x[i], EB.at[1 if i == 0 else X], EB.at[X + 1 if i == 0 else 0],
                              EB.at[0 if i == 0 else X + 1], 1 - i, i, sec, to_x[i]))
                found.append((has_x[i], row, PR.at[1 - i], PR.at[i], 5 - i, 4 + i, sec, to_x[i]))
            for j in range(2):
                found.append((has_y[j], SE.at[j], ER.at[1 - j], ER.at[j], 3 - j, 2 + j,
                              to_y[j], brick))
            return found

        def set_up():
            second.wait()

            def absorb(x):
                def store(value):
                    EB[x + 1] = value
                return (center - 6.0) - T[x], store
            for_planes(0, X, 4, absorb)

            for j, at in ((0, 0), (1, Y - 1)):
                flat, where = across(EB, at, 1, X, Y)
                SE[j] = flat[where, :]
            for there, src, dst, land, far, near, s, b in init_copies():
                @pl.when(there)
                def _():
                    remote(src, dst, isend.at[near], irecv.at[far], s, b).start()

        def second_sweep(slot, weight, scale, more):
            after = 1 - slot
            for j, at in ((0, PAD - 1), (1, PAD + Y)):
                flat, where = across(B, at, 2, X, Y + 2 * PAD)
                flat[where, :] = R2[j]
            work = plane(B, A, False, weight, scale)
            done = [work(x) for x in (0, 1, X - 2, X - 1)]
            for value, store in done:
                store(value)

            @pl.when(more)
            def _():
                pack_planes(after)
                send_beside(after)
            for_planes(2, X - 4, 7, work)

            @pl.when(more)
            def _():
                pack_rows(after)
                send_across(after)

        def step_body(step, carry):
            @pl.when(step == 0)
            def _():
                set_up()

            def prepare():
                @pl.when(step == 0)
                def _():
                    for there, src, dst, land, far, near, s, b in init_copies():
                        @pl.when(there)
                        def _():
                            got = remote(src, land, isend.at[near], irecv.at[near], s, b)
                            got.wait_recv()
                            got.wait_send()

            first_sweep(0, step, True, None, prepare)

            def current(x):
                def store(value):
                    JA[step, x] = value
                own_v = jnp.broadcast_to(own[0:1], (Y, Z))
                value = 2.0 * B[x + 2, rows, :] - (EB[x + 1] + 6.0) * A[x + 2, rows, :]
                return own_v * value, store
            for_planes(0, X, 4, current)

            @pl.when(sec != heart - 2)
            def _():
                current_copy(step).start()

            flags = [jnp.where(PR[i] == section, 1.0, 0.0) for i in range(2)]

            def place(flag):
                def work(x):
                    value = jnp.broadcast_to(flag[0:1], (Y, Z)) * GB[step, x + 1]

                    def store(value):
                        BB[x + 1] = value
                        B[x + 2, rows, :] = B[x + 2, rows, :] + 0.5 * value
                    return value, store
                return work
            for n, (low, count) in enumerate(parts):
                @pl.when(jnp.logical_or(sec != heart - 2, step == 0))
                def _():
                    wait_source(step, n)

                @pl.when(jnp.logical_and(sec == heart - 2, step == 0))
                def _():
                    relay_source(step, n).start()
                if n in inner:
                    for_planes(low - 1, count, 5, place(own))
                else:
                    for x in (low - 1, low):
                        value, store = place({-1: flags[0], X: flags[1]}.get(x, own))(x)
                        store(value)

            for j, at in ((0, Y - 1), (1, 0)):
                flat, where = across(GB, at, step * (X + 2) + 1, X, Y)
                BR[j] = jnp.broadcast_to(own_y[j][0:1], (X, Z)) * flat[where, :]
                R2[j] = R2[j] + 0.5 * BR[j]
            second_sweep(0, push[1], None, True)

            def group(g, carry):
                slot = lax.rem(g, 2)

                @pl.when(jnp.logical_and(g == 1, sec == heart - 2))
                def _():
                    remote(JB.at[step, 0], JB.at[step, 0], jsend.at[step], jrecv.at[step, 0],
                           heart, brick).wait_recv()

                    def add(x):
                        def store(value):
                            JA[step, x] = value
                        return JA[step, x] + JB[step, 0, x], store
                    for_planes(0, X, 4, add)
                    current_copy(step).start()

                @pl.when(jnp.logical_and(jnp.logical_and(g == GROUPS - 3, step + 1 < STEPS),
                                         sec == heart - 2))
                def _():
                    for n in range(len(parts)):
                        wait_source(step + 1, n)
                        relay_source(step + 1, n).start()

                first = push[2 * g]
                first_sweep(slot, g, False, first)
                second_sweep(slot, push[2 * g + 1], push[SWEEPS + g],
                             jnp.logical_or(g < GROUPS - 1, step < STEPS - 1))
                return carry

            lax.fori_loop(1, GROUPS, group, 0)
            return carry

        pack_planes(0)
        send_beside(0)
        pack_rows(0)
        send_across(0)
        lax.fori_loop(0, STEPS, step_body, 0)

        def write(x):
            def store(value):
                out[0, x] = value
            return A[x + 2, rows, :], store
        for_planes(0, X, 8, write)
        wait_sent((GROUPS - 1) % 2)
        for step in range(STEPS):
            current_copy(step).wait_send()

            @pl.when(sec == heart - 2)
            def _():
                for n in range(len(parts)):
                    relay_source(step, n).wait_send()

    pl.when(is_heart)(heart_program)
    pl.when(jnp.logical_not(is_heart))(torso_program)


def body(mesh, potentials, coefficient, recovery, excitable, row_of):
    sections, bricks = mesh.shape["sec"], mesh.shape["brick"]
    _, X, Y, Z = potentials.shape
    f32 = jnp.float32
    scratch = [
        ((X + 4, Y + 2 * PAD, Z), f32), ((X + 4, Y + 2 * PAD, Z), f32),
        ((X + 2, Y, Z), f32), ((STEPS, X + 2, Y, Z), f32), ((X + 2, Y, Z), f32),
        ((STEPS, X, Y, Z), f32), ((STEPS, 2, X, Y, Z), f32),
        ((X, Y, Z), f32), ((X, Y, Z), f32), ((X, Y, Z), jnp.int32),
        ((2, 4 * (X + Y) + 32, Z), f32), ((2, 4 * (X + Y) + 32, Z), f32),
        ((2, 4 * (X + Y) + 32, Z), f32), ((2 * max(X, Y), Z), f32),
        ((2, X + 2 * PAD, Z), f32), ((2, X, Z), f32),
        ((2, X, Z), f32), ((2, X, Z), f32), ((2, X, Z), f32),
        ((2, 8, Z), f32), ((STEPS + 1, 2, 2, Y, Z), f32), ((8, Z), f32),
    ]
    sems = [(4,), (2,), (2,), (6,), (6,), (STEPS, 5, 3), (STEPS, 5), (STEPS,), (STEPS, 2),
            (2,), (STEPS + 1, 2)]
    vmem = pl.BlockSpec(memory_space=pltpu.VMEM)
    hbm = pl.BlockSpec(memory_space=pltpu.HBM)
    cells = X * Y * Z
    return pl.pallas_call(
        functools.partial(kernel, sections, bricks),
        out_shape=jax.ShapeDtypeStruct(potentials.shape, f32),
        in_specs=[hbm] * 4 + [pl.BlockSpec(memory_space=pltpu.SMEM)],
        out_specs=vmem,
        scratch_shapes=[pltpu.VMEM(s, t) for s, t in scratch]
        + [pltpu.SMEM((len(PUSHES),), f32)]
        + [pltpu.SemaphoreType.DMA(s) for s in sems],
        compiler_params=pltpu.CompilerParams(
            collective_id=0, has_side_effects=True, vmem_limit_bytes=63 * 2**20 + 2**19),
        cost_estimate=pl.CostEstimate(
            flops=cells * STEPS * SWEEPS * 12, bytes_accessed=20 * cells, transcendentals=0),
    )(potentials, coefficient, recovery, excitable, row_of)


def solution(mesh):
    in_specs = (
        P("sec", "brick", None, None),
        P("sec", "brick", None, None),
        P("brick", None, None),
        P("brick", None, None),
        P("brick"),
    )
    out_specs = P("sec", "brick", None, None)
    return jax.shard_map(functools.partial(body, mesh), mesh=mesh, in_specs=in_specs,
                         out_specs=out_specs, check_vma=False)
```

```python
import functools

import jax
import jax.numpy as jnp
from jax import lax
from jax.experimental import pallas as pl
from jax.experimental.pallas import tpu as pltpu
from jax.sharding import PartitionSpec as P

SUBSTEPS = 8
SWEEPS = 16
STEPS = 2
GROUPS = SWEEPS // 2

coupling_gain = 0.1
ionic_timestep = 0.05
ionic_gain = 8.0
recovery_rate = 0.1
recovery_decay = 0.5
spectrum_low = 0.04
spectrum_high = 12.32

center = 0.5 * (spectrum_high + spectrum_low)
spread = 0.5 * (spectrum_high - spectrum_low)
back = (0.5 * spread) ** 2


def push_weights():
    ratio = center / spread
    values = [1.0, ratio]
    while len(values) <= SWEEPS:
        values.append(2.0 * ratio * values[-1] - values[-2])
    grown = [(0.5 * spread) ** k * values[k] for k in range(SWEEPS + 1)]
    return grown[:SWEEPS] + [1.0] * (GROUPS - 1) + [1.0 / grown[SWEEPS]]


PUSHES = push_weights()
MESH = pl.DeviceIdType.MESH
PAD = 8
DIAGONAL = ((0, 0), (0, 1), (1, 0), (1, 1))


def largest_divisor(count, limit):
    return max(u for u in range(1, limit + 1) if count % u == 0)


def for_planes(first, count, limit, work):
    unroll = largest_divisor(count, limit)

    def chunk(i, carry):
        done = [work(first + i * unroll + j) for j in range(unroll)]
        for value, store in done:
            store(value)
        return carry

    lax.fori_loop(0, count // unroll, chunk, 0)


def kernel(sections, bricks, pot, coef, rec, exc, row_of, out,
           A, B, EB, GB, BB, JA, JB, W, T, M, H, S, DUMP, ZB, R, R2, ER, SE, BR, PR, VH, row, push,
           lsem, sent, landing, isend, irecv, gsend, grecv, jsend, jrecv, vsend, vrecv):
    X, Y, Z = W.shape
    sec = lax.axis_index("sec")
    brick = lax.axis_index("brick")
    heart = sections - 1
    is_heart = sec == heart
    has_x = (brick > 0, brick < bricks - 1)
    to_x = (brick - 1, brick + 1)
    has_y = (jnp.logical_and(sec > 0, sec < heart), sec < heart - 1)
    to_y = (sec - 1, sec + 1)
    rows = pl.ds(PAD, Y)
    lane = lax.broadcasted_iota(jnp.int32, (Y, Z), 1)
    lane_x = lax.broadcasted_iota(jnp.int32, (X, Z), 1)

    def across(buf, at, first, count, pitch):
        return buf.reshape(buf.size // Z, Z), pl.ds(first * pitch + at, count, stride=pitch)

    def remote(src, dst, send, recv, s, b):
        return pltpu.make_async_remote_copy(
            src_ref=src, dst_ref=dst, send_sem=send, recv_sem=recv,
            device_id={"sec": s, "brick": b}, device_id_type=MESH)

    for n, value in enumerate(PUSHES):
        push[n] = jnp.float32(value)
    field = pltpu.make_async_copy(pot.at[0], A.at[pl.ds(2, X), rows], lsem.at[0])
    second = pltpu.make_async_copy(coef.at[0], T, lsem.at[1])
    field.start()
    second.start()

    barrier = pltpu.get_barrier_semaphore()

    @pl.when(jnp.logical_not(is_heart))
    def _():
        def clear(i, carry):
            for buf in (A, B):
                buf[i, 0:PAD, :] = jnp.zeros((PAD, Z), jnp.float32)
                buf[i, pl.ds(PAD + Y, PAD), :] = jnp.zeros((PAD, Z), jnp.float32)
            return carry

        lax.fori_loop(0, X + 4, clear, 0)
        for buf in (ZB, ER, R2):
            buf[...] = jnp.zeros(buf.shape, jnp.float32)
        EB[0] = jnp.zeros((Y, Z), jnp.float32)
        EB[X + 1] = jnp.zeros((Y, Z), jnp.float32)
        PR[...] = jnp.full(PR.shape, -1.0, jnp.float32)
        row[...] = jnp.full(row.shape, row_of[0].astype(jnp.float32), jnp.float32)

    for d in range(1, sections):
        pl.semaphore_signal(barrier, inc=1, device_id={"sec": lax.rem(sec + d, sections)},
                            device_id_type=MESH)
    total = sections - 1
    for i in range(2):
        @pl.when(has_x[i])
        def _():
            pl.semaphore_signal(barrier, inc=1, device_id={"sec": sec, "brick": to_x[i]},
                                device_id_type=MESH)
        total = total + has_x[i].astype(jnp.int32)
    for i, j in DIAGONAL:
        both = jnp.logical_and(has_x[i], has_y[j])

        @pl.when(both)
        def _():
            pl.semaphore_signal(barrier, inc=1, device_id={"sec": to_y[j], "brick": to_x[i]},
                                device_id_type=MESH)
        total = total + both.astype(jnp.int32)
    pl.semaphore_wait(barrier, total)
    field.wait()

    cuts = largest_divisor(X - 2, 3)
    size = (X - 2) // cuts
    parts = [(2 + n * size, size) for n in range(cuts)] + [(0, 2), (X, 2)]
    inner, outer = range(cuts), range(cuts, cuts + 2)

    def source_copy(step, n, lane_number, target):
        ref = GB.at[step, pl.ds(parts[n][0], parts[n][1])]
        return remote(ref, ref, gsend.at[step, n, lane_number], grecv.at[step, n], target, brick)

    def heart_program():
        recover = pltpu.make_async_copy(rec, W, lsem.at[2])
        excite = pltpu.make_async_copy(exc, M, lsem.at[3])
        recover.start()
        excite.start()

        def send_sides(round_number):
            for i in range(2):
                src = A.at[pl.ds(2, 2) if i == 0 else pl.ds(X, 2), rows]

                @pl.when(has_x[i])
                def _():
                    remote(src, VH.at[round_number, 1 - i], vsend.at[i],
                           vrecv.at[round_number, 1 - i], sec, to_x[i]).start()

        def sides(round_number):
            for i in range(2):
                src = A.at[pl.ds(2, 2) if i == 0 else pl.ds(X, 2), rows]
                at = 0 if i == 0 else X + 2

                @pl.when(has_x[i])
                def _():
                    got = remote(src, VH.at[round_number, i], vsend.at[i],
                                 vrecv.at[round_number, i], sec, to_x[i])
                    got.wait_recv()
                    got.wait_send()
                    for j in range(2):
                        A[at + j, rows, :] = VH[round_number, i, j]

                @pl.when(jnp.logical_not(has_x[i]))
                def _():
                    for j in range(2):
                        A[at + j, rows, :] = A[2 if i == 0 else X + 1, rows, :]

            edge_rows(0, 2)
            edge_rows(X + 2, X + 4)

        def edge_rows(low, high):
            def edge(i, carry):
                A[i, pl.ds(PAD - 1, 1), :] = A[i, pl.ds(PAD, 1), :]
                A[i, pl.ds(PAD + Y, 1), :] = A[i, pl.ds(PAD + Y - 1, 1), :]
                return carry

            lax.fori_loop(low, high, edge, 0)

        def laplace(x):
            c = A[x + 2, rows, :]
            total = A[x + 1, rows, :] + A[x + 3, rows, :]
            total = total + A[x + 2, pl.ds(PAD - 1, Y), :] + A[x + 2, pl.ds(PAD + 1, Y), :]
            total = total + jnp.where(lane == 0, c, pltpu.roll(c, 1, 1))
            total = total + jnp.where(lane == Z - 1, c, pltpu.roll(c, Z - 1, 1))
            return total - 6.0 * c

        def ionic(x):
            v = A[x + 2, rows, :]
            w = W[x]
            thresh = T[x]
            active = ionic_timestep * M[x].astype(jnp.float32)
            for _ in range(SUBSTEPS):
                drive = ionic_gain * v * (v - thresh) * (1.0 - v) - w
                relax = recovery_rate * (v - recovery_decay * w)
                v = v + active * drive
                w = w + active * relax

            def store(value):
                A[x + 2, rows, :] = value[0]
                W[x] = value[1]
            return (v, w), store

        def source(step, chunks):
            def work(x):
                def store(value):
                    GB[step, x + 1] = value
                return laplace(x), store
            for n in chunks:
                low, count = parts[n]
                for_planes(low - 1, count, 5, work)
                for far in (2, 1):
                    source_copy(step, n, far - 1, heart - far).start()

        def current(step):
            for n in range(2):
                remote(JB.at[step, n], JB.at[step, n], jsend.at[step], jrecv.at[step, n],
                       heart - 1 - n, brick).wait_recv()

        edge_rows(2, X + 2)
        send_sides(0)
        source(0, inner)
        sides(0)
        source(0, outer)
        second.wait()
        recover.wait()
        excite.wait()
        for step in range(STEPS):
            for_planes(0, X, 2, ionic)
            send_sides(step + 1)
            edge_rows(2, X + 2)
            sides(step + 1)
            if step + 1 < STEPS:
                source(step + 1, range(len(parts)))
                current(step)

                def advance(x):
                    def store(value):
                        A[x + 2, rows, :] = value
                    gain = GB[step + 1, x + 1] + (JB[step, 0, x] + JB[step, 1, x])
                    return A[x + 2, rows, :] + coupling_gain * gain, store
                for_planes(0, X, 4, advance)
            else:
                def before(x):
                    def store(value):
                        BB[x] = value
                    return A[x + 2, rows, :] + coupling_gain * laplace(x), store
                for_planes(0, X, 4, before)
                current(step)

                def final(x):
                    def store(value):
                        BB[x] = value
                    return BB[x] + coupling_gain * (JB[step, 0, x] + JB[step, 1, x]), store
                for_planes(0, X, 4, final)
                result = pltpu.make_async_copy(BB.at[pl.ds(0, X)], out.at[0], lsem.at[0])
                result.start()
                result.wait()
        for step in range(STEPS):
            for n in range(len(parts)):
                for far in (2, 1):
                    source_copy(step, n, far - 1, heart - far).wait_send()

    def torso_program():
        one = jnp.ones((), jnp.float32)
        zero = jnp.zeros((), jnp.float32)
        inside_x = [jnp.where(h, one, zero) for h in has_x]
        inside_y = [jnp.where(h, one, zero) for h in has_y]
        section = sec.astype(jnp.float32)
        own = jnp.where(row[...] == section, 1.0, 0.0)
        own_y = (jnp.where(row[...] == section - 1.0, 1.0, 0.0),
                 jnp.where(row[...] == section + 1.0, 1.0, 0.0))

        at_x = [(2 * Y * i, 2 * Y) for i in range(2)]
        at_y = [(4 * Y + 2 * X * j, 2 * X) for j in range(2)]
        at_c = [(4 * (X + Y) + 8 * n, 8) for n in range(4)]

        def message(slot, there, here, s, b):
            there_at, here_at = pl.ds(*there), pl.ds(*here)
            return remote(S.at[slot, here_at], H.at[slot, there_at], sent.at[slot],
                          landing.at[slot], s, b)

        def nothing(slot, here):
            zeros = ZB.at[pl.ds(0, here[1])]
            pltpu.make_async_copy(zeros, H.at[slot, pl.ds(*here)], landing.at[slot]).start()
            pltpu.make_async_copy(zeros, DUMP.at[slot, pl.ds(*here)], sent.at[slot]).start()

        def send_beside(slot):
            for n, (i, j) in enumerate(DIAGONAL):
                both = jnp.logical_and(has_x[i], has_y[j])

                @pl.when(both)
                def _():
                    message(slot, at_c[3 - n], at_c[n], to_y[j], to_x[i]).start()

                @pl.when(jnp.logical_not(both))
                def _():
                    nothing(slot, at_c[n])

            def send_planes(i):
                @pl.when(has_x[i])
                def _():
                    message(slot, at_x[1 - i], at_x[i], sec, to_x[i]).start()

                @pl.when(jnp.logical_not(has_x[i]))
                def _():
                    nothing(slot, at_x[i])

            even = lax.rem(brick, 2) == 0

            @pl.when(even)
            def _():
                send_planes(0)
                send_planes(1)

            @pl.when(jnp.logical_not(even))
            def _():
                send_planes(1)
                send_planes(0)

        def send_across(slot):
            for j in range(2):
                @pl.when(has_y[j])
                def _():
                    message(slot, at_y[1 - j], at_y[j], to_y[j], brick).start()

                @pl.when(jnp.logical_not(has_y[j]))
                def _():
                    nothing(slot, at_y[j])

        def wait_landed(slot):
            pltpu.make_async_copy(S.at[slot], H.at[slot], landing.at[slot]).wait()

        def wait_sent(slot):
            pltpu.make_async_copy(S.at[slot], DUMP.at[slot], sent.at[slot]).wait()

        def pack_rows(slot):
            for j in range(2):
                for n in range(2):
                    at = PAD + n if j == 0 else PAD + Y - 1 - n
                    flat, where = across(A, at, 2, X, Y + 2 * PAD)
                    S[slot, pl.ds(at_y[j][0] + n * X, X), :] = flat[where, :]

        def pack_planes(slot):
            for i in range(2):
                for n in range(2):
                    value = A[(2 if i == 0 else X) + n, rows, :]
                    S[slot, pl.ds(at_x[i][0] + n * Y, Y), :] = value
            for n, (i, j) in enumerate(DIAGONAL):
                corner = A[2 if i == 0 else X + 1, pl.ds(PAD if j == 0 else PAD + Y - 1, 1), :]
                S[slot, pl.ds(at_c[n][0], 1), :] = corner

        def stencil(src, x):
            c = src[x + 2, rows, :]
            total = src[x + 1, rows, :] + src[x + 3, rows, :]
            total = total + (src[x + 2, pl.ds(PAD - 1, Y), :] + src[x + 2, pl.ds(PAD + 1, Y), :])
            total = total + (jnp.where(lane == 0, 0.0, pltpu.roll(c, 1, 1))
                             + jnp.where(lane == Z - 1, 0.0, pltpu.roll(c, Z - 1, 1)))
            return total + EB[x + 1] * c

        def plane(src, dst, first, weight, scale=None):
            def work(x):
                value = stencil(src, x)
                if first:
                    value = 0.5 * value
                else:
                    value = (value + weight * BB[x + 1]) - back * dst[x + 2, rows, :]
                if scale is not None:
                    value = scale * value

                def store(value):
                    dst[x + 2, rows, :] = value
                return value, store
            return work

        def mend(dst, low, high, halo, offset, scale):
            for j, at in ((0, PAD), (1, PAD + Y - 1)):
                flat, where = across(dst, at, low + 2, high - low, Y + 2 * PAD)
                flat[where, :] = flat[where, :] + scale * halo[j, pl.ds(low + offset, high - low), :]

        def fringe(slot, first, weight):
            for j in range(2):
                c = R[j, pl.ds(PAD, X), :]
                total = R[j, pl.ds(PAD - 1, X), :] + R[j, pl.ds(PAD + 1, X), :]
                total = total + S[slot, pl.ds(at_y[j][0], X), :] + H[slot, pl.ds(at_y[j][0] + X, X), :]
                total = total + jnp.where(lane_x == 0, 0.0, pltpu.roll(c, 1, 1))
                total = total + jnp.where(lane_x == Z - 1, 0.0, pltpu.roll(c, Z - 1, 1))
                total = total + ER[j] * c
                if first:
                    R2[j] = (0.5 * inside_y[j]) * total
                else:
                    R2[j] = inside_y[j] * (total + weight * BR[j] - back * R2[j])

        def landed(slot):
            for j in range(2):
                A[j, rows, :] = H[slot, pl.ds(at_x[0][0] + j * Y, Y), :]
                A[X + 2 + j, rows, :] = H[slot, pl.ds(at_x[1][0] + j * Y, Y), :]
                R[j, pl.ds(PAD, X), :] = H[slot, pl.ds(at_y[j][0], X), :]
            for n, (i, j) in enumerate(DIAGONAL):
                R[j, pl.ds(PAD - 1 if i == 0 else PAD + X, 1), :] = H[slot, pl.ds(at_c[n][0], 1), :]

        def first_sweep(slot, number, first, weight, prepare=lambda: None):
            for_planes(1, X - 2, 6, plane(A, B, first, weight))

            @pl.when(number > 0)
            def _():
                wait_sent(1 - slot)
            wait_landed(slot)
            prepare()
            landed(slot)
            done = [plane(A, B, first, weight, scale)(x) for x, scale in
                    ((-1, inside_x[0]), (0, None), (X - 1, None), (X, inside_x[1]))]
            for value, store in done:
                store(value)
            fringe(slot, first, weight)
            mend(B, -1, X + 1, R, PAD, 0.5 if first else 1.0)

        def relay_source(step, n):
            return source_copy(step, n, 2, heart - 3)

        def wait_source(step, n):
            source_copy(step, n, 2, heart).wait_recv()

        def current_copy(step):
            inner = sec == heart - 3
            target = jnp.where(inner, heart - 2, heart)
            place = jnp.where(sec == heart - 2, 1, 0)
            return remote(JA.at[step], JB.at[step, place], jsend.at[step], jrecv.at[step, place],
                          target, brick)

        def init_copies():
            found = []
            for i in range(2):
                found.append((has_x[i], EB.at[1 if i == 0 else X], EB.at[X + 1 if i == 0 else 0],
                              EB.at[0 if i == 0 else X + 1], 1 - i, i, sec, to_x[i]))
                found.append((has_x[i], row, PR.at[1 - i], PR.at[i], 5 - i, 4 + i, sec, to_x[i]))
            for j in range(2):
                found.append((has_y[j], SE.at[j], ER.at[1 - j], ER.at[j], 3 - j, 2 + j,
                              to_y[j], brick))
            return found

        def set_up():
            second.wait()

            def absorb(x):
                def store(value):
                    EB[x + 1] = value
                return (center - 6.0) - T[x], store
            for_planes(0, X, 4, absorb)

            for j, at in ((0, 0), (1, Y - 1)):
                flat, where = across(EB, at, 1, X, Y)
                SE[j] = flat[where, :]
            for there, src, dst, land, far, near, s, b in init_copies():
                @pl.when(there)
                def _():
                    remote(src, dst, isend.at[near], irecv.at[far], s, b).start()

        def second_sweep(slot, weight, scale, more):
            after = 1 - slot
            for j, at in ((0, PAD - 1), (1, PAD + Y)):
                flat, where = across(B, at, 2, X, Y + 2 * PAD)
                flat[where, :] = R2[j]
            work = plane(B, A, False, weight, scale)
            done = [work(x) for x in (0, 1, X - 2, X - 1)]
            for value, store in done:
                store(value)

            @pl.when(more)
            def _():
                pack_planes(after)
                send_beside(after)
            for_planes(2, X - 4, 7, work)

            @pl.when(more)
            def _():
                pack_rows(after)
                send_across(after)

        def step_body(step, carry):
            @pl.when(step == 0)
            def _():
                set_up()

            def prepare():
                @pl.when(step == 0)
                def _():
                    for there, src, dst, land, far, near, s, b in init_copies():
                        @pl.when(there)
                        def _():
                            got = remote(src, land, isend.at[near], irecv.at[near], s, b)
                            got.wait_recv()
                            got.wait_send()

            first_sweep(0, step, True, None, prepare)

            def current(x):
                def store(value):
                    JA[step, x] = value
                own_v = jnp.broadcast_to(own[0:1], (Y, Z))
                value = 2.0 * B[x + 2, rows, :] - (EB[x + 1] + 6.0) * A[x + 2, rows, :]
                return own_v * value, store
            for_planes(0, X, 4, current)

            @pl.when(sec != heart - 2)
            def _():
                current_copy(step).start()

            flags = [jnp.where(PR[i] == section, 1.0, 0.0) for i in range(2)]

            def place(flag):
                def work(x):
                    value = jnp.broadcast_to(flag[0:1], (Y, Z)) * GB[step, x + 1]

                    def store(value):
                        BB[x + 1] = value
                        B[x + 2, rows, :] = B[x + 2, rows, :] + 0.5 * value
                    return value, store
                return work
            for n, (low, count) in enumerate(parts):
                @pl.when(jnp.logical_or(sec != heart - 2, step == 0))
                def _():
                    wait_source(step, n)

                @pl.when(jnp.logical_and(sec == heart - 2, step == 0))
                def _():
                    relay_source(step, n).start()
                if n in inner:
                    for_planes(low - 1, count, 5, place(own))
                else:
                    for x in (low - 1, low):
                        value, store = place({-1: flags[0], X: flags[1]}.get(x, own))(x)
                        store(value)

            for j, at in ((0, Y - 1), (1, 0)):
                flat, where = across(GB, at, step * (X + 2) + 1, X, Y)
                BR[j] = jnp.broadcast_to(own_y[j][0:1], (X, Z)) * flat[where, :]
                R2[j] = R2[j] + 0.5 * BR[j]
            second_sweep(0, push[1], None, True)

            def group(g, carry):
                slot = lax.rem(g, 2)

                @pl.when(jnp.logical_and(g == 1, sec == heart - 2))
                def _():
                    remote(JB.at[step, 0], JB.at[step, 0], jsend.at[step], jrecv.at[step, 0],
                           heart, brick).wait_recv()

                    def add(x):
                        def store(value):
                            JA[step, x] = value
                        return JA[step, x] + JB[step, 0, x], store
                    for_planes(0, X, 4, add)
                    current_copy(step).start()

                @pl.when(jnp.logical_and(jnp.logical_and(g == GROUPS - 3, step + 1 < STEPS),
                                         sec == heart - 2))
                def _():
                    for n in range(len(parts)):
                        wait_source(step + 1, n)
                        relay_source(step + 1, n).start()

                first = push[2 * g]
                first_sweep(slot, g, False, first)
                going_on = step < STEPS - 1
                second_sweep(slot, push[2 * g + 1], jnp.where(going_on, push[SWEEPS + g], 1.0),
                             jnp.logical_or(g < GROUPS - 1, going_on))
                return carry

            lax.fori_loop(1, GROUPS, group, 0)
            return carry

        pack_planes(0)
        send_beside(0)
        pack_rows(0)
        send_across(0)
        lax.fori_loop(0, STEPS, step_body, 0)

        result = pltpu.make_async_copy(A.at[pl.ds(2, X), rows], out.at[0], lsem.at[0])
        result.start()
        wait_sent((GROUPS - 1) % 2)
        for step in range(STEPS):
            current_copy(step).wait_send()

            @pl.when(sec == heart - 2)
            def _():
                for n in range(len(parts)):
                    relay_source(step, n).wait_send()

        result.wait()

    pl.when(is_heart)(heart_program)
    pl.when(jnp.logical_not(is_heart))(torso_program)


def body(mesh, potentials, coefficient, recovery, excitable, row_of):
    sections, bricks = mesh.shape["sec"], mesh.shape["brick"]
    _, X, Y, Z = potentials.shape
    f32 = jnp.float32
    scratch = [
        ((X + 4, Y + 2 * PAD, Z), f32), ((X + 4, Y + 2 * PAD, Z), f32),
        ((X + 2, Y, Z), f32), ((STEPS, X + 2, Y, Z), f32), ((X + 2, Y, Z), f32),
        ((STEPS, X, Y, Z), f32), ((STEPS, 2, X, Y, Z), f32),
        ((X, Y, Z), f32), ((X, Y, Z), f32), ((X, Y, Z), jnp.int32),
        ((2, 4 * (X + Y) + 32, Z), f32), ((2, 4 * (X + Y) + 32, Z), f32),
        ((2, 4 * (X + Y) + 32, Z), f32), ((2 * max(X, Y), Z), f32),
        ((2, X + 2 * PAD, Z), f32), ((2, X, Z), f32),
        ((2, X, Z), f32), ((2, X, Z), f32), ((2, X, Z), f32),
        ((2, 8, Z), f32), ((STEPS + 1, 2, 2, Y, Z), f32), ((8, Z), f32),
    ]
    sems = [(4,), (2,), (2,), (6,), (6,), (STEPS, 5, 3), (STEPS, 5), (STEPS,), (STEPS, 2),
            (2,), (STEPS + 1, 2)]
    hbm = pl.BlockSpec(memory_space=pltpu.HBM)
    cells = X * Y * Z
    fields = pl.pallas_call(
        functools.partial(kernel, sections, bricks),
        out_shape=jax.ShapeDtypeStruct(potentials.shape, f32),
        in_specs=[hbm] * 4 + [pl.BlockSpec(memory_space=pltpu.SMEM)],
        out_specs=hbm,
        scratch_shapes=[pltpu.VMEM(s, t) for s, t in scratch]
        + [pltpu.SMEM((len(PUSHES),), f32)]
        + [pltpu.SemaphoreType.DMA(s) for s in sems],
        compiler_params=pltpu.CompilerParams(
            collective_id=0, has_side_effects=True, vmem_limit_bytes=63 * 2**20 + 2**19),
        cost_estimate=pl.CostEstimate(
            flops=cells * STEPS * SWEEPS * 12, bytes_accessed=20 * cells, transcendentals=0),
    )(potentials, coefficient, recovery, excitable, row_of)
    torso = lax.axis_index("sec") < sections - 1
    return fields * jnp.where(torso, PUSHES[-1], 1.0).astype(f32)


def solution(mesh):
    in_specs = (
        P("sec", "brick", None, None),
        P("sec", "brick", None, None),
        P("brick", None, None),
        P("brick", None, None),
        P("brick"),
    )
    out_specs = P("sec", "brick", None, None)
    return jax.shard_map(functools.partial(body, mesh), mesh=mesh, in_specs=in_specs,
                         out_specs=out_specs, check_vma=False)
```

```python
import functools

import jax
import jax.numpy as jnp
from jax import lax
from jax.experimental import pallas as pl
from jax.experimental.pallas import tpu as pltpu
from jax.sharding import PartitionSpec as P

SUBSTEPS = 8
SWEEPS = 16
STEPS = 2
GROUPS = SWEEPS // 2

coupling_gain = 0.1
ionic_timestep = 0.05
ionic_gain = 8.0
recovery_rate = 0.1
recovery_decay = 0.5
spectrum_low = 0.04
spectrum_high = 12.32

center = 0.5 * (spectrum_high + spectrum_low)
spread = 0.5 * (spectrum_high - spectrum_low)
back = (0.5 * spread) ** 2


def push_weights():
    ratio = center / spread
    values = [1.0, ratio]
    while len(values) <= SWEEPS:
        values.append(2.0 * ratio * values[-1] - values[-2])
    grown = [(0.5 * spread) ** k * values[k] for k in range(SWEEPS + 1)]
    return grown[:SWEEPS] + [1.0] * (GROUPS - 1) + [1.0 / grown[SWEEPS]]


PUSHES = push_weights()
MESH = pl.DeviceIdType.MESH
PAD = 8
DIAGONAL = ((0, 0), (0, 1), (1, 0), (1, 1))


def largest_divisor(count, limit):
    return max(u for u in range(1, limit + 1) if count % u == 0)


def for_planes(first, count, limit, work):
    unroll = largest_divisor(count, limit)

    def chunk(i, carry):
        done = [work(first + i * unroll + j) for j in range(unroll)]
        for value, store in done:
            store(value)
        return carry

    lax.fori_loop(0, count // unroll, chunk, 0)


def in_line(first, count, work):
    for x in range(first, first + count):
        value, store = work(x)
        store(value)


def kernel(sections, bricks, pot, coef, rec, exc, row_of, out,
           A, B, EB, GB, BB, JA, JB, W, T, M, H, S, DUMP, ZB, R, R2, ER, SE, BR, PR, VH, row, push,
           lsem, sent, landing, isend, irecv, gsend, grecv, jsend, jrecv, vsend, vrecv):
    X, Y, Z = W.shape
    sec = lax.axis_index("sec")
    brick = lax.axis_index("brick")
    heart = sections - 1
    is_heart = sec == heart
    has_x = (brick > 0, brick < bricks - 1)
    to_x = (brick - 1, brick + 1)
    has_y = (jnp.logical_and(sec > 0, sec < heart), sec < heart - 1)
    to_y = (sec - 1, sec + 1)
    rows = pl.ds(PAD, Y)
    lane = lax.broadcasted_iota(jnp.int32, (Y, Z), 1)
    lane_x = lax.broadcasted_iota(jnp.int32, (X, Z), 1)

    def across(buf, at, first, count, pitch):
        return buf.reshape(buf.size // Z, Z), pl.ds(first * pitch + at, count, stride=pitch)

    def remote(src, dst, send, recv, s, b):
        return pltpu.make_async_remote_copy(
            src_ref=src, dst_ref=dst, send_sem=send, recv_sem=recv,
            device_id={"sec": s, "brick": b}, device_id_type=MESH)

    for n, value in enumerate(PUSHES):
        push[n] = jnp.float32(value)
    field = pltpu.make_async_copy(pot.at[0], A.at[pl.ds(2, X), rows], lsem.at[0])
    second = pltpu.make_async_copy(coef.at[0], T, lsem.at[1])
    field.start()
    second.start()

    barrier = pltpu.get_barrier_semaphore()

    @pl.when(jnp.logical_not(is_heart))
    def _():
        def clear(i, carry):
            for buf in (A, B):
                buf[i, 0:PAD, :] = jnp.zeros((PAD, Z), jnp.float32)
                buf[i, pl.ds(PAD + Y, PAD), :] = jnp.zeros((PAD, Z), jnp.float32)
            return carry

        lax.fori_loop(0, X + 4, clear, 0)
        for buf in (ZB, ER, R2):
            buf[...] = jnp.zeros(buf.shape, jnp.float32)
        EB[0] = jnp.zeros((Y, Z), jnp.float32)
        EB[X + 1] = jnp.zeros((Y, Z), jnp.float32)
        PR[...] = jnp.full(PR.shape, -1.0, jnp.float32)
        row[...] = jnp.full(row.shape, row_of[0].astype(jnp.float32), jnp.float32)

    for d in range(1, sections):
        pl.semaphore_signal(barrier, inc=1, device_id={"sec": lax.rem(sec + d, sections)},
                            device_id_type=MESH)
    total = sections - 1
    for i in range(2):
        @pl.when(has_x[i])
        def _():
            pl.semaphore_signal(barrier, inc=1, device_id={"sec": sec, "brick": to_x[i]},
                                device_id_type=MESH)
        total = total + has_x[i].astype(jnp.int32)
    for i, j in DIAGONAL:
        both = jnp.logical_and(has_x[i], has_y[j])

        @pl.when(both)
        def _():
            pl.semaphore_signal(barrier, inc=1, device_id={"sec": to_y[j], "brick": to_x[i]},
                                device_id_type=MESH)
        total = total + both.astype(jnp.int32)
    pl.semaphore_wait(barrier, total)
    field.wait()

    cuts = largest_divisor(X - 2, 3)
    size = (X - 2) // cuts
    parts = [(2 + n * size, size) for n in range(cuts)] + [(0, 2), (X, 2)]
    inner, outer = range(cuts), range(cuts, cuts + 2)

    def source_copy(step, n, lane_number, target):
        ref = GB.at[step, pl.ds(parts[n][0], parts[n][1])]
        return remote(ref, ref, gsend.at[step, n, lane_number], grecv.at[step, n], target, brick)

    def heart_program():
        recover = pltpu.make_async_copy(rec, W, lsem.at[2])
        excite = pltpu.make_async_copy(exc, M, lsem.at[3])
        recover.start()
        excite.start()

        def send_sides(round_number):
            for i in range(2):
                src = A.at[pl.ds(2, 2) if i == 0 else pl.ds(X, 2), rows]

                @pl.when(has_x[i])
                def _():
                    remote(src, VH.at[round_number, 1 - i], vsend.at[i],
                           vrecv.at[round_number, 1 - i], sec, to_x[i]).start()

        def sides(round_number):
            for i in range(2):
                src = A.at[pl.ds(2, 2) if i == 0 else pl.ds(X, 2), rows]
                at = 0 if i == 0 else X + 2

                @pl.when(has_x[i])
                def _():
                    got = remote(src, VH.at[round_number, i], vsend.at[i],
                                 vrecv.at[round_number, i], sec, to_x[i])
                    got.wait_recv()
                    got.wait_send()
                    for j in range(2):
                        A[at + j, rows, :] = VH[round_number, i, j]

                @pl.when(jnp.logical_not(has_x[i]))
                def _():
                    for j in range(2):
                        A[at + j, rows, :] = A[2 if i == 0 else X + 1, rows, :]

            edge_rows(0, 2)
            edge_rows(X + 2, X + 4)

        def edge_rows(low, high):
            def edge(i, carry):
                A[i, pl.ds(PAD - 1, 1), :] = A[i, pl.ds(PAD, 1), :]
                A[i, pl.ds(PAD + Y, 1), :] = A[i, pl.ds(PAD + Y - 1, 1), :]
                return carry

            lax.fori_loop(low, high, edge, 0)

        def laplace(x):
            c = A[x + 2, rows, :]
            total = A[x + 1, rows, :] + A[x + 3, rows, :]
            total = total + A[x + 2, pl.ds(PAD - 1, Y), :] + A[x + 2, pl.ds(PAD + 1, Y), :]
            total = total + jnp.where(lane == 0, c, pltpu.roll(c, 1, 1))
            total = total + jnp.where(lane == Z - 1, c, pltpu.roll(c, Z - 1, 1))
            return total - 6.0 * c

        def ionic(x):
            v = A[x + 2, rows, :]
            w = W[x]
            thresh = T[x]
            active = ionic_timestep * M[x].astype(jnp.float32)
            for _ in range(SUBSTEPS):
                drive = ionic_gain * v * (v - thresh) * (1.0 - v) - w
                relax = recovery_rate * (v - recovery_decay * w)
                v = v + active * drive
                w = w + active * relax

            def store(value):
                A[x + 2, rows, :] = value[0]
                W[x] = value[1]
            return (v, w), store

        def source(step, chunks):
            def work(x):
                def store(value):
                    GB[step, x + 1] = value
                return laplace(x), store
            for n in chunks:
                low, count = parts[n]
                for_planes(low - 1, count, 5, work)
                for far in (2, 1):
                    source_copy(step, n, far - 1, heart - far).start()

        def current(step):
            for n in range(2):
                remote(JB.at[step, n], JB.at[step, n], jsend.at[step], jrecv.at[step, n],
                       heart - 1 - n, brick).wait_recv()

        edge_rows(2, X + 2)
        send_sides(0)
        source(0, inner)
        sides(0)
        source(0, outer)
        second.wait()
        recover.wait()
        excite.wait()
        for step in range(STEPS):
            for_planes(0, X, 2, ionic)
            send_sides(step + 1)
            edge_rows(2, X + 2)
            sides(step + 1)
            if step + 1 < STEPS:
                source(step + 1, range(len(parts)))
                current(step)

                def advance(x):
                    def store(value):
                        A[x + 2, rows, :] = value
                    gain = GB[step + 1, x + 1] + (JB[step, 0, x] + JB[step, 1, x])
                    return A[x + 2, rows, :] + coupling_gain * gain, store
                for_planes(0, X, 4, advance)
            else:
                def before(x):
                    def store(value):
                        BB[x] = value
                    return A[x + 2, rows, :] + coupling_gain * laplace(x), store
                for_planes(0, X, 4, before)
                current(step)

                def final(x):
                    def store(value):
                        BB[x] = value
                    return BB[x] + coupling_gain * (JB[step, 0, x] + JB[step, 1, x]), store
                for_planes(0, X, 4, final)
                result = pltpu.make_async_copy(BB.at[pl.ds(0, X)], out.at[0], lsem.at[0])
                result.start()
                result.wait()
        for step in range(STEPS):
            for n in range(len(parts)):
                for far in (2, 1):
                    source_copy(step, n, far - 1, heart - far).wait_send()

    def torso_program():
        one = jnp.ones((), jnp.float32)
        zero = jnp.zeros((), jnp.float32)
        inside_x = [jnp.where(h, one, zero) for h in has_x]
        inside_y = [jnp.where(h, one, zero) for h in has_y]
        section = sec.astype(jnp.float32)
        own = jnp.where(row[...] == section, 1.0, 0.0)
        own_y = (jnp.where(row[...] == section - 1.0, 1.0, 0.0),
                 jnp.where(row[...] == section + 1.0, 1.0, 0.0))

        at_x = [(2 * Y * i, 2 * Y) for i in range(2)]
        at_y = [(4 * Y + 2 * X * j, 2 * X) for j in range(2)]
        at_c = [(4 * (X + Y) + 8 * n, 8) for n in range(4)]

        def message(slot, there, here, s, b):
            there_at, here_at = pl.ds(*there), pl.ds(*here)
            return remote(S.at[slot, here_at], H.at[slot, there_at], sent.at[slot],
                          landing.at[slot], s, b)

        def nothing(slot, here):
            zeros = ZB.at[pl.ds(0, here[1])]
            pltpu.make_async_copy(zeros, H.at[slot, pl.ds(*here)], landing.at[slot]).start()
            pltpu.make_async_copy(zeros, DUMP.at[slot, pl.ds(*here)], sent.at[slot]).start()

        def send_beside(slot):
            for n, (i, j) in enumerate(DIAGONAL):
                both = jnp.logical_and(has_x[i], has_y[j])

                @pl.when(both)
                def _():
                    message(slot, at_c[3 - n], at_c[n], to_y[j], to_x[i]).start()

                @pl.when(jnp.logical_not(both))
                def _():
                    nothing(slot, at_c[n])

            def send_planes(i):
                @pl.when(has_x[i])
                def _():
                    message(slot, at_x[1 - i], at_x[i], sec, to_x[i]).start()

                @pl.when(jnp.logical_not(has_x[i]))
                def _():
                    nothing(slot, at_x[i])

            even = lax.rem(brick, 2) == 0

            @pl.when(even)
            def _():
                send_planes(0)
                send_planes(1)

            @pl.when(jnp.logical_not(even))
            def _():
                send_planes(1)
                send_planes(0)

        def send_across(slot):
            for j in range(2):
                @pl.when(has_y[j])
                def _():
                    message(slot, at_y[1 - j], at_y[j], to_y[j], brick).start()

                @pl.when(jnp.logical_not(has_y[j]))
                def _():
                    nothing(slot, at_y[j])

        def wait_landed(slot):
            pltpu.make_async_copy(S.at[slot], H.at[slot], landing.at[slot]).wait()

        def wait_sent(slot):
            pltpu.make_async_copy(S.at[slot], DUMP.at[slot], sent.at[slot]).wait()

        def pack_rows(slot):
            for j in range(2):
                for n in range(2):
                    at = PAD + n if j == 0 else PAD + Y - 1 - n
                    flat, where = across(A, at, 2, X, Y + 2 * PAD)
                    S[slot, pl.ds(at_y[j][0] + n * X, X), :] = flat[where, :]

        def pack_planes(slot):
            for i in range(2):
                for n in range(2):
                    value = A[(2 if i == 0 else X) + n, rows, :]
                    S[slot, pl.ds(at_x[i][0] + n * Y, Y), :] = value
            for n, (i, j) in enumerate(DIAGONAL):
                corner = A[2 if i == 0 else X + 1, pl.ds(PAD if j == 0 else PAD + Y - 1, 1), :]
                S[slot, pl.ds(at_c[n][0], 1), :] = corner

        def stencil(src, x):
            c = src[x + 2, rows, :]
            total = src[x + 1, rows, :] + src[x + 3, rows, :]
            total = total + (src[x + 2, pl.ds(PAD - 1, Y), :] + src[x + 2, pl.ds(PAD + 1, Y), :])
            total = total + (jnp.where(lane == 0, 0.0, pltpu.roll(c, 1, 1))
                             + jnp.where(lane == Z - 1, 0.0, pltpu.roll(c, Z - 1, 1)))
            return total + EB[x + 1] * c

        def plane(src, dst, first, weight, scale=None):
            def work(x):
                value = stencil(src, x)
                if first:
                    value = 0.5 * value
                else:
                    value = (value + weight * BB[x + 1]) - back * dst[x + 2, rows, :]
                if scale is not None:
                    value = scale * value

                def store(value):
                    dst[x + 2, rows, :] = value
                return value, store
            return work

        def mend(dst, low, high, halo, offset, scale):
            for j, at in ((0, PAD), (1, PAD + Y - 1)):
                flat, where = across(dst, at, low + 2, high - low, Y + 2 * PAD)
                flat[where, :] = flat[where, :] + scale * halo[j, pl.ds(low + offset, high - low), :]

        def fringe(slot, first, weight):
            for j in range(2):
                c = R[j, pl.ds(PAD, X), :]
                total = R[j, pl.ds(PAD - 1, X), :] + R[j, pl.ds(PAD + 1, X), :]
                total = total + S[slot, pl.ds(at_y[j][0], X), :] + H[slot, pl.ds(at_y[j][0] + X, X), :]
                total = total + jnp.where(lane_x == 0, 0.0, pltpu.roll(c, 1, 1))
                total = total + jnp.where(lane_x == Z - 1, 0.0, pltpu.roll(c, Z - 1, 1))
                total = total + ER[j] * c
                if first:
                    R2[j] = (0.5 * inside_y[j]) * total
                else:
                    R2[j] = inside_y[j] * (total + weight * BR[j] - back * R2[j])

        def landed(slot):
            for j in range(2):
                A[j, rows, :] = H[slot, pl.ds(at_x[0][0] + j * Y, Y), :]
                A[X + 2 + j, rows, :] = H[slot, pl.ds(at_x[1][0] + j * Y, Y), :]
                R[j, pl.ds(PAD, X), :] = H[slot, pl.ds(at_y[j][0], X), :]
            for n, (i, j) in enumerate(DIAGONAL):
                R[j, pl.ds(PAD - 1 if i == 0 else PAD + X, 1), :] = H[slot, pl.ds(at_c[n][0], 1), :]

        def first_sweep(slot, number, first, weight, prepare=lambda: None):
            in_line(1, X - 2, plane(A, B, first, weight))

            @pl.when(number > 0)
            def _():
                wait_sent(1 - slot)
            wait_landed(slot)
            prepare()
            landed(slot)
            done = [plane(A, B, first, weight, scale)(x) for x, scale in
                    ((-1, inside_x[0]), (0, None), (X - 1, None), (X, inside_x[1]))]
            for value, store in done:
                store(value)
            fringe(slot, first, weight)
            mend(B, -1, X + 1, R, PAD, 0.5 if first else 1.0)

        def relay_source(step, n):
            return source_copy(step, n, 2, heart - 3)

        def wait_source(step, n):
            source_copy(step, n, 2, heart).wait_recv()

        def current_copy(step):
            inner = sec == heart - 3
            target = jnp.where(inner, heart - 2, heart)
            place = jnp.where(sec == heart - 2, 1, 0)
            return remote(JA.at[step], JB.at[step, place], jsend.at[step], jrecv.at[step, place],
                          target, brick)

        def init_copies():
            found = []
            for i in range(2):
                found.append((has_x[i], EB.at[1 if i == 0 else X], EB.at[X + 1 if i == 0 else 0],
                              EB.at[0 if i == 0 else X + 1], 1 - i, i, sec, to_x[i]))
                found.append((has_x[i], row, PR.at[1 - i], PR.at[i], 5 - i, 4 + i, sec, to_x[i]))
            for j in range(2):
                found.append((has_y[j], SE.at[j], ER.at[1 - j], ER.at[j], 3 - j, 2 + j,
                              to_y[j], brick))
            return found

        def set_up():
            second.wait()

            def absorb(x):
                def store(value):
                    EB[x + 1] = value
                return (center - 6.0) - T[x], store
            for_planes(0, X, 4, absorb)

            for j, at in ((0, 0), (1, Y - 1)):
                flat, where = across(EB, at, 1, X, Y)
                SE[j] = flat[where, :]
            for there, src, dst, land, far, near, s, b in init_copies():
                @pl.when(there)
                def _():
                    remote(src, dst, isend.at[near], irecv.at[far], s, b).start()

        def second_sweep(slot, weight, scale, more):
            after = 1 - slot
            for j, at in ((0, PAD - 1), (1, PAD + Y)):
                flat, where = across(B, at, 2, X, Y + 2 * PAD)
                flat[where, :] = R2[j]
            work = plane(B, A, False, weight, scale)
            done = [work(x) for x in (0, 1, X - 2, X - 1)]
            for value, store in done:
                store(value)

            @pl.when(more)
            def _():
                pack_planes(after)
                send_beside(after)
            in_line(2, X - 4, work)

            @pl.when(more)
            def _():
                pack_rows(after)
                send_across(after)

        def step_body(step, carry):
            @pl.when(step == 0)
            def _():
                set_up()

            def prepare():
                @pl.when(step == 0)
                def _():
                    for there, src, dst, land, far, near, s, b in init_copies():
                        @pl.when(there)
                        def _():
                            got = remote(src, land, isend.at[near], irecv.at[near], s, b)
                            got.wait_recv()
                            got.wait_send()

            first_sweep(0, step, True, None, prepare)

            def current(x):
                def store(value):
                    JA[step, x] = value
                own_v = jnp.broadcast_to(own[0:1], (Y, Z))
                value = 2.0 * B[x + 2, rows, :] - (EB[x + 1] + 6.0) * A[x + 2, rows, :]
                return own_v * value, store
            for_planes(0, X, 4, current)

            @pl.when(sec != heart - 2)
            def _():
                current_copy(step).start()

            flags = [jnp.where(PR[i] == section, 1.0, 0.0) for i in range(2)]

            def place(flag):
                def work(x):
                    value = jnp.broadcast_to(flag[0:1], (Y, Z)) * GB[step, x + 1]

                    def store(value):
                        BB[x + 1] = value
                        B[x + 2, rows, :] = B[x + 2, rows, :] + 0.5 * value
                    return value, store
                return work
            for n, (low, count) in enumerate(parts):
                @pl.when(jnp.logical_or(sec != heart - 2, step == 0))
                def _():
                    wait_source(step, n)

                @pl.when(jnp.logical_and(sec == heart - 2, step == 0))
                def _():
                    relay_source(step, n).start()
                if n in inner:
                    for_planes(low - 1, count, 5, place(own))
                else:
                    for x in (low - 1, low):
                        value, store = place({-1: flags[0], X: flags[1]}.get(x, own))(x)
                        store(value)

            for j, at in ((0, Y - 1), (1, 0)):
                flat, where = across(GB, at, step * (X + 2) + 1, X, Y)
                BR[j] = jnp.broadcast_to(own_y[j][0:1], (X, Z)) * flat[where, :]
                R2[j] = R2[j] + 0.5 * BR[j]
            second_sweep(0, push[1], None, True)

            def group(g, carry):
                slot = lax.rem(g, 2)

                @pl.when(jnp.logical_and(g == 1, sec == heart - 2))
                def _():
                    remote(JB.at[step, 0], JB.at[step, 0], jsend.at[step], jrecv.at[step, 0],
                           heart, brick).wait_recv()

                    def add(x):
                        def store(value):
                            JA[step, x] = value
                        return JA[step, x] + JB[step, 0, x], store
                    for_planes(0, X, 4, add)
                    current_copy(step).start()

                @pl.when(jnp.logical_and(jnp.logical_and(g == GROUPS - 3, step + 1 < STEPS),
                                         sec == heart - 2))
                def _():
                    for n in range(len(parts)):
                        wait_source(step + 1, n)
                        relay_source(step + 1, n).start()

                first = push[2 * g]
                first_sweep(slot, g, False, first)
                going_on = step < STEPS - 1
                second_sweep(slot, push[2 * g + 1], jnp.where(going_on, push[SWEEPS + g], 1.0),
                             jnp.logical_or(g < GROUPS - 1, going_on))
                return carry

            lax.fori_loop(1, GROUPS, group, 0)
            return carry

        pack_planes(0)
        send_beside(0)
        pack_rows(0)
        send_across(0)
        lax.fori_loop(0, STEPS, step_body, 0)

        result = pltpu.make_async_copy(A.at[pl.ds(2, X), rows], out.at[0], lsem.at[0])
        result.start()
        wait_sent((GROUPS - 1) % 2)
        for step in range(STEPS):
            current_copy(step).wait_send()

            @pl.when(sec == heart - 2)
            def _():
                for n in range(len(parts)):
                    relay_source(step, n).wait_send()

        result.wait()

    pl.when(is_heart)(heart_program)
    pl.when(jnp.logical_not(is_heart))(torso_program)


def body(mesh, potentials, coefficient, recovery, excitable, row_of):
    sections, bricks = mesh.shape["sec"], mesh.shape["brick"]
    _, X, Y, Z = potentials.shape
    f32 = jnp.float32
    scratch = [
        ((X + 4, Y + 2 * PAD, Z), f32), ((X + 4, Y + 2 * PAD, Z), f32),
        ((X + 2, Y, Z), f32), ((STEPS, X + 2, Y, Z), f32), ((X + 2, Y, Z), f32),
        ((STEPS, X, Y, Z), f32), ((STEPS, 2, X, Y, Z), f32),
        ((X, Y, Z), f32), ((X, Y, Z), f32), ((X, Y, Z), jnp.int32),
        ((2, 4 * (X + Y) + 32, Z), f32), ((2, 4 * (X + Y) + 32, Z), f32),
        ((2, 4 * (X + Y) + 32, Z), f32), ((2 * max(X, Y), Z), f32),
        ((2, X + 2 * PAD, Z), f32), ((2, X, Z), f32),
        ((2, X, Z), f32), ((2, X, Z), f32), ((2, X, Z), f32),
        ((2, 8, Z), f32), ((STEPS + 1, 2, 2, Y, Z), f32), ((8, Z), f32),
    ]
    sems = [(4,), (2,), (2,), (6,), (6,), (STEPS, 5, 3), (STEPS, 5), (STEPS,), (STEPS, 2),
            (2,), (STEPS + 1, 2)]
    hbm = pl.BlockSpec(memory_space=pltpu.HBM)
    cells = X * Y * Z
    fields = pl.pallas_call(
        functools.partial(kernel, sections, bricks),
        out_shape=jax.ShapeDtypeStruct(potentials.shape, f32),
        in_specs=[hbm] * 4 + [pl.BlockSpec(memory_space=pltpu.SMEM)],
        out_specs=hbm,
        scratch_shapes=[pltpu.VMEM(s, t) for s, t in scratch]
        + [pltpu.SMEM((len(PUSHES),), f32)]
        + [pltpu.SemaphoreType.DMA(s) for s in sems],
        compiler_params=pltpu.CompilerParams(
            collective_id=0, has_side_effects=True, vmem_limit_bytes=63 * 2**20 + 2**19),
        cost_estimate=pl.CostEstimate(
            flops=cells * STEPS * SWEEPS * 12, bytes_accessed=20 * cells, transcendentals=0),
    )(potentials, coefficient, recovery, excitable, row_of)
    torso = lax.axis_index("sec") < sections - 1
    return fields * jnp.where(torso, PUSHES[-1], 1.0).astype(f32)


def solution(mesh):
    in_specs = (
        P("sec", "brick", None, None),
        P("sec", "brick", None, None),
        P("brick", None, None),
        P("brick", None, None),
        P("brick"),
    )
    out_specs = P("sec", "brick", None, None)
    return jax.shard_map(functools.partial(body, mesh), mesh=mesh, in_specs=in_specs,
                         out_specs=out_specs, check_vma=False)
```

```python
import functools

import jax
import jax.numpy as jnp
from jax import lax
from jax.experimental import pallas as pl
from jax.experimental.pallas import tpu as pltpu
from jax.sharding import PartitionSpec as P

SUBSTEPS = 8
SWEEPS = 16
STEPS = 2
GROUPS = SWEEPS // 2

coupling_gain = 0.1
ionic_timestep = 0.05
ionic_gain = 8.0
recovery_rate = 0.1
recovery_decay = 0.5
spectrum_low = 0.04
spectrum_high = 12.32

center = 0.5 * (spectrum_high + spectrum_low)
spread = 0.5 * (spectrum_high - spectrum_low)
back = (0.5 * spread) ** 2


def push_weights():
    ratio = center / spread
    values = [1.0, ratio]
    while len(values) <= SWEEPS:
        values.append(2.0 * ratio * values[-1] - values[-2])
    grown = [(0.5 * spread) ** k * values[k] for k in range(SWEEPS + 1)]
    return grown[:SWEEPS] + [1.0] * (GROUPS - 1) + [1.0 / grown[SWEEPS]]


PUSHES = push_weights()
MESH = pl.DeviceIdType.MESH
PAD = 8
DIAGONAL = ((0, 0), (0, 1), (1, 0), (1, 1))


def largest_divisor(count, limit):
    return max(u for u in range(1, limit + 1) if count % u == 0)


def for_planes(first, count, limit, work):
    unroll = largest_divisor(count, limit)

    def chunk(i, carry):
        done = [work(first + i * unroll + j) for j in range(unroll)]
        for value, store in done:
            store(value)
        return carry

    lax.fori_loop(0, count // unroll, chunk, 0)


def in_line(first, count, work):
    for x in range(first, first + count):
        value, store = work(x)
        store(value)


def kernel(sections, bricks, pot, coef, rec, exc, row_of, out,
           A, B, EB, GB, BB, JA, JB, W, T, M, H, S, DUMP, ZB, R, R2, ER, SE, BR, PR, VH, row, push,
           lsem, sent, landing, isend, irecv, gsend, grecv, jsend, jrecv, vsend, vrecv):
    X, Y, Z = W.shape
    sec = lax.axis_index("sec")
    brick = lax.axis_index("brick")
    heart = sections - 1
    is_heart = sec == heart
    has_x = (brick > 0, brick < bricks - 1)
    to_x = (brick - 1, brick + 1)
    has_y = (jnp.logical_and(sec > 0, sec < heart), sec < heart - 1)
    to_y = (sec - 1, sec + 1)
    rows = pl.ds(PAD, Y)
    lane = lax.broadcasted_iota(jnp.int32, (Y, Z), 1)
    lane_x = lax.broadcasted_iota(jnp.int32, (X, Z), 1)

    def across(buf, at, first, count, pitch):
        return buf.reshape(buf.size // Z, Z), pl.ds(first * pitch + at, count, stride=pitch)

    def remote(src, dst, send, recv, s, b):
        return pltpu.make_async_remote_copy(
            src_ref=src, dst_ref=dst, send_sem=send, recv_sem=recv,
            device_id={"sec": s, "brick": b}, device_id_type=MESH)

    for n, value in enumerate(PUSHES):
        push[n] = jnp.float32(value)
    field = pltpu.make_async_copy(pot.at[0], A.at[pl.ds(2, X), rows], lsem.at[0])
    second = pltpu.make_async_copy(coef.at[0], T, lsem.at[1])
    field.start()
    second.start()

    barrier = pltpu.get_barrier_semaphore()

    @pl.when(jnp.logical_not(is_heart))
    def _():
        def clear(i, carry):
            for buf in (A, B):
                buf[i, 0:PAD, :] = jnp.zeros((PAD, Z), jnp.float32)
                buf[i, pl.ds(PAD + Y, PAD), :] = jnp.zeros((PAD, Z), jnp.float32)
            return carry

        lax.fori_loop(0, X + 4, clear, 0)
        for buf in (ZB, ER, R2):
            buf[...] = jnp.zeros(buf.shape, jnp.float32)
        EB[0] = jnp.zeros((Y, Z), jnp.float32)
        EB[X + 1] = jnp.zeros((Y, Z), jnp.float32)
        PR[...] = jnp.full(PR.shape, -1.0, jnp.float32)
        row[...] = jnp.full(row.shape, row_of[0].astype(jnp.float32), jnp.float32)

    for d in range(1, sections):
        pl.semaphore_signal(barrier, inc=1, device_id={"sec": lax.rem(sec + d, sections)},
                            device_id_type=MESH)
    total = sections - 1
    for i in range(2):
        @pl.when(has_x[i])
        def _():
            pl.semaphore_signal(barrier, inc=1, device_id={"sec": sec, "brick": to_x[i]},
                                device_id_type=MESH)
        total = total + has_x[i].astype(jnp.int32)
    for i, j in DIAGONAL:
        both = jnp.logical_and(has_x[i], has_y[j])

        @pl.when(both)
        def _():
            pl.semaphore_signal(barrier, inc=1, device_id={"sec": to_y[j], "brick": to_x[i]},
                                device_id_type=MESH)
        total = total + both.astype(jnp.int32)
    pl.semaphore_wait(barrier, total)
    field.wait()

    cuts = largest_divisor(X - 2, 3)
    size = (X - 2) // cuts
    parts = [(2 + n * size, size) for n in range(cuts)] + [(0, 2), (X, 2)]
    inner, outer = range(cuts), range(cuts, cuts + 2)

    def source_copy(step, n, lane_number, target):
        ref = GB.at[step, pl.ds(parts[n][0], parts[n][1])]
        return remote(ref, ref, gsend.at[step, n, lane_number], grecv.at[step, n], target, brick)

    def heart_program():
        recover = pltpu.make_async_copy(rec, W, lsem.at[2])
        excite = pltpu.make_async_copy(exc, M, lsem.at[3])
        recover.start()
        excite.start()

        def send_sides(round_number):
            for i in range(2):
                src = A.at[pl.ds(2, 2) if i == 0 else pl.ds(X, 2), rows]

                @pl.when(has_x[i])
                def _():
                    remote(src, VH.at[round_number, 1 - i], vsend.at[i],
                           vrecv.at[round_number, 1 - i], sec, to_x[i]).start()

        def sides(round_number):
            for i in range(2):
                src = A.at[pl.ds(2, 2) if i == 0 else pl.ds(X, 2), rows]
                at = 0 if i == 0 else X + 2

                @pl.when(has_x[i])
                def _():
                    got = remote(src, VH.at[round_number, i], vsend.at[i],
                                 vrecv.at[round_number, i], sec, to_x[i])
                    got.wait_recv()
                    got.wait_send()
                    for j in range(2):
                        A[at + j, rows, :] = VH[round_number, i, j]

                @pl.when(jnp.logical_not(has_x[i]))
                def _():
                    for j in range(2):
                        A[at + j, rows, :] = A[2 if i == 0 else X + 1, rows, :]

            edge_rows(0, 2)
            edge_rows(X + 2, X + 4)

        def edge_rows(low, high):
            def edge(i, carry):
                A[i, pl.ds(PAD - 1, 1), :] = A[i, pl.ds(PAD, 1), :]
                A[i, pl.ds(PAD + Y, 1), :] = A[i, pl.ds(PAD + Y - 1, 1), :]
                return carry

            lax.fori_loop(low, high, edge, 0)

        def laplace(x):
            c = A[x + 2, rows, :]
            total = A[x + 1, rows, :] + A[x + 3, rows, :]
            total = total + A[x + 2, pl.ds(PAD - 1, Y), :] + A[x + 2, pl.ds(PAD + 1, Y), :]
            total = total + jnp.where(lane == 0, c, pltpu.roll(c, 1, 1))
            total = total + jnp.where(lane == Z - 1, c, pltpu.roll(c, Z - 1, 1))
            return total - 6.0 * c

        def ionic(x):
            v = A[x + 2, rows, :]
            w = W[x]
            thresh = T[x]
            active = ionic_timestep * M[x].astype(jnp.float32)
            for _ in range(SUBSTEPS):
                drive = ionic_gain * v * (v - thresh) * (1.0 - v) - w
                relax = recovery_rate * (v - recovery_decay * w)
                v = v + active * drive
                w = w + active * relax

            def store(value):
                A[x + 2, rows, :] = value[0]
                W[x] = value[1]
            return (v, w), store

        def source(step, chunks):
            def work(x):
                def store(value):
                    GB[step, x + 1] = value
                return laplace(x), store
            for n in chunks:
                low, count = parts[n]
                for_planes(low - 1, count, 5, work)
                for far in (2, 1):
                    source_copy(step, n, far - 1, heart - far).start()

        def current(step):
            for n in range(2):
                remote(JB.at[step, n], JB.at[step, n], jsend.at[step], jrecv.at[step, n],
                       heart - 1 - n, brick).wait_recv()

        edge_rows(2, X + 2)
        send_sides(0)
        source(0, inner)
        sides(0)
        source(0, outer)
        second.wait()
        recover.wait()
        excite.wait()
        for step in range(STEPS):
            for_planes(0, X, 2, ionic)
            send_sides(step + 1)
            edge_rows(2, X + 2)
            sides(step + 1)
            if step + 1 < STEPS:
                source(step + 1, range(len(parts)))
                current(step)

                def advance(x):
                    def store(value):
                        A[x + 2, rows, :] = value
                    gain = GB[step + 1, x + 1] + (JB[step, 0, x] + JB[step, 1, x])
                    return A[x + 2, rows, :] + coupling_gain * gain, store
                for_planes(0, X, 4, advance)
            else:
                def before(x):
                    def store(value):
                        BB[x] = value
                    return A[x + 2, rows, :] + coupling_gain * laplace(x), store
                for_planes(0, X, 4, before)
                current(step)

                def final(x):
                    def store(value):
                        BB[x] = value
                    return BB[x] + coupling_gain * (JB[step, 0, x] + JB[step, 1, x]), store
                for_planes(0, X, 4, final)
                result = pltpu.make_async_copy(BB.at[pl.ds(0, X)], out.at[0], lsem.at[0])
                result.start()
                result.wait()
        for step in range(STEPS):
            for n in range(len(parts)):
                for far in (2, 1):
                    source_copy(step, n, far - 1, heart - far).wait_send()

    def torso_program():
        one = jnp.ones((), jnp.float32)
        zero = jnp.zeros((), jnp.float32)
        inside_x = [jnp.where(h, one, zero) for h in has_x]
        inside_y = [jnp.where(h, one, zero) for h in has_y]
        section = sec.astype(jnp.float32)
        own = jnp.where(row[...] == section, 1.0, 0.0)
        own_y = (jnp.where(row[...] == section - 1.0, 1.0, 0.0),
                 jnp.where(row[...] == section + 1.0, 1.0, 0.0))

        at_x = [(2 * Y * i, 2 * Y) for i in range(2)]
        at_y = [(4 * Y + 2 * X * j, 2 * X) for j in range(2)]
        at_c = [(4 * (X + Y) + 8 * n, 8) for n in range(4)]

        def message(slot, there, here, s, b):
            there_at, here_at = pl.ds(*there), pl.ds(*here)
            return remote(S.at[slot, here_at], H.at[slot, there_at], sent.at[slot],
                          landing.at[slot], s, b)

        def nothing(slot, here):
            zeros = ZB.at[pl.ds(0, here[1])]
            pltpu.make_async_copy(zeros, H.at[slot, pl.ds(*here)], landing.at[slot]).start()
            pltpu.make_async_copy(zeros, DUMP.at[slot, pl.ds(*here)], sent.at[slot]).start()

        def send_corners(slot):
            for n, (i, j) in enumerate(DIAGONAL):
                both = jnp.logical_and(has_x[i], has_y[j])

                @pl.when(both)
                def _():
                    message(slot, at_c[3 - n], at_c[n], to_y[j], to_x[i]).start()

                @pl.when(jnp.logical_not(both))
                def _():
                    nothing(slot, at_c[n])

        def send_planes(slot, longer):
            even = lax.rem(brick, 2) == 0
            for i in range(2):
                mine = even if (i == 0) == longer else jnp.logical_not(even)

                @pl.when(jnp.logical_and(mine, has_x[i]))
                def _():
                    message(slot, at_x[1 - i], at_x[i], sec, to_x[i]).start()

                @pl.when(jnp.logical_and(mine, jnp.logical_not(has_x[i])))
                def _():
                    nothing(slot, at_x[i])

        def send_across(slot):
            for j in range(2):
                @pl.when(has_y[j])
                def _():
                    message(slot, at_y[1 - j], at_y[j], to_y[j], brick).start()

                @pl.when(jnp.logical_not(has_y[j]))
                def _():
                    nothing(slot, at_y[j])

        def wait_landed(slot):
            pltpu.make_async_copy(S.at[slot], H.at[slot], landing.at[slot]).wait()

        def wait_sent(slot):
            pltpu.make_async_copy(S.at[slot], DUMP.at[slot], sent.at[slot]).wait()

        def pack_rows(slot):
            for j in range(2):
                for n in range(2):
                    at = PAD + n if j == 0 else PAD + Y - 1 - n
                    flat, where = across(A, at, 2, X, Y + 2 * PAD)
                    S[slot, pl.ds(at_y[j][0] + n * X, X), :] = flat[where, :]

        def pack_planes(slot):
            for i in range(2):
                for n in range(2):
                    value = A[(2 if i == 0 else X) + n, rows, :]
                    S[slot, pl.ds(at_x[i][0] + n * Y, Y), :] = value
            for n, (i, j) in enumerate(DIAGONAL):
                corner = A[2 if i == 0 else X + 1, pl.ds(PAD if j == 0 else PAD + Y - 1, 1), :]
                S[slot, pl.ds(at_c[n][0], 1), :] = corner

        def stencil(src, x):
            c = src[x + 2, rows, :]
            total = src[x + 1, rows, :] + src[x + 3, rows, :]
            total = total + (src[x + 2, pl.ds(PAD - 1, Y), :] + src[x + 2, pl.ds(PAD + 1, Y), :])
            total = total + (jnp.where(lane == 0, 0.0, pltpu.roll(c, 1, 1))
                             + jnp.where(lane == Z - 1, 0.0, pltpu.roll(c, Z - 1, 1)))
            return total + EB[x + 1] * c

        def plane(src, dst, first, weight, scale=None):
            def work(x):
                value = stencil(src, x)
                if first:
                    value = 0.5 * value
                else:
                    value = (value + weight * BB[x + 1]) - back * dst[x + 2, rows, :]
                if scale is not None:
                    value = scale * value

                def store(value):
                    dst[x + 2, rows, :] = value
                return value, store
            return work

        def mend(dst, low, high, halo, offset, scale):
            for j, at in ((0, PAD), (1, PAD + Y - 1)):
                flat, where = across(dst, at, low + 2, high - low, Y + 2 * PAD)
                flat[where, :] = flat[where, :] + scale * halo[j, pl.ds(low + offset, high - low), :]

        def fringe(slot, first, weight):
            for j in range(2):
                c = R[j, pl.ds(PAD, X), :]
                total = R[j, pl.ds(PAD - 1, X), :] + R[j, pl.ds(PAD + 1, X), :]
                total = total + S[slot, pl.ds(at_y[j][0], X), :] + H[slot, pl.ds(at_y[j][0] + X, X), :]
                total = total + jnp.where(lane_x == 0, 0.0, pltpu.roll(c, 1, 1))
                total = total + jnp.where(lane_x == Z - 1, 0.0, pltpu.roll(c, Z - 1, 1))
                total = total + ER[j] * c
                if first:
                    R2[j] = (0.5 * inside_y[j]) * total
                else:
                    R2[j] = inside_y[j] * (total + weight * BR[j] - back * R2[j])

        def landed(slot):
            for j in range(2):
                A[j, rows, :] = H[slot, pl.ds(at_x[0][0] + j * Y, Y), :]
                A[X + 2 + j, rows, :] = H[slot, pl.ds(at_x[1][0] + j * Y, Y), :]
                R[j, pl.ds(PAD, X), :] = H[slot, pl.ds(at_y[j][0], X), :]
            for n, (i, j) in enumerate(DIAGONAL):
                R[j, pl.ds(PAD - 1 if i == 0 else PAD + X, 1), :] = H[slot, pl.ds(at_c[n][0], 1), :]

        def first_sweep(slot, number, first, weight, prepare=lambda: None):
            in_line(1, X - 2, plane(A, B, first, weight))

            @pl.when(number > 0)
            def _():
                wait_sent(1 - slot)
            wait_landed(slot)
            prepare()
            landed(slot)
            done = [plane(A, B, first, weight, scale)(x) for x, scale in
                    ((-1, inside_x[0]), (0, None), (X - 1, None), (X, inside_x[1]))]
            for value, store in done:
                store(value)
            fringe(slot, first, weight)
            mend(B, -1, X + 1, R, PAD, 0.5 if first else 1.0)

        def relay_source(step, n):
            return source_copy(step, n, 2, heart - 3)

        def wait_source(step, n):
            source_copy(step, n, 2, heart).wait_recv()

        def current_copy(step):
            inner = sec == heart - 3
            target = jnp.where(inner, heart - 2, heart)
            place = jnp.where(sec == heart - 2, 1, 0)
            return remote(JA.at[step], JB.at[step, place], jsend.at[step], jrecv.at[step, place],
                          target, brick)

        def init_copies():
            found = []
            for i in range(2):
                found.append((has_x[i], EB.at[1 if i == 0 else X], EB.at[X + 1 if i == 0 else 0],
                              EB.at[0 if i == 0 else X + 1], 1 - i, i, sec, to_x[i]))
                found.append((has_x[i], row, PR.at[1 - i], PR.at[i], 5 - i, 4 + i, sec, to_x[i]))
            for j in range(2):
                found.append((has_y[j], SE.at[j], ER.at[1 - j], ER.at[j], 3 - j, 2 + j,
                              to_y[j], brick))
            return found

        def set_up():
            second.wait()

            def absorb(x):
                def store(value):
                    EB[x + 1] = value
                return (center - 6.0) - T[x], store
            for_planes(0, X, 4, absorb)

            for j, at in ((0, 0), (1, Y - 1)):
                flat, where = across(EB, at, 1, X, Y)
                SE[j] = flat[where, :]
            for there, src, dst, land, far, near, s, b in init_copies():
                @pl.when(there)
                def _():
                    remote(src, dst, isend.at[near], irecv.at[far], s, b).start()

        def second_sweep(slot, weight, scale, more):
            after = 1 - slot
            for j, at in ((0, PAD - 1), (1, PAD + Y)):
                flat, where = across(B, at, 2, X, Y + 2 * PAD)
                flat[where, :] = R2[j]
            work = plane(B, A, False, weight, scale)
            done = [work(x) for x in (0, 1, X - 2, X - 1)]
            for value, store in done:
                store(value)

            @pl.when(more)
            def _():
                pack_planes(after)
                send_corners(after)
                send_planes(after, True)
            half = (X - 4) // 2
            in_line(2, half, work)

            @pl.when(more)
            def _():
                send_planes(after, False)
            in_line(2 + half, X - 4 - half, work)

            @pl.when(more)
            def _():
                pack_rows(after)
                send_across(after)

        def step_body(step, carry):
            @pl.when(step == 0)
            def _():
                set_up()

            def prepare():
                @pl.when(step == 0)
                def _():
                    for there, src, dst, land, far, near, s, b in init_copies():
                        @pl.when(there)
                        def _():
                            got = remote(src, land, isend.at[near], irecv.at[near], s, b)
                            got.wait_recv()
                            got.wait_send()

            first_sweep(0, step, True, None, prepare)

            def current(x):
                def store(value):
                    JA[step, x] = value
                own_v = jnp.broadcast_to(own[0:1], (Y, Z))
                value = 2.0 * B[x + 2, rows, :] - (EB[x + 1] + 6.0) * A[x + 2, rows, :]
                return own_v * value, store
            for_planes(0, X, 4, current)

            @pl.when(sec != heart - 2)
            def _():
                current_copy(step).start()

            flags = [jnp.where(PR[i] == section, 1.0, 0.0) for i in range(2)]

            def place(flag):
                def work(x):
                    value = jnp.broadcast_to(flag[0:1], (Y, Z)) * GB[step, x + 1]

                    def store(value):
                        BB[x + 1] = value
                        B[x + 2, rows, :] = B[x + 2, rows, :] + 0.5 * value
                    return value, store
                return work
            for n, (low, count) in enumerate(parts):
                @pl.when(jnp.logical_or(sec != heart - 2, step == 0))
                def _():
                    wait_source(step, n)

                @pl.when(jnp.logical_and(sec == heart - 2, step == 0))
                def _():
                    relay_source(step, n).start()
                if n in inner:
                    for_planes(low - 1, count, 5, place(own))
                else:
                    for x in (low - 1, low):
                        value, store = place({-1: flags[0], X: flags[1]}.get(x, own))(x)
                        store(value)

            for j, at in ((0, Y - 1), (1, 0)):
                flat, where = across(GB, at, step * (X + 2) + 1, X, Y)
                BR[j] = jnp.broadcast_to(own_y[j][0:1], (X, Z)) * flat[where, :]
                R2[j] = R2[j] + 0.5 * BR[j]
            second_sweep(0, push[1], None, True)

            def group(g, carry):
                slot = lax.rem(g, 2)

                @pl.when(jnp.logical_and(g == 1, sec == heart - 2))
                def _():
                    remote(JB.at[step, 0], JB.at[step, 0], jsend.at[step], jrecv.at[step, 0],
                           heart, brick).wait_recv()

                    def add(x):
                        def store(value):
                            JA[step, x] = value
                        return JA[step, x] + JB[step, 0, x], store
                    for_planes(0, X, 4, add)
                    current_copy(step).start()

                @pl.when(jnp.logical_and(jnp.logical_and(g == GROUPS - 3, step + 1 < STEPS),
                                         sec == heart - 2))
                def _():
                    for n in range(len(parts)):
                        wait_source(step + 1, n)
                        relay_source(step + 1, n).start()

                first = push[2 * g]
                first_sweep(slot, g, False, first)
                going_on = step < STEPS - 1
                second_sweep(slot, push[2 * g + 1], jnp.where(going_on, push[SWEEPS + g], 1.0),
                             jnp.logical_or(g < GROUPS - 1, going_on))
                return carry

            lax.fori_loop(1, GROUPS, group, 0)
            return carry

        pack_planes(0)
        send_corners(0)
        send_planes(0, True)
        send_planes(0, False)
        pack_rows(0)
        send_across(0)
        lax.fori_loop(0, STEPS, step_body, 0)

        result = pltpu.make_async_copy(A.at[pl.ds(2, X), rows], out.at[0], lsem.at[0])
        result.start()
        wait_sent((GROUPS - 1) % 2)
        for step in range(STEPS):
            current_copy(step).wait_send()

            @pl.when(sec == heart - 2)
            def _():
                for n in range(len(parts)):
                    relay_source(step, n).wait_send()

        result.wait()

    pl.when(is_heart)(heart_program)
    pl.when(jnp.logical_not(is_heart))(torso_program)


def body(mesh, potentials, coefficient, recovery, excitable, row_of):
    sections, bricks = mesh.shape["sec"], mesh.shape["brick"]
    _, X, Y, Z = potentials.shape
    f32 = jnp.float32
    scratch = [
        ((X + 4, Y + 2 * PAD, Z), f32), ((X + 4, Y + 2 * PAD, Z), f32),
        ((X + 2, Y, Z), f32), ((STEPS, X + 2, Y, Z), f32), ((X + 2, Y, Z), f32),
        ((STEPS, X, Y, Z), f32), ((STEPS, 2, X, Y, Z), f32),
        ((X, Y, Z), f32), ((X, Y, Z), f32), ((X, Y, Z), jnp.int32),
        ((2, 4 * (X + Y) + 32, Z), f32), ((2, 4 * (X + Y) + 32, Z), f32),
        ((2, 4 * (X + Y) + 32, Z), f32), ((2 * max(X, Y), Z), f32),
        ((2, X + 2 * PAD, Z), f32), ((2, X, Z), f32),
        ((2, X, Z), f32), ((2, X, Z), f32), ((2, X, Z), f32),
        ((2, 8, Z), f32), ((STEPS + 1, 2, 2, Y, Z), f32), ((8, Z), f32),
    ]
    sems = [(4,), (2,), (2,), (6,), (6,), (STEPS, 5, 3), (STEPS, 5), (STEPS,), (STEPS, 2),
            (2,), (STEPS + 1, 2)]
    hbm = pl.BlockSpec(memory_space=pltpu.HBM)
    cells = X * Y * Z
    fields = pl.pallas_call(
        functools.partial(kernel, sections, bricks),
        out_shape=jax.ShapeDtypeStruct(potentials.shape, f32),
        in_specs=[hbm] * 4 + [pl.BlockSpec(memory_space=pltpu.SMEM)],
        out_specs=hbm,
        scratch_shapes=[pltpu.VMEM(s, t) for s, t in scratch]
        + [pltpu.SMEM((len(PUSHES),), f32)]
        + [pltpu.SemaphoreType.DMA(s) for s in sems],
        compiler_params=pltpu.CompilerParams(
            collective_id=0, has_side_effects=True, vmem_limit_bytes=63 * 2**20 + 2**19),
        cost_estimate=pl.CostEstimate(
            flops=cells * STEPS * SWEEPS * 12, bytes_accessed=20 * cells, transcendentals=0),
    )(potentials, coefficient, recovery, excitable, row_of)
    torso = lax.axis_index("sec") < sections - 1
    return fields * jnp.where(torso, PUSHES[-1], 1.0).astype(f32)


def solution(mesh):
    in_specs = (
        P("sec", "brick", None, None),
        P("sec", "brick", None, None),
        P("brick", None, None),
        P("brick", None, None),
        P("brick"),
    )
    out_specs = P("sec", "brick", None, None)
    return jax.shard_map(functools.partial(body, mesh), mesh=mesh, in_specs=in_specs,
                         out_specs=out_specs, check_vma=False)
```

```python
import functools

import jax
import jax.numpy as jnp
from jax import lax
from jax.experimental import pallas as pl
from jax.experimental.pallas import tpu as pltpu
from jax.sharding import PartitionSpec as P

SUBSTEPS = 8
SWEEPS = 16
STEPS = 2
GROUPS = SWEEPS // 2

coupling_gain = 0.1
ionic_timestep = 0.05
ionic_gain = 8.0
recovery_rate = 0.1
recovery_decay = 0.5
spectrum_low = 0.04
spectrum_high = 12.32

center = 0.5 * (spectrum_high + spectrum_low)
spread = 0.5 * (spectrum_high - spectrum_low)
back = (0.5 * spread) ** 2


def push_weights():
    ratio = center / spread
    values = [1.0, ratio]
    while len(values) <= SWEEPS:
        values.append(2.0 * ratio * values[-1] - values[-2])
    grown = [(0.5 * spread) ** k * values[k] for k in range(SWEEPS + 1)]
    return grown[:SWEEPS] + [1.0] * (GROUPS - 1) + [1.0 / grown[SWEEPS]]


PUSHES = push_weights()
MESH = pl.DeviceIdType.MESH
PAD = 8
DIAGONAL = ((0, 0), (0, 1), (1, 0), (1, 1))


def largest_divisor(count, limit):
    return max(u for u in range(1, limit + 1) if count % u == 0)


def for_planes(first, count, limit, work):
    unroll = largest_divisor(count, limit)

    def chunk(i, carry):
        done = [work(first + i * unroll + j) for j in range(unroll)]
        for value, store in done:
            store(value)
        return carry

    lax.fori_loop(0, count // unroll, chunk, 0)


def in_line(first, count, work):
    for x in range(first, first + count):
        value, store = work(x)
        store(value)


def kernel(sections, bricks, pot, coef, rec, exc, row_of, out,
           A, B, EB, GB, BB, JA, JB, W, T, M, H, S, DUMP, ZB, R, R2, ER, SE, BR, PR, VH, row, push,
           lsem, sent, landing, isend, irecv, gsend, grecv, jsend, jrecv, vsend, vrecv):
    X, Y, Z = W.shape
    sec = lax.axis_index("sec")
    brick = lax.axis_index("brick")
    heart = sections - 1
    is_heart = sec == heart
    has_x = (brick > 0, brick < bricks - 1)
    to_x = (brick - 1, brick + 1)
    has_y = (jnp.logical_and(sec > 0, sec < heart), sec < heart - 1)
    to_y = (sec - 1, sec + 1)
    rows = pl.ds(PAD, Y)
    lane = lax.broadcasted_iota(jnp.int32, (Y, Z), 1)
    lane_x = lax.broadcasted_iota(jnp.int32, (X, Z), 1)

    def across(buf, at, first, count, pitch):
        return buf.reshape(buf.size // Z, Z), pl.ds(first * pitch + at, count, stride=pitch)

    def remote(src, dst, send, recv, s, b):
        return pltpu.make_async_remote_copy(
            src_ref=src, dst_ref=dst, send_sem=send, recv_sem=recv,
            device_id={"sec": s, "brick": b}, device_id_type=MESH)

    for n, value in enumerate(PUSHES):
        push[n] = jnp.float32(value)
    field = pltpu.make_async_copy(pot.at[0], A.at[pl.ds(2, X), rows], lsem.at[0])
    second = pltpu.make_async_copy(coef.at[0], T, lsem.at[1])
    field.start()
    second.start()

    barrier = pltpu.get_barrier_semaphore()

    @pl.when(jnp.logical_not(is_heart))
    def _():
        def clear(i, carry):
            for buf in (A, B):
                buf[i, 0:PAD, :] = jnp.zeros((PAD, Z), jnp.float32)
                buf[i, pl.ds(PAD + Y, PAD), :] = jnp.zeros((PAD, Z), jnp.float32)
            return carry

        lax.fori_loop(0, X + 4, clear, 0)
        for buf in (ZB, ER, R2):
            buf[...] = jnp.zeros(buf.shape, jnp.float32)
        EB[0] = jnp.zeros((Y, Z), jnp.float32)
        EB[X + 1] = jnp.zeros((Y, Z), jnp.float32)
        PR[...] = jnp.full(PR.shape, -1.0, jnp.float32)
        row[...] = jnp.full(row.shape, row_of[0].astype(jnp.float32), jnp.float32)

    for d in range(1, sections):
        pl.semaphore_signal(barrier, inc=1, device_id={"sec": lax.rem(sec + d, sections)},
                            device_id_type=MESH)
    total = sections - 1
    for i in range(2):
        @pl.when(has_x[i])
        def _():
            pl.semaphore_signal(barrier, inc=1, device_id={"sec": sec, "brick": to_x[i]},
                                device_id_type=MESH)
        total = total + has_x[i].astype(jnp.int32)
    for i, j in DIAGONAL:
        both = jnp.logical_and(has_x[i], has_y[j])

        @pl.when(both)
        def _():
            pl.semaphore_signal(barrier, inc=1, device_id={"sec": to_y[j], "brick": to_x[i]},
                                device_id_type=MESH)
        total = total + both.astype(jnp.int32)
    pl.semaphore_wait(barrier, total)
    field.wait()

    cuts = largest_divisor(X - 2, 3)
    size = (X - 2) // cuts
    parts = [(2 + n * size, size) for n in range(cuts)] + [(0, 2), (X, 2)]
    inner, outer = range(cuts), range(cuts, cuts + 2)

    def source_copy(step, n, lane_number, target):
        ref = GB.at[step, pl.ds(parts[n][0], parts[n][1])]
        return remote(ref, ref, gsend.at[step, n, lane_number], grecv.at[step, n], target, brick)

    def heart_program():
        recover = pltpu.make_async_copy(rec, W, lsem.at[2])
        excite = pltpu.make_async_copy(exc, M, lsem.at[3])
        recover.start()
        excite.start()

        def send_sides(round_number):
            for i in range(2):
                src = A.at[pl.ds(2, 2) if i == 0 else pl.ds(X, 2), rows]

                @pl.when(has_x[i])
                def _():
                    remote(src, VH.at[round_number, 1 - i], vsend.at[i],
                           vrecv.at[round_number, 1 - i], sec, to_x[i]).start()

        def sides(round_number):
            for i in range(2):
                src = A.at[pl.ds(2, 2) if i == 0 else pl.ds(X, 2), rows]
                at = 0 if i == 0 else X + 2

                @pl.when(has_x[i])
                def _():
                    got = remote(src, VH.at[round_number, i], vsend.at[i],
                                 vrecv.at[round_number, i], sec, to_x[i])
                    got.wait_recv()
                    got.wait_send()
                    for j in range(2):
                        A[at + j, rows, :] = VH[round_number, i, j]

                @pl.when(jnp.logical_not(has_x[i]))
                def _():
                    for j in range(2):
                        A[at + j, rows, :] = A[2 if i == 0 else X + 1, rows, :]

            edge_rows(0, 2)
            edge_rows(X + 2, X + 4)

        def edge_rows(low, high):
            def edge(i, carry):
                A[i, pl.ds(PAD - 1, 1), :] = A[i, pl.ds(PAD, 1), :]
                A[i, pl.ds(PAD + Y, 1), :] = A[i, pl.ds(PAD + Y - 1, 1), :]
                return carry

            lax.fori_loop(low, high, edge, 0)

        def laplace(x):
            c = A[x + 2, rows, :]
            total = A[x + 1, rows, :] + A[x + 3, rows, :]
            total = total + A[x + 2, pl.ds(PAD - 1, Y), :] + A[x + 2, pl.ds(PAD + 1, Y), :]
            total = total + jnp.where(lane == 0, c, pltpu.roll(c, 1, 1))
            total = total + jnp.where(lane == Z - 1, c, pltpu.roll(c, Z - 1, 1))
            return total - 6.0 * c

        def ionic(x):
            v = A[x + 2, rows, :]
            w = W[x]
            thresh = T[x]
            active = ionic_timestep * M[x].astype(jnp.float32)
            for _ in range(SUBSTEPS):
                drive = ionic_gain * v * (v - thresh) * (1.0 - v) - w
                relax = recovery_rate * (v - recovery_decay * w)
                v = v + active * drive
                w = w + active * relax

            def store(value):
                A[x + 2, rows, :] = value[0]
                W[x] = value[1]
            return (v, w), store

        def source(step, chunks):
            def work(x):
                def store(value):
                    GB[step, x + 1] = value
                return laplace(x), store
            for n in chunks:
                low, count = parts[n]
                for_planes(low - 1, count, 5, work)
                for far in (2, 1):
                    source_copy(step, n, far - 1, heart - far).start()

        def current(step):
            for n in range(2):
                remote(JB.at[step, n], JB.at[step, n], jsend.at[step], jrecv.at[step, n],
                       heart - 1 - n, brick).wait_recv()

        edge_rows(2, X + 2)
        send_sides(0)
        source(0, inner)
        sides(0)
        source(0, outer)
        second.wait()
        recover.wait()
        excite.wait()
        for step in range(STEPS):
            for_planes(0, X, 2, ionic)
            send_sides(step + 1)
            edge_rows(2, X + 2)
            sides(step + 1)
            if step + 1 < STEPS:
                source(step + 1, range(len(parts)))
                current(step)

                def advance(x):
                    def store(value):
                        A[x + 2, rows, :] = value
                    gain = GB[step + 1, x + 1] + (JB[step, 0, x] + JB[step, 1, x])
                    return A[x + 2, rows, :] + coupling_gain * gain, store
                for_planes(0, X, 4, advance)
            else:
                def before(x):
                    def store(value):
                        BB[x] = value
                    return A[x + 2, rows, :] + coupling_gain * laplace(x), store
                for_planes(0, X, 4, before)
                current(step)

                def final(x):
                    def store(value):
                        BB[x] = value
                    return BB[x] + coupling_gain * (JB[step, 0, x] + JB[step, 1, x]), store
                for_planes(0, X, 4, final)
                result = pltpu.make_async_copy(BB.at[pl.ds(0, X)], out.at[0], lsem.at[0])
                result.start()
                result.wait()
        for step in range(STEPS):
            for n in range(len(parts)):
                for far in (2, 1):
                    source_copy(step, n, far - 1, heart - far).wait_send()

    def torso_program():
        one = jnp.ones((), jnp.float32)
        zero = jnp.zeros((), jnp.float32)
        inside_x = [jnp.where(h, one, zero) for h in has_x]
        inside_y = [jnp.where(h, one, zero) for h in has_y]
        section = sec.astype(jnp.float32)
        own = jnp.where(row[...] == section, 1.0, 0.0)
        own_y = (jnp.where(row[...] == section - 1.0, 1.0, 0.0),
                 jnp.where(row[...] == section + 1.0, 1.0, 0.0))

        at_x = [(2 * Y * i, 2 * Y) for i in range(2)]
        at_y = [(4 * Y + 2 * X * j, 2 * X) for j in range(2)]
        at_c = [(4 * (X + Y) + 8 * n, 8) for n in range(4)]

        def message(slot, there, here, s, b):
            there_at, here_at = pl.ds(*there), pl.ds(*here)
            return remote(S.at[slot, here_at], H.at[slot, there_at], sent.at[slot],
                          landing.at[slot], s, b)

        def nothing(slot, here):
            zeros = ZB.at[pl.ds(0, here[1])]
            pltpu.make_async_copy(zeros, H.at[slot, pl.ds(*here)], landing.at[slot]).start()
            pltpu.make_async_copy(zeros, DUMP.at[slot, pl.ds(*here)], sent.at[slot]).start()

        def send_beside(slot):
            for n, (i, j) in enumerate(DIAGONAL):
                both = jnp.logical_and(has_x[i], has_y[j])

                @pl.when(both)
                def _():
                    message(slot, at_c[3 - n], at_c[n], to_y[j], to_x[i]).start()

                @pl.when(jnp.logical_not(both))
                def _():
                    nothing(slot, at_c[n])

            def send_planes(i):
                @pl.when(has_x[i])
                def _():
                    message(slot, at_x[1 - i], at_x[i], sec, to_x[i]).start()

                @pl.when(jnp.logical_not(has_x[i]))
                def _():
                    nothing(slot, at_x[i])

            even = lax.rem(brick, 2) == 0

            @pl.when(even)
            def _():
                send_planes(0)
                send_planes(1)

            @pl.when(jnp.logical_not(even))
            def _():
                send_planes(1)
                send_planes(0)

        def send_across(slot):
            for j in range(2):
                @pl.when(has_y[j])
                def _():
                    message(slot, at_y[1 - j], at_y[j], to_y[j], brick).start()

                @pl.when(jnp.logical_not(has_y[j]))
                def _():
                    nothing(slot, at_y[j])

        def wait_landed(slot):
            pltpu.make_async_copy(S.at[slot], H.at[slot], landing.at[slot]).wait()

        def wait_sent(slot):
            pltpu.make_async_copy(S.at[slot], DUMP.at[slot], sent.at[slot]).wait()

        def pack_rows(slot):
            for j in range(2):
                for n in range(2):
                    at = PAD + n if j == 0 else PAD + Y - 1 - n
                    flat, where = across(A, at, 2, X, Y + 2 * PAD)
                    S[slot, pl.ds(at_y[j][0] + n * X, X), :] = flat[where, :]

        def pack_planes(slot):
            for i in range(2):
                for n in range(2):
                    value = A[(2 if i == 0 else X) + n, rows, :]
                    S[slot, pl.ds(at_x[i][0] + n * Y, Y), :] = value
            for n, (i, j) in enumerate(DIAGONAL):
                corner = A[2 if i == 0 else X + 1, pl.ds(PAD if j == 0 else PAD + Y - 1, 1), :]
                S[slot, pl.ds(at_c[n][0], 1), :] = corner

        def stencil(src, x, low, high):
            here = pl.ds(PAD + low, high - low)
            at_lane = lane[0:high - low]
            c = src[x + 2, here, :]
            total = src[x + 1, here, :] + src[x + 3, here, :]
            total = total + (src[x + 2, pl.ds(PAD + low - 1, high - low), :]
                             + src[x + 2, pl.ds(PAD + low + 1, high - low), :])
            total = total + (jnp.where(at_lane == 0, 0.0, pltpu.roll(c, 1, 1))
                             + jnp.where(at_lane == Z - 1, 0.0, pltpu.roll(c, Z - 1, 1)))
            return total + EB[x + 1, pl.ds(low, high - low), :] * c

        def plane(src, dst, first, weight, scale=None, low=0, high=Y):
            here = pl.ds(PAD + low, high - low)

            def work(x):
                value = stencil(src, x, low, high)
                if first:
                    value = 0.5 * value
                else:
                    value = ((value + weight * BB[x + 1, pl.ds(low, high - low), :])
                             - back * dst[x + 2, here, :])
                if scale is not None:
                    value = scale * value

                def store(value):
                    dst[x + 2, here, :] = value
                return value, store
            return work

        def mend(dst, low, high, halo, offset, scale):
            for j, at in ((0, PAD), (1, PAD + Y - 1)):
                flat, where = across(dst, at, low + 2, high - low, Y + 2 * PAD)
                flat[where, :] = flat[where, :] + scale * halo[j, pl.ds(low + offset, high - low), :]

        def fringe(slot, first, weight):
            for j in range(2):
                c = R[j, pl.ds(PAD, X), :]
                total = R[j, pl.ds(PAD - 1, X), :] + R[j, pl.ds(PAD + 1, X), :]
                total = total + S[slot, pl.ds(at_y[j][0], X), :] + H[slot, pl.ds(at_y[j][0] + X, X), :]
                total = total + jnp.where(lane_x == 0, 0.0, pltpu.roll(c, 1, 1))
                total = total + jnp.where(lane_x == Z - 1, 0.0, pltpu.roll(c, Z - 1, 1))
                total = total + ER[j] * c
                if first:
                    R2[j] = (0.5 * inside_y[j]) * total
                else:
                    R2[j] = inside_y[j] * (total + weight * BR[j] - back * R2[j])

        def landed(slot):
            for j in range(2):
                A[j, rows, :] = H[slot, pl.ds(at_x[0][0] + j * Y, Y), :]
                A[X + 2 + j, rows, :] = H[slot, pl.ds(at_x[1][0] + j * Y, Y), :]
                R[j, pl.ds(PAD, X), :] = H[slot, pl.ds(at_y[j][0], X), :]
            for n, (i, j) in enumerate(DIAGONAL):
                R[j, pl.ds(PAD - 1 if i == 0 else PAD + X, 1), :] = H[slot, pl.ds(at_c[n][0], 1), :]

        def first_sweep(slot, number, first, weight, prepare=lambda: None):
            in_line(1, X - 2, plane(A, B, first, weight))

            @pl.when(number > 0)
            def _():
                wait_sent(1 - slot)
            wait_landed(slot)
            prepare()
            landed(slot)
            done = [plane(A, B, first, weight, scale)(x) for x, scale in
                    ((-1, inside_x[0]), (0, None), (X - 1, None), (X, inside_x[1]))]
            for value, store in done:
                store(value)
            fringe(slot, first, weight)
            mend(B, -1, X + 1, R, PAD, 0.5 if first else 1.0)

        def relay_source(step, n):
            return source_copy(step, n, 2, heart - 3)

        def wait_source(step, n):
            source_copy(step, n, 2, heart).wait_recv()

        inner_layer = sec == heart - 3
        pieces = largest_divisor(X, 4)
        piece = X // pieces

        def current_copy(step, low, count):
            target = jnp.where(inner_layer, heart - 2, heart)
            place = jnp.where(sec == heart - 2, 1, 0)
            span = pl.ds(low, count)
            return remote(JA.at[step, span], JB.at[step, place, span], jsend.at[step],
                          jrecv.at[step, place], target, brick)

        def init_copies():
            found = []
            for i in range(2):
                found.append((has_x[i], EB.at[1 if i == 0 else X], EB.at[X + 1 if i == 0 else 0],
                              EB.at[0 if i == 0 else X + 1], 1 - i, i, sec, to_x[i]))
                found.append((has_x[i], row, PR.at[1 - i], PR.at[i], 5 - i, 4 + i, sec, to_x[i]))
            for j in range(2):
                found.append((has_y[j], SE.at[j], ER.at[1 - j], ER.at[j], 3 - j, 2 + j,
                              to_y[j], brick))
            return found

        def set_up():
            second.wait()

            def absorb(x):
                def store(value):
                    EB[x + 1] = value
                return (center - 6.0) - T[x], store
            for_planes(0, X, 4, absorb)

            for j, at in ((0, 0), (1, Y - 1)):
                flat, where = across(EB, at, 1, X, Y)
                SE[j] = flat[where, :]
            for there, src, dst, land, far, near, s, b in init_copies():
                @pl.when(there)
                def _():
                    remote(src, dst, isend.at[near], irecv.at[far], s, b).start()

        def second_sweep(slot, weight, scale, more):
            after = 1 - slot
            for j, at in ((0, PAD - 1), (1, PAD + Y)):
                flat, where = across(B, at, 2, X, Y + 2 * PAD)
                flat[where, :] = R2[j]
            work = plane(B, A, False, weight, scale)
            done = [work(x) for x in (0, 1, X - 2, X - 1)]
            for value, store in done:
                store(value)

            @pl.when(more)
            def _():
                pack_planes(after)
                send_beside(after)
            band = 8 if Y > 16 else Y // 2
            for low in (0, Y - band):
                in_line(2, X - 4, plane(B, A, False, weight, scale, low, low + band))

            @pl.when(more)
            def _():
                pack_rows(after)
                send_across(after)
            if Y > 2 * band:
                in_line(2, X - 4, plane(B, A, False, weight, scale, band, Y - band))

        def step_body(step, carry):
            @pl.when(step == 0)
            def _():
                set_up()

            def prepare():
                @pl.when(step == 0)
                def _():
                    for there, src, dst, land, far, near, s, b in init_copies():
                        @pl.when(there)
                        def _():
                            got = remote(src, land, isend.at[near], irecv.at[near], s, b)
                            got.wait_recv()
                            got.wait_send()

            first_sweep(0, step, True, None, prepare)

            def current(x):
                def store(value):
                    JA[step, x] = value
                own_v = jnp.broadcast_to(own[0:1], (Y, Z))
                value = 2.0 * B[x + 2, rows, :] - (EB[x + 1] + 6.0) * A[x + 2, rows, :]
                return own_v * value, store
            for_planes(0, X, 4, current)

            @pl.when(inner_layer)
            def _():
                current_copy(step, 0, X).start()

            flags = [jnp.where(PR[i] == section, 1.0, 0.0) for i in range(2)]

            def place(flag):
                def work(x):
                    value = jnp.broadcast_to(flag[0:1], (Y, Z)) * GB[step, x + 1]

                    def store(value):
                        BB[x + 1] = value
                        B[x + 2, rows, :] = B[x + 2, rows, :] + 0.5 * value
                    return value, store
                return work
            for n, (low, count) in enumerate(parts):
                @pl.when(jnp.logical_or(sec != heart - 2, step == 0))
                def _():
                    wait_source(step, n)

                @pl.when(jnp.logical_and(sec == heart - 2, step == 0))
                def _():
                    relay_source(step, n).start()
                if n in inner:
                    for_planes(low - 1, count, 5, place(own))
                else:
                    for x in (low - 1, low):
                        value, store = place({-1: flags[0], X: flags[1]}.get(x, own))(x)
                        store(value)

            for j, at in ((0, Y - 1), (1, 0)):
                flat, where = across(GB, at, step * (X + 2) + 1, X, Y)
                BR[j] = jnp.broadcast_to(own_y[j][0:1], (X, Z)) * flat[where, :]
                R2[j] = R2[j] + 0.5 * BR[j]
            second_sweep(0, push[1], None, True)

            def group(g, carry):
                slot = lax.rem(g, 2)

                @pl.when(jnp.logical_and(g == 1, sec == heart - 2))
                def _():
                    remote(JB.at[step, 0], JB.at[step, 0], jsend.at[step], jrecv.at[step, 0],
                           heart, brick).wait_recv()

                    def add(x):
                        def store(value):
                            JA[step, x] = value
                        return JA[step, x] + JB[step, 0, x], store
                    for_planes(0, X, 4, add)

                @pl.when(jnp.logical_and(g <= pieces, jnp.logical_not(inner_layer)))
                def _():
                    current_copy(step, (g - 1) * piece, piece).start()

                @pl.when(jnp.logical_and(jnp.logical_and(g == GROUPS - 3, step + 1 < STEPS),
                                         sec == heart - 2))
                def _():
                    for n in range(len(parts)):
                        wait_source(step + 1, n)
                        relay_source(step + 1, n).start()

                first = push[2 * g]
                first_sweep(slot, g, False, first)
                going_on = step < STEPS - 1
                second_sweep(slot, push[2 * g + 1], jnp.where(going_on, push[SWEEPS + g], 1.0),
                             jnp.logical_or(g < GROUPS - 1, going_on))
                return carry

            lax.fori_loop(1, GROUPS, group, 0)
            return carry

        pack_planes(0)
        send_beside(0)
        pack_rows(0)
        send_across(0)
        lax.fori_loop(0, STEPS, step_body, 0)

        result = pltpu.make_async_copy(A.at[pl.ds(2, X), rows], out.at[0], lsem.at[0])
        result.start()
        wait_sent((GROUPS - 1) % 2)
        for step in range(STEPS):
            current_copy(step, 0, X).wait_send()

            @pl.when(sec == heart - 2)
            def _():
                for n in range(len(parts)):
                    relay_source(step, n).wait_send()

        result.wait()

    pl.when(is_heart)(heart_program)
    pl.when(jnp.logical_not(is_heart))(torso_program)


def body(mesh, potentials, coefficient, recovery, excitable, row_of):
    sections, bricks = mesh.shape["sec"], mesh.shape["brick"]
    _, X, Y, Z = potentials.shape
    f32 = jnp.float32
    scratch = [
        ((X + 4, Y + 2 * PAD, Z), f32), ((X + 4, Y + 2 * PAD, Z), f32),
        ((X + 2, Y, Z), f32), ((STEPS, X + 2, Y, Z), f32), ((X + 2, Y, Z), f32),
        ((STEPS, X, Y, Z), f32), ((STEPS, 2, X, Y, Z), f32),
        ((X, Y, Z), f32), ((X, Y, Z), f32), ((X, Y, Z), jnp.int32),
        ((2, 4 * (X + Y) + 32, Z), f32), ((2, 4 * (X + Y) + 32, Z), f32),
        ((2, 4 * (X + Y) + 32, Z), f32), ((2 * max(X, Y), Z), f32),
        ((2, X + 2 * PAD, Z), f32), ((2, X, Z), f32),
        ((2, X, Z), f32), ((2, X, Z), f32), ((2, X, Z), f32),
        ((2, 8, Z), f32), ((STEPS + 1, 2, 2, Y, Z), f32), ((8, Z), f32),
    ]
    sems = [(4,), (2,), (2,), (6,), (6,), (STEPS, 5, 3), (STEPS, 5), (STEPS,), (STEPS, 2),
            (2,), (STEPS + 1, 2)]
    hbm = pl.BlockSpec(memory_space=pltpu.HBM)
    cells = X * Y * Z
    fields = pl.pallas_call(
        functools.partial(kernel, sections, bricks),
        out_shape=jax.ShapeDtypeStruct(potentials.shape, f32),
        in_specs=[hbm] * 4 + [pl.BlockSpec(memory_space=pltpu.SMEM)],
        out_specs=hbm,
        scratch_shapes=[pltpu.VMEM(s, t) for s, t in scratch]
        + [pltpu.SMEM((len(PUSHES),), f32)]
        + [pltpu.SemaphoreType.DMA(s) for s in sems],
        compiler_params=pltpu.CompilerParams(
            collective_id=0, has_side_effects=True, vmem_limit_bytes=63 * 2**20 + 2**19),
        cost_estimate=pl.CostEstimate(
            flops=cells * STEPS * SWEEPS * 12, bytes_accessed=20 * cells, transcendentals=0),
    )(potentials, coefficient, recovery, excitable, row_of)
    torso = lax.axis_index("sec") < sections - 1
    return fields * jnp.where(torso, PUSHES[-1], 1.0).astype(f32)


def solution(mesh):
    in_specs = (
        P("sec", "brick", None, None),
        P("sec", "brick", None, None),
        P("brick", None, None),
        P("brick", None, None),
        P("brick"),
    )
    out_specs = P("sec", "brick", None, None)
    return jax.shard_map(functools.partial(body, mesh), mesh=mesh, in_specs=in_specs,
                         out_specs=out_specs, check_vma=False)
```

```python
import functools

import jax
import jax.numpy as jnp
from jax import lax
from jax.experimental import pallas as pl
from jax.experimental.pallas import tpu as pltpu
from jax.sharding import PartitionSpec as P

SUBSTEPS = 8
SWEEPS = 16
STEPS = 2
GROUPS = SWEEPS // 2

coupling_gain = 0.1
ionic_timestep = 0.05
ionic_gain = 8.0
recovery_rate = 0.1
recovery_decay = 0.5
spectrum_low = 0.04
spectrum_high = 12.32

center = 0.5 * (spectrum_high + spectrum_low)
spread = 0.5 * (spectrum_high - spectrum_low)
back = (0.5 * spread) ** 2


def push_weights():
    ratio = center / spread
    values = [1.0, ratio]
    while len(values) <= SWEEPS:
        values.append(2.0 * ratio * values[-1] - values[-2])
    grown = [(0.5 * spread) ** k * values[k] for k in range(SWEEPS + 1)]
    return grown[:SWEEPS] + [1.0] * (GROUPS - 1) + [1.0 / grown[SWEEPS]]


PUSHES = push_weights()
MESH = pl.DeviceIdType.MESH
PAD = 8
DIAGONAL = ((0, 0), (0, 1), (1, 0), (1, 1))


def largest_divisor(count, limit):
    return max(u for u in range(1, limit + 1) if count % u == 0)


def for_planes(first, count, limit, work):
    unroll = largest_divisor(count, limit)

    def chunk(i, carry):
        done = [work(first + i * unroll + j) for j in range(unroll)]
        for value, store in done:
            store(value)
        return carry

    lax.fori_loop(0, count // unroll, chunk, 0)


def in_line(first, count, work):
    for x in range(first, first + count):
        value, store = work(x)
        store(value)


def kernel(sections, bricks, pot, coef, rec, exc, row_of, out,
           A, B, EB, GB, BB, JA, JB, W, T, M, H, S, DUMP, ZB, R, R2, ER, SE, BR, PR, VH, row, push,
           lsem, sent, landing, isend, irecv, gsend, grecv, jsend, jrecv, vsend, vrecv):
    X, Y, Z = W.shape
    sec = lax.axis_index("sec")
    brick = lax.axis_index("brick")
    heart = sections - 1
    is_heart = sec == heart
    has_x = (brick > 0, brick < bricks - 1)
    to_x = (brick - 1, brick + 1)
    has_y = (jnp.logical_and(sec > 0, sec < heart), sec < heart - 1)
    to_y = (sec - 1, sec + 1)
    rows = pl.ds(PAD, Y)
    lane = lax.broadcasted_iota(jnp.int32, (Y, Z), 1)
    lane_x = lax.broadcasted_iota(jnp.int32, (X, Z), 1)

    def across(buf, at, first, count, pitch):
        return buf.reshape(buf.size // Z, Z), pl.ds(first * pitch + at, count, stride=pitch)

    def remote(src, dst, send, recv, s, b):
        return pltpu.make_async_remote_copy(
            src_ref=src, dst_ref=dst, send_sem=send, recv_sem=recv,
            device_id={"sec": s, "brick": b}, device_id_type=MESH)

    for n, value in enumerate(PUSHES):
        push[n] = jnp.float32(value)
    field = pltpu.make_async_copy(pot.at[0], A.at[pl.ds(2, X), rows], lsem.at[0])
    second = pltpu.make_async_copy(coef.at[0], T, lsem.at[1])
    field.start()
    second.start()

    barrier = pltpu.get_barrier_semaphore()

    @pl.when(jnp.logical_not(is_heart))
    def _():
        def clear(i, carry):
            for buf in (A, B):
                buf[i, 0:PAD, :] = jnp.zeros((PAD, Z), jnp.float32)
                buf[i, pl.ds(PAD + Y, PAD), :] = jnp.zeros((PAD, Z), jnp.float32)
            return carry

        lax.fori_loop(0, X + 4, clear, 0)
        for buf in (ZB, ER, R2):
            buf[...] = jnp.zeros(buf.shape, jnp.float32)
        EB[0] = jnp.zeros((Y, Z), jnp.float32)
        EB[X + 1] = jnp.zeros((Y, Z), jnp.float32)
        PR[...] = jnp.full(PR.shape, -1.0, jnp.float32)
        row[...] = jnp.full(row.shape, row_of[0].astype(jnp.float32), jnp.float32)

    for d in range(1, sections):
        pl.semaphore_signal(barrier, inc=1, device_id={"sec": lax.rem(sec + d, sections)},
                            device_id_type=MESH)
    total = sections - 1
    for i in range(2):
        @pl.when(has_x[i])
        def _():
            pl.semaphore_signal(barrier, inc=1, device_id={"sec": sec, "brick": to_x[i]},
                                device_id_type=MESH)
        total = total + has_x[i].astype(jnp.int32)
    for i, j in DIAGONAL:
        both = jnp.logical_and(has_x[i], has_y[j])

        @pl.when(both)
        def _():
            pl.semaphore_signal(barrier, inc=1, device_id={"sec": to_y[j], "brick": to_x[i]},
                                device_id_type=MESH)
        total = total + both.astype(jnp.int32)

    cuts = largest_divisor(X - 2, 3)
    size = (X - 2) // cuts
    parts = [(2 + n * size, size) for n in range(cuts)] + [(0, 2), (X, 2)]
    inner, outer = range(cuts), range(cuts, cuts + 2)

    def source_copy(step, n, lane_number, target):
        ref = GB.at[step, pl.ds(parts[n][0], parts[n][1])]
        return remote(ref, ref, gsend.at[step, n, lane_number], grecv.at[step, n], target, brick)

    def heart_program(early):
        recover = pltpu.make_async_copy(rec, W, lsem.at[2])
        excite = pltpu.make_async_copy(exc, M, lsem.at[3])

        def send_sides(round_number):
            for i in range(2):
                src = A.at[pl.ds(2, 2) if i == 0 else pl.ds(X, 2), rows]

                @pl.when(has_x[i])
                def _():
                    remote(src, VH.at[round_number, 1 - i], vsend.at[i],
                           vrecv.at[round_number, 1 - i], sec, to_x[i]).start()

        def sides(round_number):
            for i in range(2):
                src = A.at[pl.ds(2, 2) if i == 0 else pl.ds(X, 2), rows]
                at = 0 if i == 0 else X + 2

                @pl.when(has_x[i])
                def _():
                    got = remote(src, VH.at[round_number, i], vsend.at[i],
                                 vrecv.at[round_number, i], sec, to_x[i])
                    got.wait_recv()
                    got.wait_send()
                    for j in range(2):
                        A[at + j, rows, :] = VH[round_number, i, j]

                @pl.when(jnp.logical_not(has_x[i]))
                def _():
                    for j in range(2):
                        A[at + j, rows, :] = A[2 if i == 0 else X + 1, rows, :]

            edge_rows(0, 2)
            edge_rows(X + 2, X + 4)

        def edge_rows(low, high):
            def edge(i, carry):
                A[i, pl.ds(PAD - 1, 1), :] = A[i, pl.ds(PAD, 1), :]
                A[i, pl.ds(PAD + Y, 1), :] = A[i, pl.ds(PAD + Y - 1, 1), :]
                return carry

            lax.fori_loop(low, high, edge, 0)

        def laplace(x):
            c = A[x + 2, rows, :]
            total = A[x + 1, rows, :] + A[x + 3, rows, :]
            total = total + A[x + 2, pl.ds(PAD - 1, Y), :] + A[x + 2, pl.ds(PAD + 1, Y), :]
            total = total + jnp.where(lane == 0, c, pltpu.roll(c, 1, 1))
            total = total + jnp.where(lane == Z - 1, c, pltpu.roll(c, Z - 1, 1))
            return total - 6.0 * c

        def ionic(x):
            v = A[x + 2, rows, :]
            w = W[x]
            thresh = T[x]
            active = ionic_timestep * M[x].astype(jnp.float32)
            for _ in range(SUBSTEPS):
                drive = ionic_gain * v * (v - thresh) * (1.0 - v) - w
                relax = recovery_rate * (v - recovery_decay * w)
                v = v + active * drive
                w = w + active * relax

            def store(value):
                A[x + 2, rows, :] = value[0]
                W[x] = value[1]
            return (v, w), store

        def sum_up(step, chunks):
            def work(x):
                def store(value):
                    GB[step, x + 1] = value
                return laplace(x), store
            for n in chunks:
                low, count = parts[n]
                for_planes(low - 1, count, 5, work)

        def hand_out(step, chunks):
            for n in chunks:
                for far in (2, 1):
                    source_copy(step, n, far - 1, heart - far).start()

        def current(step):
            for n in range(2):
                remote(JB.at[step, n], JB.at[step, n], jsend.at[step], jrecv.at[step, n],
                       heart - 1 - n, brick).wait_recv()

        if early:
            recover.start()
            excite.start()
            edge_rows(2, X + 2)
            sum_up(0, inner)
            return
        send_sides(0)
        hand_out(0, inner)
        sides(0)
        sum_up(0, outer)
        hand_out(0, outer)
        second.wait()
        recover.wait()
        excite.wait()
        for step in range(STEPS):
            for_planes(0, X, 2, ionic)
            send_sides(step + 1)
            edge_rows(2, X + 2)
            sides(step + 1)
            if step + 1 < STEPS:
                sum_up(step + 1, range(len(parts)))
                hand_out(step + 1, range(len(parts)))
                current(step)

                def advance(x):
                    def store(value):
                        A[x + 2, rows, :] = value
                    gain = GB[step + 1, x + 1] + (JB[step, 0, x] + JB[step, 1, x])
                    return A[x + 2, rows, :] + coupling_gain * gain, store
                for_planes(0, X, 4, advance)
            else:
                def before(x):
                    def store(value):
                        BB[x] = value
                    return A[x + 2, rows, :] + coupling_gain * laplace(x), store
                for_planes(0, X, 4, before)
                current(step)

                def final(x):
                    def store(value):
                        BB[x] = value
                    return BB[x] + coupling_gain * (JB[step, 0, x] + JB[step, 1, x]), store
                for_planes(0, X, 4, final)
                result = pltpu.make_async_copy(BB.at[pl.ds(0, X)], out.at[0], lsem.at[0])
                result.start()
                result.wait()
        for step in range(STEPS):
            for n in range(len(parts)):
                for far in (2, 1):
                    source_copy(step, n, far - 1, heart - far).wait_send()

    def torso_program(early):
        one = jnp.ones((), jnp.float32)
        zero = jnp.zeros((), jnp.float32)
        inside_x = [jnp.where(h, one, zero) for h in has_x]
        inside_y = [jnp.where(h, one, zero) for h in has_y]
        section = sec.astype(jnp.float32)
        own = jnp.where(row[...] == section, 1.0, 0.0)
        own_y = (jnp.where(row[...] == section - 1.0, 1.0, 0.0),
                 jnp.where(row[...] == section + 1.0, 1.0, 0.0))

        at_x = [(2 * Y * i, 2 * Y) for i in range(2)]
        at_y = [(4 * Y + 2 * X * j, 2 * X) for j in range(2)]
        at_c = [(4 * (X + Y) + 8 * n, 8) for n in range(4)]

        def message(slot, there, here, s, b):
            there_at, here_at = pl.ds(*there), pl.ds(*here)
            return remote(S.at[slot, here_at], H.at[slot, there_at], sent.at[slot],
                          landing.at[slot], s, b)

        def nothing(slot, here):
            zeros = ZB.at[pl.ds(0, here[1])]
            pltpu.make_async_copy(zeros, H.at[slot, pl.ds(*here)], landing.at[slot]).start()
            pltpu.make_async_copy(zeros, DUMP.at[slot, pl.ds(*here)], sent.at[slot]).start()

        def send_corners(slot):
            for n, (i, j) in enumerate(DIAGONAL):
                both = jnp.logical_and(has_x[i], has_y[j])

                @pl.when(both)
                def _():
                    message(slot, at_c[3 - n], at_c[n], to_y[j], to_x[i]).start()

                @pl.when(jnp.logical_not(both))
                def _():
                    nothing(slot, at_c[n])

        def send_planes(slot):
            for i in range(2):
                @pl.when(has_x[i])
                def _():
                    message(slot, at_x[1 - i], at_x[i], sec, to_x[i]).start()

                @pl.when(jnp.logical_not(has_x[i]))
                def _():
                    nothing(slot, at_x[i])

        def send_across(slot):
            for j in range(2):
                @pl.when(has_y[j])
                def _():
                    message(slot, at_y[1 - j], at_y[j], to_y[j], brick).start()

                @pl.when(jnp.logical_not(has_y[j]))
                def _():
                    nothing(slot, at_y[j])

        def wait_landed(slot):
            pltpu.make_async_copy(S.at[slot], H.at[slot], landing.at[slot]).wait()

        def wait_sent(slot):
            pltpu.make_async_copy(S.at[slot], DUMP.at[slot], sent.at[slot]).wait()

        def pack_rows(slot):
            for j in range(2):
                for n in range(2):
                    at = PAD + n if j == 0 else PAD + Y - 1 - n
                    flat, where = across(A, at, 2, X, Y + 2 * PAD)
                    S[slot, pl.ds(at_y[j][0] + n * X, X), :] = flat[where, :]

        def pack_planes(slot):
            for i in range(2):
                for n in range(2):
                    value = A[(2 if i == 0 else X) + n, rows, :]
                    S[slot, pl.ds(at_x[i][0] + n * Y, Y), :] = value
        def pack_corners(slot):
            for n, (i, j) in enumerate(DIAGONAL):
                corner = A[2 if i == 0 else X + 1, pl.ds(PAD if j == 0 else PAD + Y - 1, 1), :]
                S[slot, pl.ds(at_c[n][0], 1), :] = corner

        def stencil(src, x, low, high):
            here = pl.ds(PAD + low, high - low)
            at_lane = lane[0:high - low]
            c = src[x + 2, here, :]
            total = src[x + 1, here, :] + src[x + 3, here, :]
            total = total + (src[x + 2, pl.ds(PAD + low - 1, high - low), :]
                             + src[x + 2, pl.ds(PAD + low + 1, high - low), :])
            total = total + (jnp.where(at_lane == 0, 0.0, pltpu.roll(c, 1, 1))
                             + jnp.where(at_lane == Z - 1, 0.0, pltpu.roll(c, Z - 1, 1)))
            return total + EB[x + 1, pl.ds(low, high - low), :] * c

        def plane(src, dst, first, weight, scale=None, low=0, high=Y):
            here = pl.ds(PAD + low, high - low)

            def work(x):
                value = stencil(src, x, low, high)
                if first:
                    value = 0.5 * value
                else:
                    value = ((value + weight * BB[x + 1, pl.ds(low, high - low), :])
                             - back * dst[x + 2, here, :])
                if scale is not None:
                    value = scale * value

                def store(value):
                    dst[x + 2, here, :] = value
                return value, store
            return work

        def mend(dst, low, high, halo, offset, scale):
            for j, at in ((0, PAD), (1, PAD + Y - 1)):
                flat, where = across(dst, at, low + 2, high - low, Y + 2 * PAD)
                flat[where, :] = flat[where, :] + scale * halo[j, pl.ds(low + offset, high - low), :]

        def fringe(slot, first, weight):
            for j in range(2):
                c = R[j, pl.ds(PAD, X), :]
                total = R[j, pl.ds(PAD - 1, X), :] + R[j, pl.ds(PAD + 1, X), :]
                total = total + S[slot, pl.ds(at_y[j][0], X), :] + H[slot, pl.ds(at_y[j][0] + X, X), :]
                total = total + jnp.where(lane_x == 0, 0.0, pltpu.roll(c, 1, 1))
                total = total + jnp.where(lane_x == Z - 1, 0.0, pltpu.roll(c, Z - 1, 1))
                total = total + ER[j] * c
                if first:
                    R2[j] = (0.5 * inside_y[j]) * total
                else:
                    R2[j] = inside_y[j] * (total + weight * BR[j] - back * R2[j])

        def landed(slot):
            for j in range(2):
                A[j, rows, :] = H[slot, pl.ds(at_x[0][0] + j * Y, Y), :]
                A[X + 2 + j, rows, :] = H[slot, pl.ds(at_x[1][0] + j * Y, Y), :]
                R[j, pl.ds(PAD, X), :] = H[slot, pl.ds(at_y[j][0], X), :]
            for n, (i, j) in enumerate(DIAGONAL):
                R[j, pl.ds(PAD - 1 if i == 0 else PAD + X, 1), :] = H[slot, pl.ds(at_c[n][0], 1), :]

        def first_sweep(slot, number, first, weight, prepare=lambda: None):
            in_line(1, X - 2, plane(A, B, first, weight))

            @pl.when(number > 0)
            def _():
                wait_sent(1 - slot)
            wait_landed(slot)
            prepare()
            landed(slot)
            done = [plane(A, B, first, weight, scale)(x) for x, scale in
                    ((-1, inside_x[0]), (0, None), (X - 1, None), (X, inside_x[1]))]
            for value, store in done:
                store(value)
            fringe(slot, first, weight)
            mend(B, -1, X + 1, R, PAD, 0.5 if first else 1.0)

        def relay_source(step, n):
            return source_copy(step, n, 2, heart - 3)

        def wait_source(step, n):
            source_copy(step, n, 2, heart).wait_recv()

        inner_layer = sec == heart - 3
        pieces = largest_divisor(X, 4)
        piece = X // pieces

        def current_copy(step, low, count):
            target = jnp.where(inner_layer, heart - 2, heart)
            place = jnp.where(sec == heart - 2, 1, 0)
            span = pl.ds(low, count)
            return remote(JA.at[step, span], JB.at[step, place, span], jsend.at[step],
                          jrecv.at[step, place], target, brick)

        def init_copies():
            found = []
            for i in range(2):
                found.append((has_x[i], EB.at[1 if i == 0 else X], EB.at[X + 1 if i == 0 else 0],
                              EB.at[0 if i == 0 else X + 1], 1 - i, i, sec, to_x[i]))
                found.append((has_x[i], row, PR.at[1 - i], PR.at[i], 5 - i, 4 + i, sec, to_x[i]))
            for j in range(2):
                found.append((has_y[j], SE.at[j], ER.at[1 - j], ER.at[j], 3 - j, 2 + j,
                              to_y[j], brick))
            return found

        def set_up():
            second.wait()

            def absorb(x):
                def store(value):
                    EB[x + 1] = value
                return (center - 6.0) - T[x], store
            for_planes(0, X, 4, absorb)

            for j, at in ((0, 0), (1, Y - 1)):
                flat, where = across(EB, at, 1, X, Y)
                SE[j] = flat[where, :]
            pack_rows(0)
            pack_corners(0)
            pack_planes(0)

        if early:
            set_up()
            return

        def second_sweep(slot, weight, scale, more):
            after = 1 - slot
            for j, at in ((0, PAD - 1), (1, PAD + Y)):
                flat, where = across(B, at, 2, X, Y + 2 * PAD)
                flat[where, :] = R2[j]
            band = 8 if Y > 16 else Y // 2
            for low in (0, Y - band):
                in_line(0, X, plane(B, A, False, weight, scale, low, low + band))

            @pl.when(more)
            def _():
                pack_rows(after)
                send_across(after)
                pack_corners(after)
                send_corners(after)
            work = plane(B, A, False, weight, scale, band, Y - band)
            if Y > 2 * band:
                for low in (0, X - 2):
                    in_line(low, 2, work)

            @pl.when(more)
            def _():
                pack_planes(after)
                send_planes(after)
            if Y > 2 * band:
                in_line(2, X - 4, work)

        def step_body(step, carry):
            def prepare():
                @pl.when(step == 0)
                def _():
                    for there, src, dst, land, far, near, s, b in init_copies():
                        @pl.when(there)
                        def _():
                            got = remote(src, land, isend.at[near], irecv.at[near], s, b)
                            got.wait_recv()
                            got.wait_send()

            first_sweep(0, step, True, None, prepare)

            def current(x):
                def store(value):
                    JA[step, x] = value
                own_v = jnp.broadcast_to(own[0:1], (Y, Z))
                value = 2.0 * B[x + 2, rows, :] - (EB[x + 1] + 6.0) * A[x + 2, rows, :]
                return own_v * value, store
            for_planes(0, X, 4, current)

            @pl.when(inner_layer)
            def _():
                current_copy(step, 0, X).start()

            flags = [jnp.where(PR[i] == section, 1.0, 0.0) for i in range(2)]

            def place(flag):
                def work(x):
                    value = jnp.broadcast_to(flag[0:1], (Y, Z)) * GB[step, x + 1]

                    def store(value):
                        BB[x + 1] = value
                        B[x + 2, rows, :] = B[x + 2, rows, :] + 0.5 * value
                    return value, store
                return work
            for n, (low, count) in enumerate(parts):
                @pl.when(jnp.logical_or(sec != heart - 2, step == 0))
                def _():
                    wait_source(step, n)

                @pl.when(jnp.logical_and(sec == heart - 2, step == 0))
                def _():
                    relay_source(step, n).start()
                if n in inner:
                    for_planes(low - 1, count, 5, place(own))
                else:
                    for x in (low - 1, low):
                        value, store = place({-1: flags[0], X: flags[1]}.get(x, own))(x)
                        store(value)

            for j, at in ((0, Y - 1), (1, 0)):
                flat, where = across(GB, at, step * (X + 2) + 1, X, Y)
                BR[j] = jnp.broadcast_to(own_y[j][0:1], (X, Z)) * flat[where, :]
                R2[j] = R2[j] + 0.5 * BR[j]
            second_sweep(0, push[1], None, True)

            def group(g, carry):
                slot = lax.rem(g, 2)

                @pl.when(jnp.logical_and(g == 1, sec == heart - 2))
                def _():
                    remote(JB.at[step, 0], JB.at[step, 0], jsend.at[step], jrecv.at[step, 0],
                           heart, brick).wait_recv()

                    def add(x):
                        def store(value):
                            JA[step, x] = value
                        return JA[step, x] + JB[step, 0, x], store
                    for_planes(0, X, 4, add)

                @pl.when(jnp.logical_and(g <= pieces, jnp.logical_not(inner_layer)))
                def _():
                    current_copy(step, (g - 1) * piece, piece).start()

                @pl.when(jnp.logical_and(jnp.logical_and(g == GROUPS - 3, step + 1 < STEPS),
                                         sec == heart - 2))
                def _():
                    for n in range(len(parts)):
                        wait_source(step + 1, n)
                        relay_source(step + 1, n).start()

                first = push[2 * g]
                first_sweep(slot, g, False, first)
                going_on = step < STEPS - 1
                second_sweep(slot, push[2 * g + 1], jnp.where(going_on, push[SWEEPS + g], 1.0),
                             jnp.logical_or(g < GROUPS - 1, going_on))
                return carry

            lax.fori_loop(1, GROUPS, group, 0)
            return carry

        send_across(0)
        send_corners(0)
        send_planes(0)
        for there, src, dst, land, far, near, s, b in init_copies():
            @pl.when(there)
            def _():
                remote(src, dst, isend.at[near], irecv.at[far], s, b).start()
        lax.fori_loop(0, STEPS, step_body, 0)

        result = pltpu.make_async_copy(A.at[pl.ds(2, X), rows], out.at[0], lsem.at[0])
        result.start()
        wait_sent((GROUPS - 1) % 2)
        for step in range(STEPS):
            current_copy(step, 0, X).wait_send()

            @pl.when(sec == heart - 2)
            def _():
                for n in range(len(parts)):
                    relay_source(step, n).wait_send()

        result.wait()

    field.wait()
    for early in (True, False):
        pl.when(is_heart)(functools.partial(heart_program, early))
        pl.when(jnp.logical_not(is_heart))(functools.partial(torso_program, early))
        if early:
            pl.semaphore_wait(barrier, total)


def body(mesh, potentials, coefficient, recovery, excitable, row_of):
    sections, bricks = mesh.shape["sec"], mesh.shape["brick"]
    _, X, Y, Z = potentials.shape
    f32 = jnp.float32
    scratch = [
        ((X + 4, Y + 2 * PAD, Z), f32), ((X + 4, Y + 2 * PAD, Z), f32),
        ((X + 2, Y, Z), f32), ((STEPS, X + 2, Y, Z), f32), ((X + 2, Y, Z), f32),
        ((STEPS, X, Y, Z), f32), ((STEPS, 2, X, Y, Z), f32),
        ((X, Y, Z), f32), ((X, Y, Z), f32), ((X, Y, Z), jnp.int32),
        ((2, 4 * (X + Y) + 32, Z), f32), ((2, 4 * (X + Y) + 32, Z), f32),
        ((2, 4 * (X + Y) + 32, Z), f32), ((2 * max(X, Y), Z), f32),
        ((2, X + 2 * PAD, Z), f32), ((2, X, Z), f32),
        ((2, X, Z), f32), ((2, X, Z), f32), ((2, X, Z), f32),
        ((2, 8, Z), f32), ((STEPS + 1, 2, 2, Y, Z), f32), ((8, Z), f32),
    ]
    sems = [(4,), (2,), (2,), (6,), (6,), (STEPS, 5, 3), (STEPS, 5), (STEPS,), (STEPS, 2),
            (2,), (STEPS + 1, 2)]
    hbm = pl.BlockSpec(memory_space=pltpu.HBM)
    cells = X * Y * Z
    fields = pl.pallas_call(
        functools.partial(kernel, sections, bricks),
        out_shape=jax.ShapeDtypeStruct(potentials.shape, f32),
        in_specs=[hbm] * 4 + [pl.BlockSpec(memory_space=pltpu.SMEM)],
        out_specs=hbm,
        scratch_shapes=[pltpu.VMEM(s, t) for s, t in scratch]
        + [pltpu.SMEM((len(PUSHES),), f32)]
        + [pltpu.SemaphoreType.DMA(s) for s in sems],
        compiler_params=pltpu.CompilerParams(
            collective_id=0, has_side_effects=True, vmem_limit_bytes=63 * 2**20 + 2**19),
        cost_estimate=pl.CostEstimate(
            flops=cells * STEPS * SWEEPS * 12, bytes_accessed=20 * cells, transcendentals=0),
    )(potentials, coefficient, recovery, excitable, row_of)
    torso = lax.axis_index("sec") < sections - 1
    return fields * jnp.where(torso, PUSHES[-1], 1.0).astype(f32)


def solution(mesh):
    in_specs = (
        P("sec", "brick", None, None),
        P("sec", "brick", None, None),
        P("brick", None, None),
        P("brick", None, None),
        P("brick"),
    )
    out_specs = P("sec", "brick", None, None)
    return jax.shard_map(functools.partial(body, mesh), mesh=mesh, in_specs=in_specs,
                         out_specs=out_specs, check_vma=False)
```

```python
import functools

import jax
import jax.numpy as jnp
from jax import lax
from jax.experimental import pallas as pl
from jax.experimental.pallas import tpu as pltpu
from jax.sharding import PartitionSpec as P

SUBSTEPS = 8
SWEEPS = 16
STEPS = 2
GROUPS = SWEEPS // 2

coupling_gain = 0.1
ionic_timestep = 0.05
ionic_gain = 8.0
recovery_rate = 0.1
recovery_decay = 0.5
spectrum_low = 0.04
spectrum_high = 12.32

center = 0.5 * (spectrum_high + spectrum_low)
spread = 0.5 * (spectrum_high - spectrum_low)
back = (0.5 * spread) ** 2


def push_weights():
    ratio = center / spread
    values = [1.0, ratio]
    while len(values) <= SWEEPS:
        values.append(2.0 * ratio * values[-1] - values[-2])
    grown = [(0.5 * spread) ** k * values[k] for k in range(SWEEPS + 1)]
    return grown[:SWEEPS] + [1.0] * (GROUPS - 1) + [1.0 / grown[SWEEPS]]


PUSHES = push_weights()
MESH = pl.DeviceIdType.MESH
PAD = 8
DIAGONAL = ((0, 0), (0, 1), (1, 0), (1, 1))


def largest_divisor(count, limit):
    return max(u for u in range(1, limit + 1) if count % u == 0)


def for_planes(first, count, limit, work):
    unroll = largest_divisor(count, limit)

    def chunk(i, carry):
        done = [work(first + i * unroll + j) for j in range(unroll)]
        for value, store in done:
            store(value)
        return carry

    lax.fori_loop(0, count // unroll, chunk, 0)


def in_line(first, count, work):
    for x in range(first, first + count):
        value, store = work(x)
        store(value)


def kernel(sections, bricks, pot, coef, rec, exc, row_of, out,
           A, B, EB, GB, BB, JA, JB, W, T, M, H, S, DUMP, ZB, R, R2, ER, SE, BR, PR, VH, row, push,
           lsem, sent, landing, isend, irecv, gsend, grecv, jsend, jrecv, vsend, vrecv):
    X, Y, Z = W.shape
    sec = lax.axis_index("sec")
    brick = lax.axis_index("brick")
    heart = sections - 1
    is_heart = sec == heart
    has_x = (brick > 0, brick < bricks - 1)
    to_x = (brick - 1, brick + 1)
    has_y = (jnp.logical_and(sec > 0, sec < heart), sec < heart - 1)
    to_y = (sec - 1, sec + 1)
    rows = pl.ds(PAD, Y)
    lane = lax.broadcasted_iota(jnp.int32, (Y, Z), 1)
    lane_x = lax.broadcasted_iota(jnp.int32, (X, Z), 1)

    def across(buf, at, first, count, pitch):
        return buf.reshape(buf.size // Z, Z), pl.ds(first * pitch + at, count, stride=pitch)

    def remote(src, dst, send, recv, s, b):
        return pltpu.make_async_remote_copy(
            src_ref=src, dst_ref=dst, send_sem=send, recv_sem=recv,
            device_id={"sec": s, "brick": b}, device_id_type=MESH)

    for n, value in enumerate(PUSHES):
        push[n] = jnp.float32(value)
    field = pltpu.make_async_copy(pot.at[0], A.at[pl.ds(2, X), rows], lsem.at[0])
    second = pltpu.make_async_copy(coef.at[0], T, lsem.at[1])
    field.start()
    second.start()

    barrier = pltpu.get_barrier_semaphore()

    @pl.when(jnp.logical_not(is_heart))
    def _():
        def clear(i, carry):
            for buf in (A, B):
                buf[i, 0:PAD, :] = jnp.zeros((PAD, Z), jnp.float32)
                buf[i, pl.ds(PAD + Y, PAD), :] = jnp.zeros((PAD, Z), jnp.float32)
            return carry

        lax.fori_loop(0, X + 4, clear, 0)
        for buf in (ZB, ER, R2):
            buf[...] = jnp.zeros(buf.shape, jnp.float32)
        EB[0] = jnp.zeros((Y, Z), jnp.float32)
        EB[X + 1] = jnp.zeros((Y, Z), jnp.float32)
        PR[...] = jnp.full(PR.shape, -1.0, jnp.float32)
        row[...] = jnp.full(row.shape, row_of[0].astype(jnp.float32), jnp.float32)

    for d in range(1, sections):
        pl.semaphore_signal(barrier, inc=1, device_id={"sec": lax.rem(sec + d, sections)},
                            device_id_type=MESH)
    total = sections - 1
    for i in range(2):
        @pl.when(has_x[i])
        def _():
            pl.semaphore_signal(barrier, inc=1, device_id={"sec": sec, "brick": to_x[i]},
                                device_id_type=MESH)
        total = total + has_x[i].astype(jnp.int32)
    for i, j in DIAGONAL:
        both = jnp.logical_and(has_x[i], has_y[j])

        @pl.when(both)
        def _():
            pl.semaphore_signal(barrier, inc=1, device_id={"sec": to_y[j], "brick": to_x[i]},
                                device_id_type=MESH)
        total = total + both.astype(jnp.int32)

    cuts = largest_divisor(X - 2, 3)
    size = (X - 2) // cuts
    parts = [(2 + n * size, size) for n in range(cuts)] + [(0, 2), (X, 2)]
    inner, outer = range(cuts), range(cuts, cuts + 2)

    def source_copy(step, n, lane_number, target):
        ref = GB.at[step, pl.ds(parts[n][0], parts[n][1])]
        return remote(ref, ref, gsend.at[step, n, lane_number], grecv.at[step, n], target, brick)

    def heart_program(early):
        recover = pltpu.make_async_copy(rec, W, lsem.at[2])
        excite = pltpu.make_async_copy(exc, M, lsem.at[3])

        def send_sides(round_number):
            for i in range(2):
                src = A.at[pl.ds(2, 2) if i == 0 else pl.ds(X, 2), rows]

                @pl.when(has_x[i])
                def _():
                    remote(src, VH.at[round_number, 1 - i], vsend.at[i],
                           vrecv.at[round_number, 1 - i], sec, to_x[i]).start()

        def sides(round_number):
            for i in range(2):
                src = A.at[pl.ds(2, 2) if i == 0 else pl.ds(X, 2), rows]
                at = 0 if i == 0 else X + 2

                @pl.when(has_x[i])
                def _():
                    got = remote(src, VH.at[round_number, i], vsend.at[i],
                                 vrecv.at[round_number, i], sec, to_x[i])
                    got.wait_recv()
                    got.wait_send()
                    for j in range(2):
                        A[at + j, rows, :] = VH[round_number, i, j]

                @pl.when(jnp.logical_not(has_x[i]))
                def _():
                    for j in range(2):
                        A[at + j, rows, :] = A[2 if i == 0 else X + 1, rows, :]

            edge_rows(0, 2)
            edge_rows(X + 2, X + 4)

        def edge_rows(low, high):
            def edge(i, carry):
                A[i, pl.ds(PAD - 1, 1), :] = A[i, pl.ds(PAD, 1), :]
                A[i, pl.ds(PAD + Y, 1), :] = A[i, pl.ds(PAD + Y - 1, 1), :]
                return carry

            lax.fori_loop(low, high, edge, 0)

        def laplace(x):
            c = A[x + 2, rows, :]
            total = A[x + 1, rows, :] + A[x + 3, rows, :]
            total = total + A[x + 2, pl.ds(PAD - 1, Y), :] + A[x + 2, pl.ds(PAD + 1, Y), :]
            total = total + jnp.where(lane == 0, c, pltpu.roll(c, 1, 1))
            total = total + jnp.where(lane == Z - 1, c, pltpu.roll(c, Z - 1, 1))
            return total - 6.0 * c

        def ionic(x):
            v = A[x + 2, rows, :]
            w = W[x]
            thresh = T[x]
            active = ionic_timestep * M[x].astype(jnp.float32)
            for _ in range(SUBSTEPS):
                drive = ionic_gain * v * (v - thresh) * (1.0 - v) - w
                relax = recovery_rate * (v - recovery_decay * w)
                v = v + active * drive
                w = w + active * relax

            def store(value):
                A[x + 2, rows, :] = value[0]
                W[x] = value[1]
            return (v, w), store

        def sum_up(step, chunks):
            def work(x):
                def store(value):
                    GB[step, x + 1] = value
                return laplace(x), store
            for n in chunks:
                low, count = parts[n]
                for_planes(low - 1, count, 5, work)

        def hand_out(step, chunks):
            for n in chunks:
                for far in (2, 1):
                    source_copy(step, n, far - 1, heart - far).start()

        def current(step):
            for n in range(2):
                remote(JB.at[step, n], JB.at[step, n], jsend.at[step], jrecv.at[step, n],
                       heart - 1 - n, brick).wait_recv()

        if early:
            recover.start()
            excite.start()
            edge_rows(2, X + 2)
            sum_up(0, inner)
            return
        send_sides(0)
        hand_out(0, inner)
        sides(0)
        sum_up(0, outer)
        hand_out(0, outer)
        second.wait()
        recover.wait()
        excite.wait()
        for step in range(STEPS):
            for_planes(0, X, 2, ionic)
            send_sides(step + 1)
            edge_rows(2, X + 2)
            sides(step + 1)
            if step + 1 < STEPS:
                sum_up(step + 1, range(len(parts)))
                hand_out(step + 1, range(len(parts)))
                current(step)

                def advance(x):
                    def store(value):
                        A[x + 2, rows, :] = value
                    gain = GB[step + 1, x + 1] + (JB[step, 0, x] + JB[step, 1, x])
                    return A[x + 2, rows, :] + coupling_gain * gain, store
                for_planes(0, X, 4, advance)
            else:
                def before(x):
                    def store(value):
                        BB[x] = value
                    return A[x + 2, rows, :] + coupling_gain * laplace(x), store
                for_planes(0, X, 4, before)
                current(step)

                def final(x):
                    def store(value):
                        BB[x] = value
                    return BB[x] + coupling_gain * (JB[step, 0, x] + JB[step, 1, x]), store
                for_planes(0, X, 4, final)
                result = pltpu.make_async_copy(BB.at[pl.ds(0, X)], out.at[0], lsem.at[0])
                result.start()
                result.wait()
        for step in range(STEPS):
            for n in range(len(parts)):
                for far in (2, 1):
                    source_copy(step, n, far - 1, heart - far).wait_send()

    def torso_program(early):
        one = jnp.ones((), jnp.float32)
        zero = jnp.zeros((), jnp.float32)
        inside_x = [jnp.where(h, one, zero) for h in has_x]
        inside_y = [jnp.where(h, one, zero) for h in has_y]
        section = sec.astype(jnp.float32)
        own = jnp.where(row[...] == section, 1.0, 0.0)
        own_y = (jnp.where(row[...] == section - 1.0, 1.0, 0.0),
                 jnp.where(row[...] == section + 1.0, 1.0, 0.0))

        at_x = [(2 * Y * i, 2 * Y) for i in range(2)]
        at_y = [(4 * Y + 2 * X * j, 2 * X) for j in range(2)]
        at_c = [(4 * (X + Y) + 8 * n, 8) for n in range(4)]

        def message(slot, there, here, s, b):
            there_at, here_at = pl.ds(*there), pl.ds(*here)
            return remote(S.at[slot, here_at], H.at[slot, there_at], sent.at[slot],
                          landing.at[slot], s, b)

        def nothing(slot, here):
            zeros = ZB.at[pl.ds(0, here[1])]
            pltpu.make_async_copy(zeros, H.at[slot, pl.ds(*here)], landing.at[slot]).start()
            pltpu.make_async_copy(zeros, DUMP.at[slot, pl.ds(*here)], sent.at[slot]).start()

        def send_corners(slot):
            for n, (i, j) in enumerate(DIAGONAL):
                both = jnp.logical_and(has_x[i], has_y[j])

                @pl.when(both)
                def _():
                    message(slot, at_c[3 - n], at_c[n], to_y[j], to_x[i]).start()

                @pl.when(jnp.logical_not(both))
                def _():
                    nothing(slot, at_c[n])

        def send_planes(slot):
            def one_side(i):
                @pl.when(has_x[i])
                def _():
                    for n in range(2):
                        message(slot, (at_x[1 - i][0] + n * Y, Y), (at_x[i][0] + n * Y, Y),
                                sec, to_x[i]).start()

                @pl.when(jnp.logical_not(has_x[i]))
                def _():
                    nothing(slot, at_x[i])

            even = lax.rem(brick, 2) == 0

            @pl.when(even)
            def _():
                one_side(0)
                one_side(1)

            @pl.when(jnp.logical_not(even))
            def _():
                one_side(1)
                one_side(0)

        def send_across(slot):
            for j in range(2):
                @pl.when(has_y[j])
                def _():
                    message(slot, at_y[1 - j], at_y[j], to_y[j], brick).start()

                @pl.when(jnp.logical_not(has_y[j]))
                def _():
                    nothing(slot, at_y[j])

        def wait_landed(slot):
            pltpu.make_async_copy(S.at[slot], H.at[slot], landing.at[slot]).wait()

        def wait_sent(slot):
            pltpu.make_async_copy(S.at[slot], DUMP.at[slot], sent.at[slot]).wait()

        def pack_rows(slot):
            for j in range(2):
                for n in range(2):
                    at = PAD + n if j == 0 else PAD + Y - 1 - n
                    flat, where = across(A, at, 2, X, Y + 2 * PAD)
                    S[slot, pl.ds(at_y[j][0] + n * X, X), :] = flat[where, :]

        def pack_planes(slot):
            for i in range(2):
                for n in range(2):
                    value = A[(2 if i == 0 else X) + n, rows, :]
                    S[slot, pl.ds(at_x[i][0] + n * Y, Y), :] = value
        def pack_corners(slot):
            for n, (i, j) in enumerate(DIAGONAL):
                corner = A[2 if i == 0 else X + 1, pl.ds(PAD if j == 0 else PAD + Y - 1, 1), :]
                S[slot, pl.ds(at_c[n][0], 1), :] = corner

        def stencil(src, x, low, high):
            here = pl.ds(PAD + low, high - low)
            at_lane = lane[0:high - low]
            c = src[x + 2, here, :]
            total = src[x + 1, here, :] + src[x + 3, here, :]
            total = total + (src[x + 2, pl.ds(PAD + low - 1, high - low), :]
                             + src[x + 2, pl.ds(PAD + low + 1, high - low), :])
            total = total + (jnp.where(at_lane == 0, 0.0, pltpu.roll(c, 1, 1))
                             + jnp.where(at_lane == Z - 1, 0.0, pltpu.roll(c, Z - 1, 1)))
            return total + EB[x + 1, pl.ds(low, high - low), :] * c

        def plane(src, dst, first, weight, scale=None, low=0, high=Y):
            here = pl.ds(PAD + low, high - low)

            def work(x):
                value = stencil(src, x, low, high)
                if first:
                    value = 0.5 * value
                else:
                    value = ((value + weight * BB[x + 1, pl.ds(low, high - low), :])
                             - back * dst[x + 2, here, :])
                if scale is not None:
                    value = scale * value

                def store(value):
                    dst[x + 2, here, :] = value
                return value, store
            return work

        def mend(dst, low, high, halo, offset, scale):
            for j, at in ((0, PAD), (1, PAD + Y - 1)):
                flat, where = across(dst, at, low + 2, high - low, Y + 2 * PAD)
                flat[where, :] = flat[where, :] + scale * halo[j, pl.ds(low + offset, high - low), :]

        def fringe(slot, first, weight):
            for j in range(2):
                c = R[j, pl.ds(PAD, X), :]
                total = R[j, pl.ds(PAD - 1, X), :] + R[j, pl.ds(PAD + 1, X), :]
                total = total + S[slot, pl.ds(at_y[j][0], X), :] + H[slot, pl.ds(at_y[j][0] + X, X), :]
                total = total + jnp.where(lane_x == 0, 0.0, pltpu.roll(c, 1, 1))
                total = total + jnp.where(lane_x == Z - 1, 0.0, pltpu.roll(c, Z - 1, 1))
                total = total + ER[j] * c
                if first:
                    R2[j] = (0.5 * inside_y[j]) * total
                else:
                    R2[j] = inside_y[j] * (total + weight * BR[j] - back * R2[j])

        def landed(slot):
            for j in range(2):
                A[j, rows, :] = H[slot, pl.ds(at_x[0][0] + j * Y, Y), :]
                A[X + 2 + j, rows, :] = H[slot, pl.ds(at_x[1][0] + j * Y, Y), :]
                R[j, pl.ds(PAD, X), :] = H[slot, pl.ds(at_y[j][0], X), :]
            for n, (i, j) in enumerate(DIAGONAL):
                R[j, pl.ds(PAD - 1 if i == 0 else PAD + X, 1), :] = H[slot, pl.ds(at_c[n][0], 1), :]

        def first_sweep(slot, number, first, weight, prepare=lambda: None):
            in_line(1, X - 2, plane(A, B, first, weight))

            @pl.when(number > 0)
            def _():
                wait_sent(1 - slot)
            wait_landed(slot)
            prepare()
            landed(slot)
            done = [plane(A, B, first, weight, scale)(x) for x, scale in
                    ((-1, inside_x[0]), (0, None), (X - 1, None), (X, inside_x[1]))]
            for value, store in done:
                store(value)
            fringe(slot, first, weight)
            mend(B, -1, X + 1, R, PAD, 0.5 if first else 1.0)

        def relay_source(step, n):
            return source_copy(step, n, 2, heart - 3)

        def wait_source(step, n):
            source_copy(step, n, 2, heart).wait_recv()

        inner_layer = sec == heart - 3
        pieces = largest_divisor(X, 4)
        piece = X // pieces

        def current_copy(step, low, count):
            target = jnp.where(inner_layer, heart - 2, heart)
            place = jnp.where(sec == heart - 2, 1, 0)
            span = pl.ds(low, count)
            return remote(JA.at[step, span], JB.at[step, place, span], jsend.at[step],
                          jrecv.at[step, place], target, brick)

        def init_copies():
            found = []
            for i in range(2):
                found.append((has_x[i], EB.at[1 if i == 0 else X], EB.at[X + 1 if i == 0 else 0],
                              EB.at[0 if i == 0 else X + 1], 1 - i, i, sec, to_x[i]))
                found.append((has_x[i], row, PR.at[1 - i], PR.at[i], 5 - i, 4 + i, sec, to_x[i]))
            for j in range(2):
                found.append((has_y[j], SE.at[j], ER.at[1 - j], ER.at[j], 3 - j, 2 + j,
                              to_y[j], brick))
            return found

        def set_up():
            second.wait()

            def absorb(x):
                def store(value):
                    EB[x + 1] = value
                return (center - 6.0) - T[x], store
            for_planes(0, X, 4, absorb)

            for j, at in ((0, 0), (1, Y - 1)):
                flat, where = across(EB, at, 1, X, Y)
                SE[j] = flat[where, :]
            pack_rows(0)
            pack_corners(0)
            pack_planes(0)

        if early:
            set_up()
            return

        def second_sweep(slot, weight, scale, more):
            after = 1 - slot
            for j, at in ((0, PAD - 1), (1, PAD + Y)):
                flat, where = across(B, at, 2, X, Y + 2 * PAD)
                flat[where, :] = R2[j]
            outer_planes = plane(B, A, False, weight, scale)
            done = [outer_planes(x) for x in (0, 1, X - 2, X - 1)]
            for value, store in done:
                store(value)

            @pl.when(more)
            def _():
                pack_corners(after)
                pack_planes(after)
                send_corners(after)
                send_planes(after)
            band = 8 if Y > 16 else Y // 2
            for low in (0, Y - band):
                in_line(2, X - 4, plane(B, A, False, weight, scale, low, low + band))

            @pl.when(more)
            def _():
                pack_rows(after)
                send_across(after)
            if Y > 2 * band:
                in_line(2, X - 4, plane(B, A, False, weight, scale, band, Y - band))

        def step_body(step, carry):
            def prepare():
                @pl.when(step == 0)
                def _():
                    for there, src, dst, land, far, near, s, b in init_copies():
                        @pl.when(there)
                        def _():
                            got = remote(src, land, isend.at[near], irecv.at[near], s, b)
                            got.wait_recv()
                            got.wait_send()

            first_sweep(0, step, True, None, prepare)

            def current(x):
                def store(value):
                    JA[step, x] = value
                own_v = jnp.broadcast_to(own[0:1], (Y, Z))
                value = 2.0 * B[x + 2, rows, :] - (EB[x + 1] + 6.0) * A[x + 2, rows, :]
                return own_v * value, store
            for_planes(0, X, 4, current)


            flags = [jnp.where(PR[i] == section, 1.0, 0.0) for i in range(2)]

            def place(flag):
                def work(x):
                    value = jnp.broadcast_to(flag[0:1], (Y, Z)) * GB[step, x + 1]

                    def store(value):
                        BB[x + 1] = value
                        B[x + 2, rows, :] = B[x + 2, rows, :] + 0.5 * value
                    return value, store
                return work
            for n, (low, count) in enumerate(parts):
                @pl.when(jnp.logical_or(sec != heart - 2, step == 0))
                def _():
                    wait_source(step, n)

                @pl.when(jnp.logical_and(sec == heart - 2, step == 0))
                def _():
                    relay_source(step, n).start()
                if n in inner:
                    for_planes(low - 1, count, 5, place(own))
                else:
                    for x in (low - 1, low):
                        value, store = place({-1: flags[0], X: flags[1]}.get(x, own))(x)
                        store(value)

            for j, at in ((0, Y - 1), (1, 0)):
                flat, where = across(GB, at, step * (X + 2) + 1, X, Y)
                BR[j] = jnp.broadcast_to(own_y[j][0:1], (X, Z)) * flat[where, :]
                R2[j] = R2[j] + 0.5 * BR[j]
            second_sweep(0, push[1], None, True)

            @pl.when(inner_layer)
            def _():
                current_copy(step, 0, X).start()

            def group(g, carry):
                slot = lax.rem(g, 2)

                @pl.when(jnp.logical_and(g == 2, sec == heart - 2))
                def _():
                    remote(JB.at[step, 0], JB.at[step, 0], jsend.at[step], jrecv.at[step, 0],
                           heart, brick).wait_recv()

                    def add(x):
                        def store(value):
                            JA[step, x] = value
                        return JA[step, x] + JB[step, 0, x], store
                    for_planes(0, X, 4, add)

                @pl.when(jnp.logical_and(jnp.logical_and(g >= 2, g < pieces + 2),
                                         jnp.logical_not(inner_layer)))
                def _():
                    current_copy(step, (g - 2) * piece, piece).start()

                @pl.when(jnp.logical_and(jnp.logical_and(g == GROUPS - 3, step + 1 < STEPS),
                                         sec == heart - 2))
                def _():
                    for n in range(len(parts)):
                        wait_source(step + 1, n)
                        relay_source(step + 1, n).start()

                first = push[2 * g]
                first_sweep(slot, g, False, first)
                going_on = step < STEPS - 1
                second_sweep(slot, push[2 * g + 1], jnp.where(going_on, push[SWEEPS + g], 1.0),
                             jnp.logical_or(g < GROUPS - 1, going_on))
                return carry

            lax.fori_loop(1, GROUPS, group, 0)
            return carry

        send_across(0)
        send_corners(0)
        send_planes(0)
        for there, src, dst, land, far, near, s, b in init_copies():
            @pl.when(there)
            def _():
                remote(src, dst, isend.at[near], irecv.at[far], s, b).start()
        lax.fori_loop(0, STEPS, step_body, 0)

        result = pltpu.make_async_copy(A.at[pl.ds(2, X), rows], out.at[0], lsem.at[0])
        result.start()
        wait_sent((GROUPS - 1) % 2)
        for step in range(STEPS):
            current_copy(step, 0, X).wait_send()

            @pl.when(sec == heart - 2)
            def _():
                for n in range(len(parts)):
                    relay_source(step, n).wait_send()

        result.wait()

    field.wait()
    for early in (True, False):
        pl.when(is_heart)(functools.partial(heart_program, early))
        pl.when(jnp.logical_not(is_heart))(functools.partial(torso_program, early))
        if early:
            pl.semaphore_wait(barrier, total)


def body(mesh, potentials, coefficient, recovery, excitable, row_of):
    sections, bricks = mesh.shape["sec"], mesh.shape["brick"]
    _, X, Y, Z = potentials.shape
    f32 = jnp.float32
    scratch = [
        ((X + 4, Y + 2 * PAD, Z), f32), ((X + 4, Y + 2 * PAD, Z), f32),
        ((X + 2, Y, Z), f32), ((STEPS, X + 2, Y, Z), f32), ((X + 2, Y, Z), f32),
        ((STEPS, X, Y, Z), f32), ((STEPS, 2, X, Y, Z), f32),
        ((X, Y, Z), f32), ((X, Y, Z), f32), ((X, Y, Z), jnp.int32),
        ((2, 4 * (X + Y) + 32, Z), f32), ((2, 4 * (X + Y) + 32, Z), f32),
        ((2, 4 * (X + Y) + 32, Z), f32), ((2 * max(X, Y), Z), f32),
        ((2, X + 2 * PAD, Z), f32), ((2, X, Z), f32),
        ((2, X, Z), f32), ((2, X, Z), f32), ((2, X, Z), f32),
        ((2, 8, Z), f32), ((STEPS + 1, 2, 2, Y, Z), f32), ((8, Z), f32),
    ]
    sems = [(4,), (2,), (2,), (6,), (6,), (STEPS, 5, 3), (STEPS, 5), (STEPS,), (STEPS, 2),
            (2,), (STEPS + 1, 2)]
    hbm = pl.BlockSpec(memory_space=pltpu.HBM)
    cells = X * Y * Z
    fields = pl.pallas_call(
        functools.partial(kernel, sections, bricks),
        out_shape=jax.ShapeDtypeStruct(potentials.shape, f32),
        in_specs=[hbm] * 4 + [pl.BlockSpec(memory_space=pltpu.SMEM)],
        out_specs=hbm,
        scratch_shapes=[pltpu.VMEM(s, t) for s, t in scratch]
        + [pltpu.SMEM((len(PUSHES),), f32)]
        + [pltpu.SemaphoreType.DMA(s) for s in sems],
        compiler_params=pltpu.CompilerParams(
            collective_id=0, has_side_effects=True, vmem_limit_bytes=63 * 2**20 + 2**19),
        cost_estimate=pl.CostEstimate(
            flops=cells * STEPS * SWEEPS * 12, bytes_accessed=20 * cells, transcendentals=0),
    )(potentials, coefficient, recovery, excitable, row_of)
    torso = lax.axis_index("sec") < sections - 1
    return fields * jnp.where(torso, PUSHES[-1], 1.0).astype(f32)


def solution(mesh):
    in_specs = (
        P("sec", "brick", None, None),
        P("sec", "brick", None, None),
        P("brick", None, None),
        P("brick", None, None),
        P("brick"),
    )
    out_specs = P("sec", "brick", None, None)
    return jax.shard_map(functools.partial(body, mesh), mesh=mesh, in_specs=in_specs,
                         out_specs=out_specs, check_vma=False)
```

```python
import functools

import jax
import jax.numpy as jnp
from jax import lax
from jax.experimental import pallas as pl
from jax.experimental.pallas import tpu as pltpu
from jax.sharding import PartitionSpec as P

SUBSTEPS = 8
SWEEPS = 16
STEPS = 2
GROUPS = SWEEPS // 2

coupling_gain = 0.1
ionic_timestep = 0.05
ionic_gain = 8.0
recovery_rate = 0.1
recovery_decay = 0.5
spectrum_low = 0.04
spectrum_high = 12.32

center = 0.5 * (spectrum_high + spectrum_low)
spread = 0.5 * (spectrum_high - spectrum_low)
back = (0.5 * spread) ** 2


def push_weights():
    ratio = center / spread
    values = [1.0, ratio]
    while len(values) <= SWEEPS:
        values.append(2.0 * ratio * values[-1] - values[-2])
    grown = [(0.5 * spread) ** k * values[k] for k in range(SWEEPS + 1)]
    return grown[:SWEEPS] + [1.0] * (GROUPS - 1) + [1.0 / grown[SWEEPS]]


PUSHES = push_weights()
MESH = pl.DeviceIdType.MESH
PAD = 8
DIAGONAL = ((0, 0), (0, 1), (1, 0), (1, 1))


def largest_divisor(count, limit):
    return max(u for u in range(1, limit + 1) if count % u == 0)


def for_planes(first, count, limit, work):
    unroll = largest_divisor(count, limit)

    def chunk(i, carry):
        done = [work(first + i * unroll + j) for j in range(unroll)]
        for value, store in done:
            store(value)
        return carry

    lax.fori_loop(0, count // unroll, chunk, 0)


def in_line(first, count, work):
    for x in range(first, first + count):
        value, store = work(x)
        store(value)


def kernel(sections, bricks, pot, coef, rec, exc, row_of, out,
           A, B, EB, GB, BB, JA, JB, W, T, M, H, S, DUMP, ZB, R, R2, ER, SE, BR, PR, VH, row, push,
           lsem, sent, landing, isend, irecv, gsend, grecv, jsend, jrecv, vsend, vrecv):
    X, Y, Z = W.shape
    sec = lax.axis_index("sec")
    brick = lax.axis_index("brick")
    heart = sections - 1
    is_heart = sec == heart
    has_x = (brick > 0, brick < bricks - 1)
    to_x = (brick - 1, brick + 1)
    has_y = (jnp.logical_and(sec > 0, sec < heart), sec < heart - 1)
    to_y = (sec - 1, sec + 1)
    rows = pl.ds(PAD, Y)
    lane = lax.broadcasted_iota(jnp.int32, (Y, Z), 1)
    lane_x = lax.broadcasted_iota(jnp.int32, (X, Z), 1)

    def across(buf, at, first, count, pitch):
        return buf.reshape(buf.size // Z, Z), pl.ds(first * pitch + at, count, stride=pitch)

    def remote(src, dst, send, recv, s, b):
        return pltpu.make_async_remote_copy(
            src_ref=src, dst_ref=dst, send_sem=send, recv_sem=recv,
            device_id={"sec": s, "brick": b}, device_id_type=MESH)

    for n, value in enumerate(PUSHES):
        push[n] = jnp.float32(value)
    field = pltpu.make_async_copy(pot.at[0], A.at[pl.ds(2, X), rows], lsem.at[0])
    second = pltpu.make_async_copy(coef.at[0], T, lsem.at[1])
    field.start()
    second.start()

    barrier = pltpu.get_barrier_semaphore()

    @pl.when(jnp.logical_not(is_heart))
    def _():
        def clear(i, carry):
            for buf in (A, B):
                buf[i, 0:PAD, :] = jnp.zeros((PAD, Z), jnp.float32)
                buf[i, pl.ds(PAD + Y, PAD), :] = jnp.zeros((PAD, Z), jnp.float32)
            return carry

        lax.fori_loop(0, X + 4, clear, 0)
        for buf in (ZB, ER, R2):
            buf[...] = jnp.zeros(buf.shape, jnp.float32)
        EB[0] = jnp.zeros((Y, Z), jnp.float32)
        EB[X + 1] = jnp.zeros((Y, Z), jnp.float32)
        PR[...] = jnp.full(PR.shape, -1.0, jnp.float32)
        row[...] = jnp.full(row.shape, row_of[0].astype(jnp.float32), jnp.float32)

    for d in range(1, sections):
        pl.semaphore_signal(barrier, inc=1, device_id={"sec": lax.rem(sec + d, sections)},
                            device_id_type=MESH)
    total = sections - 1
    for i in range(2):
        @pl.when(has_x[i])
        def _():
            pl.semaphore_signal(barrier, inc=1, device_id={"sec": sec, "brick": to_x[i]},
                                device_id_type=MESH)
        total = total + has_x[i].astype(jnp.int32)
    for i, j in DIAGONAL:
        both = jnp.logical_and(has_x[i], has_y[j])

        @pl.when(both)
        def _():
            pl.semaphore_signal(barrier, inc=1, device_id={"sec": to_y[j], "brick": to_x[i]},
                                device_id_type=MESH)
        total = total + both.astype(jnp.int32)

    cuts = largest_divisor(X - 2, 3)
    size = (X - 2) // cuts
    parts = [(2 + n * size, size) for n in range(cuts)] + [(0, 2), (X, 2)]
    inner, outer = range(cuts), range(cuts, cuts + 2)

    def source_copy(step, n, lane_number, target):
        ref = GB.at[step, pl.ds(parts[n][0], parts[n][1])]
        return remote(ref, ref, gsend.at[step, n, lane_number], grecv.at[step, n], target, brick)

    def heart_program(early):
        recover = pltpu.make_async_copy(rec, W, lsem.at[2])
        excite = pltpu.make_async_copy(exc, M, lsem.at[3])

        def send_sides(round_number):
            for i in range(2):
                src = A.at[pl.ds(2, 2) if i == 0 else pl.ds(X, 2), rows]

                @pl.when(has_x[i])
                def _():
                    remote(src, VH.at[round_number, 1 - i], vsend.at[i],
                           vrecv.at[round_number, 1 - i], sec, to_x[i]).start()

        def sides(round_number):
            for i in range(2):
                src = A.at[pl.ds(2, 2) if i == 0 else pl.ds(X, 2), rows]
                at = 0 if i == 0 else X + 2

                @pl.when(has_x[i])
                def _():
                    got = remote(src, VH.at[round_number, i], vsend.at[i],
                                 vrecv.at[round_number, i], sec, to_x[i])
                    got.wait_recv()
                    got.wait_send()
                    for j in range(2):
                        A[at + j, rows, :] = VH[round_number, i, j]

                @pl.when(jnp.logical_not(has_x[i]))
                def _():
                    for j in range(2):
                        A[at + j, rows, :] = A[2 if i == 0 else X + 1, rows, :]

            edge_rows(0, 2)
            edge_rows(X + 2, X + 4)

        def edge_rows(low, high):
            def edge(i, carry):
                A[i, pl.ds(PAD - 1, 1), :] = A[i, pl.ds(PAD, 1), :]
                A[i, pl.ds(PAD + Y, 1), :] = A[i, pl.ds(PAD + Y - 1, 1), :]
                return carry

            lax.fori_loop(low, high, edge, 0)

        def laplace(x):
            c = A[x + 2, rows, :]
            total = A[x + 1, rows, :] + A[x + 3, rows, :]
            total = total + A[x + 2, pl.ds(PAD - 1, Y), :] + A[x + 2, pl.ds(PAD + 1, Y), :]
            total = total + jnp.where(lane == 0, c, pltpu.roll(c, 1, 1))
            total = total + jnp.where(lane == Z - 1, c, pltpu.roll(c, Z - 1, 1))
            return total - 6.0 * c

        def ionic(x):
            v = A[x + 2, rows, :]
            w = W[x]
            thresh = T[x]
            active = ionic_timestep * M[x].astype(jnp.float32)
            for _ in range(SUBSTEPS):
                drive = ionic_gain * v * (v - thresh) * (1.0 - v) - w
                relax = recovery_rate * (v - recovery_decay * w)
                v = v + active * drive
                w = w + active * relax

            def store(value):
                A[x + 2, rows, :] = value[0]
                W[x] = value[1]
            return (v, w), store

        def sum_up(step, chunks):
            def work(x):
                def store(value):
                    GB[step, x + 1] = value
                return laplace(x), store
            for n in chunks:
                low, count = parts[n]
                for_planes(low - 1, count, 5, work)

        def hand_out(step, chunks):
            for n in chunks:
                for far in (2, 1):
                    source_copy(step, n, far - 1, heart - far).start()

        def current(step):
            for n in range(2):
                remote(JB.at[step, n], JB.at[step, n], jsend.at[step], jrecv.at[step, n],
                       heart - 1 - n, brick).wait_recv()

        if early:
            recover.start()
            excite.start()
            edge_rows(2, X + 2)
            sum_up(0, inner)
            return
        send_sides(0)
        hand_out(0, inner)
        sides(0)
        sum_up(0, outer)
        hand_out(0, outer)
        second.wait()
        recover.wait()
        excite.wait()
        for step in range(STEPS):
            for_planes(0, X, 2, ionic)
            send_sides(step + 1)
            edge_rows(2, X + 2)
            sides(step + 1)
            if step + 1 < STEPS:
                sum_up(step + 1, range(len(parts)))
                hand_out(step + 1, range(len(parts)))
                current(step)

                def advance(x):
                    def store(value):
                        A[x + 2, rows, :] = value
                    gain = GB[step + 1, x + 1] + (JB[step, 0, x] + JB[step, 1, x])
                    return A[x + 2, rows, :] + coupling_gain * gain, store
                for_planes(0, X, 4, advance)
            else:
                def before(x):
                    def store(value):
                        BB[x] = value
                    return A[x + 2, rows, :] + coupling_gain * laplace(x), store
                for_planes(0, X, 4, before)
                current(step)

                def final(x):
                    def store(value):
                        BB[x] = value
                    return BB[x] + coupling_gain * (JB[step, 0, x] + JB[step, 1, x]), store
                for_planes(0, X, 4, final)
                result = pltpu.make_async_copy(BB.at[pl.ds(0, X)], out.at[0], lsem.at[0])
                result.start()
                result.wait()
        for step in range(STEPS):
            for n in range(len(parts)):
                for far in (2, 1):
                    source_copy(step, n, far - 1, heart - far).wait_send()

    def torso_program(early):
        one = jnp.ones((), jnp.float32)
        zero = jnp.zeros((), jnp.float32)
        inside_x = [jnp.where(h, one, zero) for h in has_x]
        inside_y = [jnp.where(h, one, zero) for h in has_y]
        section = sec.astype(jnp.float32)
        own = jnp.where(row[...] == section, 1.0, 0.0)
        own_y = (jnp.where(row[...] == section - 1.0, 1.0, 0.0),
                 jnp.where(row[...] == section + 1.0, 1.0, 0.0))

        at_x = [(2 * Y * i, 2 * Y) for i in range(2)]
        at_y = [(4 * Y + 2 * X * j, 2 * X) for j in range(2)]
        at_c = [(4 * (X + Y) + 8 * n, 8) for n in range(4)]

        def message(slot, there, here, s, b):
            there_at, here_at = pl.ds(*there), pl.ds(*here)
            return remote(S.at[slot, here_at], H.at[slot, there_at], sent.at[slot],
                          landing.at[slot], s, b)

        def nothing(slot, here):
            zeros = ZB.at[pl.ds(0, here[1])]
            pltpu.make_async_copy(zeros, H.at[slot, pl.ds(*here)], landing.at[slot]).start()
            pltpu.make_async_copy(zeros, DUMP.at[slot, pl.ds(*here)], sent.at[slot]).start()

        def send_corners(slot):
            for n, (i, j) in enumerate(DIAGONAL):
                both = jnp.logical_and(has_x[i], has_y[j])

                @pl.when(both)
                def _():
                    message(slot, at_c[3 - n], at_c[n], to_y[j], to_x[i]).start()

                @pl.when(jnp.logical_not(both))
                def _():
                    nothing(slot, at_c[n])

        def send_planes(slot):
            def one_side(i):
                @pl.when(has_x[i])
                def _():
                    message(slot, at_x[1 - i], at_x[i], sec, to_x[i]).start()

                @pl.when(jnp.logical_not(has_x[i]))
                def _():
                    nothing(slot, at_x[i])

            even = lax.rem(brick, 2) == 0

            @pl.when(even)
            def _():
                one_side(0)
                one_side(1)

            @pl.when(jnp.logical_not(even))
            def _():
                one_side(1)
                one_side(0)

        def send_across(slot):
            for j in range(2):
                @pl.when(has_y[j])
                def _():
                    message(slot, at_y[1 - j], at_y[j], to_y[j], brick).start()

                @pl.when(jnp.logical_not(has_y[j]))
                def _():
                    nothing(slot, at_y[j])

        def wait_landed(slot):
            pltpu.make_async_copy(S.at[slot], H.at[slot], landing.at[slot]).wait()

        def wait_sent(slot):
            pltpu.make_async_copy(S.at[slot], DUMP.at[slot], sent.at[slot]).wait()

        def pack_rows(slot):
            for j in range(2):
                for n in range(2):
                    at = PAD + n if j == 0 else PAD + Y - 1 - n
                    flat, where = across(A, at, 2, X, Y + 2 * PAD)
                    S[slot, pl.ds(at_y[j][0] + n * X, X), :] = flat[where, :]

        def pack_planes(slot):
            for i in range(2):
                for n in range(2):
                    value = A[(2 if i == 0 else X) + n, rows, :]
                    S[slot, pl.ds(at_x[i][0] + n * Y, Y), :] = value
        def pack_corners(slot):
            for n, (i, j) in enumerate(DIAGONAL):
                corner = A[2 if i == 0 else X + 1, pl.ds(PAD if j == 0 else PAD + Y - 1, 1), :]
                S[slot, pl.ds(at_c[n][0], 1), :] = corner

        def stencil(src, x, low, high):
            here = pl.ds(PAD + low, high - low)
            at_lane = lane[0:high - low]
            c = src[x + 2, here, :]
            total = src[x + 1, here, :] + src[x + 3, here, :]
            total = total + (src[x + 2, pl.ds(PAD + low - 1, high - low), :]
                             + src[x + 2, pl.ds(PAD + low + 1, high - low), :])
            total = total + (jnp.where(at_lane == 0, 0.0, pltpu.roll(c, 1, 1))
                             + jnp.where(at_lane == Z - 1, 0.0, pltpu.roll(c, Z - 1, 1)))
            return total + EB[x + 1, pl.ds(low, high - low), :] * c

        def plane(src, dst, first, weight, scale=None, low=0, high=Y):
            here = pl.ds(PAD + low, high - low)

            def work(x):
                value = stencil(src, x, low, high)
                if first:
                    value = 0.5 * value
                else:
                    value = ((value + weight * BB[x + 1, pl.ds(low, high - low), :])
                             - back * dst[x + 2, here, :])
                if scale is not None:
                    value = scale * value

                def store(value):
                    dst[x + 2, here, :] = value
                return value, store
            return work

        def mend(dst, low, high, halo, offset, scale):
            for j, at in ((0, PAD), (1, PAD + Y - 1)):
                flat, where = across(dst, at, low + 2, high - low, Y + 2 * PAD)
                flat[where, :] = flat[where, :] + scale * halo[j, pl.ds(low + offset, high - low), :]

        def fringe(slot, first, weight):
            for j in range(2):
                c = R[j, pl.ds(PAD, X), :]
                total = R[j, pl.ds(PAD - 1, X), :] + R[j, pl.ds(PAD + 1, X), :]
                total = total + S[slot, pl.ds(at_y[j][0], X), :] + H[slot, pl.ds(at_y[j][0] + X, X), :]
                total = total + jnp.where(lane_x == 0, 0.0, pltpu.roll(c, 1, 1))
                total = total + jnp.where(lane_x == Z - 1, 0.0, pltpu.roll(c, Z - 1, 1))
                total = total + ER[j] * c
                if first:
                    R2[j] = (0.5 * inside_y[j]) * total
                else:
                    R2[j] = inside_y[j] * (total + weight * BR[j] - back * R2[j])

        def landed(slot):
            for j in range(2):
                A[j, rows, :] = H[slot, pl.ds(at_x[0][0] + j * Y, Y), :]
                A[X + 2 + j, rows, :] = H[slot, pl.ds(at_x[1][0] + j * Y, Y), :]
                R[j, pl.ds(PAD, X), :] = H[slot, pl.ds(at_y[j][0], X), :]
            for j, at in ((0, PAD - 1), (1, PAD + Y)):
                for i, x in ((0, 0), (1, X - 1)):
                    A[x + 2, pl.ds(at, 1), :] = H[slot, pl.ds(at_y[j][0] + x, 1), :]
                    corner = H[slot, pl.ds(at_c[2 * i + j][0], 1), :]
                    A[1 if i == 0 else X + 2, pl.ds(at, 1), :] = corner
            for n, (i, j) in enumerate(DIAGONAL):
                R[j, pl.ds(PAD - 1 if i == 0 else PAD + X, 1), :] = H[slot, pl.ds(at_c[n][0], 1), :]

        def first_sweep(slot, number, first, weight, prepare=lambda: None):
            in_line(1, X - 2, plane(A, B, first, weight))

            @pl.when(number > 0)
            def _():
                wait_sent(1 - slot)
            wait_landed(slot)
            prepare()
            landed(slot)
            done = [plane(A, B, first, weight, scale)(x) for x, scale in
                    ((-1, inside_x[0]), (0, None), (X - 1, None), (X, inside_x[1]))]
            for value, store in done:
                store(value)
            fringe(slot, first, weight)
            mend(B, 1, X - 1, R, PAD, 0.5 if first else 1.0)

        def relay_source(step, n):
            return source_copy(step, n, 2, heart - 3)

        def wait_source(step, n):
            source_copy(step, n, 2, heart).wait_recv()

        inner_layer = sec == heart - 3
        pieces = largest_divisor(X, 4)
        piece = X // pieces

        def current_copy(step, low, count):
            target = jnp.where(inner_layer, heart - 2, heart)
            place = jnp.where(sec == heart - 2, 1, 0)
            span = pl.ds(low, count)
            return remote(JA.at[step, span], JB.at[step, place, span], jsend.at[step],
                          jrecv.at[step, place], target, brick)

        def init_copies():
            found = []
            for i in range(2):
                found.append((has_x[i], EB.at[1 if i == 0 else X], EB.at[X + 1 if i == 0 else 0],
                              EB.at[0 if i == 0 else X + 1], 1 - i, i, sec, to_x[i]))
                found.append((has_x[i], row, PR.at[1 - i], PR.at[i], 5 - i, 4 + i, sec, to_x[i]))
            for j in range(2):
                found.append((has_y[j], SE.at[j], ER.at[1 - j], ER.at[j], 3 - j, 2 + j,
                              to_y[j], brick))
            return found

        def set_up():
            second.wait()

            def absorb(x):
                def store(value):
                    EB[x + 1] = value
                return (center - 6.0) - T[x], store
            for_planes(0, X, 4, absorb)

            for j, at in ((0, 0), (1, Y - 1)):
                flat, where = across(EB, at, 1, X, Y)
                SE[j] = flat[where, :]
            pack_rows(0)
            pack_corners(0)
            pack_planes(0)

        if early:
            set_up()
            return

        def second_sweep(slot, weight, scale, more):
            after = 1 - slot
            for j, at in ((0, PAD - 1), (1, PAD + Y)):
                flat, where = across(B, at, 2, X, Y + 2 * PAD)
                flat[where, :] = R2[j]
            outer_planes = plane(B, A, False, weight, scale)
            done = [outer_planes(x) for x in (0, 1, X - 2, X - 1)]
            for value, store in done:
                store(value)

            @pl.when(more)
            def _():
                pack_planes(after)
                send_planes(after)
                pack_corners(after)
                send_corners(after)
            band = 8 if Y > 16 else Y // 2
            for low in (0, Y - band):
                in_line(2, X - 4, plane(B, A, False, weight, scale, low, low + band))

            @pl.when(more)
            def _():
                pack_rows(after)
                send_across(after)
            if Y > 2 * band:
                in_line(2, X - 4, plane(B, A, False, weight, scale, band, Y - band))

        def step_body(step, carry):
            def prepare():
                @pl.when(step == 0)
                def _():
                    for there, src, dst, land, far, near, s, b in init_copies():
                        @pl.when(there)
                        def _():
                            got = remote(src, land, isend.at[near], irecv.at[near], s, b)
                            got.wait_recv()
                            got.wait_send()

            first_sweep(0, step, True, None, prepare)

            def current(x):
                def store(value):
                    JA[step, x] = value
                own_v = jnp.broadcast_to(own[0:1], (Y, Z))
                value = 2.0 * B[x + 2, rows, :] - (EB[x + 1] + 6.0) * A[x + 2, rows, :]
                return own_v * value, store
            for_planes(0, X, 4, current)


            flags = [jnp.where(PR[i] == section, 1.0, 0.0) for i in range(2)]

            def place(flag):
                def work(x):
                    value = jnp.broadcast_to(flag[0:1], (Y, Z)) * GB[step, x + 1]

                    def store(value):
                        BB[x + 1] = value
                        B[x + 2, rows, :] = B[x + 2, rows, :] + 0.5 * value
                    return value, store
                return work
            for n, (low, count) in enumerate(parts):
                @pl.when(jnp.logical_or(sec != heart - 2, step == 0))
                def _():
                    wait_source(step, n)

                @pl.when(jnp.logical_and(sec == heart - 2, step == 0))
                def _():
                    relay_source(step, n).start()
                if n in inner:
                    for_planes(low - 1, count, 5, place(own))
                else:
                    for x in (low - 1, low):
                        value, store = place({-1: flags[0], X: flags[1]}.get(x, own))(x)
                        store(value)

            for j, at in ((0, Y - 1), (1, 0)):
                flat, where = across(GB, at, step * (X + 2) + 1, X, Y)
                BR[j] = jnp.broadcast_to(own_y[j][0:1], (X, Z)) * flat[where, :]
                R2[j] = R2[j] + 0.5 * BR[j]
            second_sweep(0, push[1], None, True)

            @pl.when(inner_layer)
            def _():
                current_copy(step, 0, X).start()

            def group(g, carry):
                slot = lax.rem(g, 2)

                @pl.when(jnp.logical_and(g == 2, sec == heart - 2))
                def _():
                    remote(JB.at[step, 0], JB.at[step, 0], jsend.at[step], jrecv.at[step, 0],
                           heart, brick).wait_recv()

                    def add(x):
                        def store(value):
                            JA[step, x] = value
                        return JA[step, x] + JB[step, 0, x], store
                    for_planes(0, X, 4, add)

                @pl.when(jnp.logical_and(jnp.logical_and(g >= 2, g < pieces + 2),
                                         jnp.logical_not(inner_layer)))
                def _():
                    current_copy(step, (g - 2) * piece, piece).start()

                @pl.when(jnp.logical_and(jnp.logical_and(g == GROUPS - 3, step + 1 < STEPS),
                                         sec == heart - 2))
                def _():
                    for n in range(len(parts)):
                        wait_source(step + 1, n)
                        relay_source(step + 1, n).start()

                first = push[2 * g]
                first_sweep(slot, g, False, first)
                going_on = step < STEPS - 1
                second_sweep(slot, push[2 * g + 1], jnp.where(going_on, push[SWEEPS + g], 1.0),
                             jnp.logical_or(g < GROUPS - 1, going_on))
                return carry

            lax.fori_loop(1, GROUPS, group, 0)
            return carry

        send_across(0)
        send_corners(0)
        send_planes(0)
        for there, src, dst, land, far, near, s, b in init_copies():
            @pl.when(there)
            def _():
                remote(src, dst, isend.at[near], irecv.at[far], s, b).start()
        lax.fori_loop(0, STEPS, step_body, 0)

        result = pltpu.make_async_copy(A.at[pl.ds(2, X), rows], out.at[0], lsem.at[0])
        result.start()
        wait_sent((GROUPS - 1) % 2)
        for step in range(STEPS):
            current_copy(step, 0, X).wait_send()

            @pl.when(sec == heart - 2)
            def _():
                for n in range(len(parts)):
                    relay_source(step, n).wait_send()

        result.wait()

    field.wait()
    for early in (True, False):
        pl.when(is_heart)(functools.partial(heart_program, early))
        pl.when(jnp.logical_not(is_heart))(functools.partial(torso_program, early))
        if early:
            pl.semaphore_wait(barrier, total)


def body(mesh, potentials, coefficient, recovery, excitable, row_of):
    sections, bricks = mesh.shape["sec"], mesh.shape["brick"]
    _, X, Y, Z = potentials.shape
    f32 = jnp.float32
    scratch = [
        ((X + 4, Y + 2 * PAD, Z), f32), ((X + 4, Y + 2 * PAD, Z), f32),
        ((X + 2, Y, Z), f32), ((STEPS, X + 2, Y, Z), f32), ((X + 2, Y, Z), f32),
        ((STEPS, X, Y, Z), f32), ((STEPS, 2, X, Y, Z), f32),
        ((X, Y, Z), f32), ((X, Y, Z), f32), ((X, Y, Z), jnp.int32),
        ((2, 4 * (X + Y) + 32, Z), f32), ((2, 4 * (X + Y) + 32, Z), f32),
        ((2, 4 * (X + Y) + 32, Z), f32), ((2 * max(X, Y), Z), f32),
        ((2, X + 2 * PAD, Z), f32), ((2, X, Z), f32),
        ((2, X, Z), f32), ((2, X, Z), f32), ((2, X, Z), f32),
        ((2, 8, Z), f32), ((STEPS + 1, 2, 2, Y, Z), f32), ((8, Z), f32),
    ]
    sems = [(4,), (2,), (2,), (6,), (6,), (STEPS, 5, 3), (STEPS, 5), (STEPS,), (STEPS, 2),
            (2,), (STEPS + 1, 2)]
    hbm = pl.BlockSpec(memory_space=pltpu.HBM)
    cells = X * Y * Z
    fields = pl.pallas_call(
        functools.partial(kernel, sections, bricks),
        out_shape=jax.ShapeDtypeStruct(potentials.shape, f32),
        in_specs=[hbm] * 4 + [pl.BlockSpec(memory_space=pltpu.SMEM)],
        out_specs=hbm,
        scratch_shapes=[pltpu.VMEM(s, t) for s, t in scratch]
        + [pltpu.SMEM((len(PUSHES),), f32)]
        + [pltpu.SemaphoreType.DMA(s) for s in sems],
        compiler_params=pltpu.CompilerParams(
            collective_id=0, has_side_effects=True, vmem_limit_bytes=63 * 2**20 + 2**19),
        cost_estimate=pl.CostEstimate(
            flops=cells * STEPS * SWEEPS * 12, bytes_accessed=20 * cells, transcendentals=0),
    )(potentials, coefficient, recovery, excitable, row_of)
    torso = lax.axis_index("sec") < sections - 1
    return fields * jnp.where(torso, PUSHES[-1], 1.0).astype(f32)


def solution(mesh):
    in_specs = (
        P("sec", "brick", None, None),
        P("sec", "brick", None, None),
        P("brick", None, None),
        P("brick", None, None),
        P("brick"),
    )
    out_specs = P("sec", "brick", None, None)
    return jax.shard_map(functools.partial(body, mesh), mesh=mesh, in_specs=in_specs,
                         out_specs=out_specs, check_vma=False)
```
